32 devices in a mesh: dp: 2 (over core), expert: 16 (over z, y, x).
Axes of the slice: x: 2, y: 2, z: 4, core: 2. Of those that a mesh axis runs over, the one named last changes fastest.
Arguments:
- tokens: bfloat16 [16, 256, 768], P('expert', 'dp'), may hold values from -6 to 6
- gain_one: bfloat16 [768], P(('dp', 'expert')), may hold values from 0.5 to 1.5
- w_query: bfloat16 [768, 768], P(('dp', 'expert')), may hold values from -0.21875 to 0.21875
- w_key: bfloat16 [768, 768], P(('dp', 'expert')), may hold values from -0.21875 to 0.21875
- w_value: bfloat16 [768, 768], P(('dp', 'expert')), may hold values from -0.21875 to 0.21875
- w_out: bfloat16 [768, 768], P(('dp', 'expert')), may hold values from -0.875 to 0.875
- bias_table: float32 [32, 12], replicated, may hold values from -6 to 6
- gain_two: bfloat16 [768], P(('dp', 'expert')), may hold values from 0.5 to 1.5
- w_router: bfloat16 [768, 16], P(('dp', 'expert')), may hold values from -0.15625 to 0.15625
- w_inner: bfloat16 [16, 768, 3072], P('expert', None, 'dp'), may hold values from -0.21875 to 0.21875
- w_outer: bfloat16 [16, 3072, 768], P('expert', 'dp'), may hold values from -2.5 to 2.5
- segment_ids: int32 [16, 256], P('expert'), may hold values from 0 to 3, never falling along the last dimension, each value on 1 to 128 neighbouring positions
- routes: int32 [16, 256, 1], P('expert', 'dp'), may hold values from 0 to 15
- out_grad: bfloat16 [16, 256, 768], P('expert', 'dp'), may hold values from -6 to 6
Outputs:
- layer_output: bfloat16 [16, 256, 768], P('expert', 'dp')
- input_grad: bfloat16 [16, 256, 768], P('expert', 'dp')
- gain_one_grad: float32 [768], P(('dp', 'expert'))
- query_grad: float32 [768, 768], P(('dp', 'expert'))
- key_grad: float32 [768, 768], P(('dp', 'expert'))
- value_grad: float32 [768, 768], P(('dp', 'expert'))
- out_proj_grad: float32 [768, 768], P(('dp', 'expert'))
- table_grad: float32 [32, 12], replicated
- gain_two_grad: float32 [768], P(('dp', 'expert'))
- router_grad: float32 [768, 16], P(('dp', 'expert'))
- inner_grad: float32 [16, 768, 3072], P('expert', None, 'dp')
- outer_grad: float32 [16, 3072, 768], P('expert', 'dp')
The draws below stay inside these ranges and needn't reach their ends.
Inputs may be any that keep to these rules, and one draw needn't show every extreme that they name: `segment_ids`: in each row the ids never fall; every document holds 1 to 128 tokens, one exactly 128.
All inputs are finite; a program needn't handle non-finite values.
Results may differ from the reference program's by a relative error of at most 0.015.
Values may be sent and summed in bfloat16 or wider, within the bound.
No kernel may reach another device: no remote copies, remote signals or barrier semaphores. Data moves between devices by JAX's collectives and lax.ppermute only.
A program may use at most 128 MiB of HBM per device.

```python
import math
import jax
import jax.numpy as jnp
import numpy as np
from jax import lax

D = 768
HEADS = 12
HD = 64
FF = 3072
BUCKETS = 32
TOK_DEV = 128
DOCS = 4
LENGTH = 256
SEQS = 16
EXPERTS = 16
CAP = 10
DOC_MOST = 128
N_DP = 2


def shard_levels(stream_key, dims, cuts, low, largest):
    level, own = 1.0, jax.random.fold_in(stream_key, 6)
    for axis_at, parts in cuts:
        draws = jnp.exp(jax.random.uniform(jax.random.fold_in(own, axis_at), (parts,), jnp.float32, low / len(cuts), largest / len(cuts)))
        level = level * jnp.repeat(draws, dims[axis_at] // parts).reshape([-1 if axis == axis_at else 1 for axis in range(len(dims))])
    return level


def different_ones(own_key, rows, number_of, top, lift):
    ranking = jax.random.permutation(jax.random.fold_in(own_key, 1), number_of)
    favour = ranking
    for power in range(3):
        favour = favour * favour // number_of
    favour = favour * lift // number_of
    lots = jax.random.randint(jax.random.fold_in(own_key, 2), (rows, number_of), 0, 4096) + favour
    sure = jax.random.permutation(jax.random.fold_in(own_key, 3), rows)[jnp.arange(number_of) % rows]
    lots = jnp.where(jnp.arange(rows)[:, None] == sure[None, :], 1 << 14, lots)
    score = lots * number_of + jnp.arange(number_of)
    return lax.top_k(score.astype(jnp.int32), top)[1].astype(jnp.int32)


def profile(amount, total, limit, slope):
    portions = [(1 << 20) // math.isqrt(rank ** slope) + 1 for rank in range(2, amount + 1)]
    rest, given = total - limit - (amount - 1), [1] * (amount - 1)
    while rest > 0:
        movable = [i for i in range(amount - 1) if given[i] < limit]
        whole, remaining = sum([portions[i] for i in movable]), rest
        for i in movable:
            more = min(limit - given[i], max(1, remaining * portions[i] // whole), rest)
            given[i] = given[i] + more
            rest = rest - more
    return np.array([limit] + given)


def uneven_parts(stream_key, count, total, bound, slope):
    if count == 2:
        one = jax.random.randint(stream_key, (), max(1, total - bound), min(bound, total - 1) + 1)
        return jnp.stack([one, total - one])
    sizes = jnp.asarray(profile(count, total, bound, slope), jnp.int32)
    pairs = (count - 1) // 2
    source_of, sink = sizes[1:1 + 2 * pairs:2], sizes[2:2 + 2 * pairs:2]
    slack = jnp.minimum(source_of - 1, bound - sink)
    passed = jax.random.randint(jax.random.fold_in(stream_key, 1), (pairs,), 0, 1 << 20) % (slack + 1)
    sizes = sizes.at[1:1 + 2 * pairs:2].set(source_of - passed).at[2:2 + 2 * pairs:2].set(sink + passed)
    return sizes[jax.random.permutation(jax.random.fold_in(stream_key, 2), count)]


def noise(own_key, extent, width, reach, shards=(), kind=jnp.bfloat16):
    values = jax.random.normal(own_key, extent, jnp.float32) * width
    if len(shards) > 0:
        values = shard_levels(own_key, extent, shards, -0.22, 0.18) * values
    return jnp.clip(values, min=-reach, max=reach).astype(kind)


def setup_inputs(seed: int = 0) -> dict:
    seeds = jax.random.split(jax.random.key(seed), 15)
    return {
        "tokens": noise(seeds[0], (SEQS, LENGTH, D), 1.0, 6.0, ((0, 16), (1, 2))),
        "gain_one": jnp.clip(1.0 + 0.1 * jax.random.normal(seeds[1], (D,), jnp.float32), 0.5, 1.5).astype(jnp.bfloat16),
        "w_query": noise(seeds[2], (D, D), D ** -0.5, 0.21875, ((0, 32),)),
        "w_key": noise(seeds[3], (D, D), D ** -0.5, 0.21875, ((0, 32),)),
        "w_value": noise(seeds[4], (D, D), D ** -0.5, 0.21875, ((0, 32),)),
        "w_out": noise(seeds[5], (D, D), (D // 16) ** -0.5, 0.875, ((0, 32),)),
        "bias_table": noise(seeds[6], (BUCKETS, HEADS), 1.0, 6.0, (), jnp.float32),
        "gain_two": jnp.clip(1.0 + 0.1 * jax.random.normal(seeds[7], (D,), jnp.float32), 0.5, 1.5).astype(jnp.bfloat16),
        "w_router": noise(seeds[8], (D, EXPERTS), 0.025, 0.15625, ((0, 32),)),
        "w_inner": noise(seeds[9], (EXPERTS, D, FF), D ** -0.5, 0.21875, ((0, 16), (2, 2))),
        "w_outer": noise(seeds[10], (EXPERTS, FF, D), (0.026 * EXPERTS), 2.5, ((0, 16), (1, 2))),
        "segment_ids": jax.vmap(lambda own: jnp.searchsorted(jnp.cumsum(uneven_parts(own, DOCS, LENGTH, DOC_MOST, 2)), jnp.arange(LENGTH), side="right"))(jax.random.split(seeds[11], SEQS)).reshape((SEQS, LENGTH)).astype(jnp.int32),
        "routes": different_ones(seeds[12], SEQS * LENGTH, EXPERTS, 1, 512).reshape((SEQS, LENGTH, 1)),
        "out_grad": noise(seeds[13], (SEQS, LENGTH, D), 1.0, 6.0, ((0, 16), (1, 2))),
    }


EPSILON = 1e-06
MASKED = -1000000000.0
BUCKET_EDGES = (1, 2, 3, 4, 5, 6, 7, 8, 12, 16, 23, 32, 46, 64, 91)

@jax.custom_vjp
def low(v):
    return lax.optimization_barrier(v.astype(jnp.bfloat16)).astype(jnp.float32)

@jax.custom_vjp
def low_back(v):
    return v

def low_keep(v):
    return (low(v), None)

def low_pass(kept, grad):
    return (grad,)

def back_keep(v):
    return (v, None)

def back_low(kept, grad):
    return (low(grad),)
low.defvjp(low_keep, low_pass)
low_back.defvjp(back_keep, back_low)

def exact_dot(left, right):
    return jnp.dot(left, right, precision=lax.Precision.HIGHEST, preferred_element_type=jnp.float32)

def exact_sum(formula, left, right):
    return jnp.einsum(formula, left, right, precision=lax.Precision.HIGHEST, preferred_element_type=jnp.float32)

def rms_inverse(values):
    return lax.rsqrt(lax.optimization_barrier(jnp.mean(values * values, axis=-1, keepdims=True)) + EPSILON)

def smooth_gate(values):
    return jax.nn.gelu(values, approximate=False)

def relative_buckets(length):
    positions = jnp.arange(length, dtype=jnp.int32)
    offset = positions[None, :] - positions[:, None]
    distance = jnp.abs(offset)
    bucket = jnp.zeros(offset.shape, jnp.int32)
    for border in BUCKET_EDGES:
        bucket = bucket + (distance >= border).astype(jnp.int32)
    return bucket + BUCKETS // 2 * (offset > 0).astype(jnp.int32)

def sequence_forward(params, seq_tokens, seq_docs, seq_routes):
    gain_first, query_w, key_w, value_w, out_w, table_w, gain_second, router_w, inner_w, outer_w = params
    length = seq_tokens.shape[0]
    normed_one = low(seq_tokens * rms_inverse(seq_tokens) * gain_first)
    query_low = low(low_back(exact_dot(normed_one, query_w))).reshape(length, HEADS, HD)
    key_low = low(low_back(exact_dot(normed_one, key_w))).reshape(length, HEADS, HD)
    value_low = low(low_back(exact_dot(normed_one, value_w))).reshape(length, HEADS, HD)
    raw_scores = exact_sum('qhd,khd->hqk', query_low, key_low) * HD ** (-0.5)
    rel_bias = jnp.transpose(table_w[relative_buckets(length)], (2, 0, 1))
    scores = low_back(raw_scores + rel_bias)
    same_doc = seq_docs[:, None] == seq_docs[None, :]
    attn_probs = jax.nn.softmax(jnp.where(same_doc[None], scores, MASKED), axis=-1)
    attended = low(low_back(exact_sum('hqk,khd->qhd', low(attn_probs), value_low).reshape(length, D)))
    middle = seq_tokens + low_back(exact_dot(attended, out_w))
    normed_two = low(middle * rms_inverse(middle) * gain_second)
    router_probs = jax.nn.softmax(low_back(exact_dot(normed_two, router_w)), axis=-1)
    chosen = seq_routes[:, None] == jnp.arange(EXPERTS, dtype=jnp.int32)[None, :]
    gate = lax.optimization_barrier(jnp.sum(router_probs * chosen.astype(jnp.float32), axis=-1))
    chosen_blocks = chosen.reshape(N_DP, TOK_DEV, EXPERTS)
    chosen_int = chosen_blocks.astype(jnp.int32)
    slot_index = lax.optimization_barrier(jnp.sum(jnp.cumsum(chosen_int, axis=1, dtype=jnp.int32) * chosen_int, axis=-1, dtype=jnp.int32)) - 1
    in_slot = slot_index[:, :, None] == jnp.arange(CAP, dtype=jnp.int32)[None, None, :]
    dispatch = (chosen_blocks[:, :, :, None] & in_slot[:, :, None, :]).astype(jnp.float32)
    buffers = low_back(exact_sum('btec,btd->becd', dispatch, normed_two.reshape(N_DP, TOK_DEV, D)))
    pre_act = exact_sum('becd,edf->becf', buffers, inner_w)
    hidden = low(smooth_gate(low_back(pre_act)))
    expert_out = low(low_back(exact_sum('becf,efd->becd', hidden, outer_w)))
    combined = exact_sum('btec,becd->btd', dispatch, expert_out).reshape(length, D)
    return middle + gate[:, None] * combined

def reference(tokens, gain_one, w_query, w_key, w_value, w_out, bias_table, gain_two, w_router, w_inner, w_outer, segment_ids, routes, out_grad):
    params = (gain_one.astype(jnp.float32), w_query.astype(jnp.float32), w_key.astype(jnp.float32), w_value.astype(jnp.float32), w_out.astype(jnp.float32), bias_table.astype(jnp.float32), gain_two.astype(jnp.float32), w_router.astype(jnp.float32), w_inner.astype(jnp.float32), w_outer.astype(jnp.float32))
    inputs = tokens.astype(jnp.float32)
    route_ids = routes[:, :, 0]
    step_forward = jax.checkpoint(sequence_forward)

    def forward(token_values, weights):

        def one_row(sliced):
            return step_forward(weights, sliced[0], sliced[1], sliced[2])
        return lax.map(one_row, (token_values, segment_ids, route_ids))
    result, pullback = jax.vjp(forward, inputs, params)
    grad_tokens, grad_params = pullback(out_grad.astype(jnp.float32))
    return (result.astype(jnp.bfloat16), grad_tokens.astype(jnp.bfloat16), grad_params[0], grad_params[1], grad_params[2], grad_params[3], grad_params[4], grad_params[5], grad_params[6], grad_params[7], grad_params[8], grad_params[9])
```

```python
import jax
import jax.numpy as jnp
from jax import lax
from jax.sharding import PartitionSpec as P

EPSILON = 1e-06
MASKED = -1000000000.0
BUCKET_EDGES = (1, 2, 3, 4, 5, 6, 7, 8, 12, 16, 23, 32, 46, 64, 91)
F32 = jnp.float32
BF16 = jnp.bfloat16
SMALL = 64
PAIR = 1


def dot(left, right, dims=((1,), (0,))):
    return lax.dot_general(left, right, (dims, ((), ())), preferred_element_type=F32)


def rms_inverse(values):
    return lax.rsqrt(jnp.mean(values * values, axis=-1, keepdims=True) + EPSILON)


def norm_backward(grad_normed, unit_values, inverse, gain_values):
    grad_unit = grad_normed * gain_values
    projected = jnp.mean(grad_unit * unit_values, axis=-1, keepdims=True)
    return inverse * (grad_unit - unit_values * projected)


def swap_core(value):
    return lax.ppermute(value, "dp", [(0, 1), (1, 0)])


def swap_pair(value):
    n = lax.axis_size("expert")
    return lax.ppermute(value, "expert", [(i, i ^ PAIR) for i in range(n)])


def exchange(value):
    return lax.all_to_all(value, "expert", split_axis=0, concat_axis=0, tiled=True)


def bucket_of(offset, total):
    distance = jnp.abs(offset)
    bucket = jnp.zeros(offset.shape, jnp.int32)
    for border in BUCKET_EDGES:
        bucket = bucket + (distance >= border).astype(jnp.int32)
    return bucket + total // 2 * (offset > 0).astype(jnp.int32)


def local(
    tokens,
    gain_one,
    w_query,
    w_key,
    w_value,
    w_out,
    bias_table,
    gain_two,
    w_router,
    w_inner,
    w_outer,
    segment_ids,
    routes,
    out_grad,
):
    toks = tokens.shape[1]
    width = tokens.shape[2]
    heads = bias_table.shape[1]
    buckets = bias_table.shape[0]
    head_dim = width // heads
    own_heads = heads // 4
    cols = own_heads * head_dim
    half = width // 2
    scale = head_dim ** (-0.5)
    sources = lax.axis_size("expert")
    experts = sources
    capacity = (5 * toks + 4 * experts - 1) // (4 * experts)
    slots = experts * capacity
    rows = w_query.shape[0]
    core = lax.axis_index("dp")
    place = lax.axis_index("expert")
    member = place & PAIR
    first_core = core == 0

    def halves(w):
        return jnp.where(first_core, w[:, :half], w[:, half:]), jnp.where(
            first_core, w[:, half:], w[:, :half]
        )

    keep, send = zip(halves(w_query), halves(w_key), halves(w_value))
    small = jnp.concatenate([w_router, gain_one[:, None], gain_two[:, None]], axis=1)
    keep = jnp.concatenate(keep + (small,), axis=1)
    send = jnp.concatenate(send + (small,), axis=1)
    got = swap_core(send)
    both = jnp.where(first_core, jnp.stack([keep, got]), jnp.stack([got, keep]))
    both = both.reshape(2 * rows, -1)
    small_at = 3 * half
    parts = []
    for variant in range(2):
        at = variant * cols
        parts.append(
            jnp.concatenate(
                [both[:, k * half + at : k * half + at + cols] for k in range(3)]
                + [both[:, small_at:]],
                axis=1,
            )
        )
    message = jnp.stack(parts)
    wide = message.shape[2]
    message = jnp.broadcast_to(message[None], (sources // 2, 2, 2 * rows, wide)).reshape(
        sources, 2 * rows, wide
    )
    weights = exchange(message)
    weights = (
        weights.reshape(sources, 2, rows, wide).transpose(1, 0, 2, 3).reshape(width, wide)
    )
    qkv_w = weights[:, : 3 * cols]
    router_w = weights[:, 3 * cols : 3 * cols + experts]
    gain_first = weights[:, 3 * cols + experts].astype(F32)[None]
    gain_second = weights[:, 3 * cols + experts + 1].astype(F32)[None]
    out_half = exchange(jnp.broadcast_to(w_out[None], (sources, rows, width))).reshape(half, width)
    out_w = lax.dynamic_slice_in_dim(out_half, member * cols, cols)

    own_tokens = tokens.reshape(toks, width)
    pair_tokens = swap_pair(own_tokens)
    two = jnp.stack([own_tokens, pair_tokens])
    group_tokens = jnp.stack([two, swap_core(two)], axis=1)
    x_all = group_tokens.reshape(4 * toks, width).astype(F32)
    unit_all = x_all * rms_inverse(x_all)
    normed_all = (unit_all * gain_first).astype(BF16)
    docs_two = jnp.concatenate([segment_ids, swap_pair(segment_ids)], axis=0)
    docs = jnp.where(first_core, docs_two, jnp.roll(docs_two, toks, axis=1))

    length = 2 * toks
    spot = jnp.arange(length, dtype=jnp.int32)
    offset = spot[None, :] - spot[:, None]
    offset = jnp.where(offset >= toks, offset - length, offset)
    offset = jnp.where(offset <= -toks, offset + length, offset)
    onehot = (
        bucket_of(offset, buckets)[:, :, None] == jnp.arange(buckets, dtype=jnp.int32)
    ).astype(F32)
    group = 2 * core + member
    own_table = lax.dynamic_slice_in_dim(bias_table, group * own_heads, own_heads, axis=1)
    rel_bias = jnp.einsum(
        "qkb,bh->hqk", onehot, own_table, precision=lax.Precision.HIGHEST,
        preferred_element_type=F32,
    )
    same = docs[:, :, None] == docs[:, None, :]

    qkv = dot(normed_all, qkv_w).astype(BF16).reshape(2, length, 3, own_heads, head_dim)
    query, key, value = qkv[:, :, 0], qkv[:, :, 1], qkv[:, :, 2]
    scores = (
        jnp.einsum("rqhd,rkhd->rhqk", query, key, preferred_element_type=F32) * scale
        + rel_bias[None]
    )
    scores = jnp.where(same[:, None], scores, MASKED)
    top = jnp.max(scores, axis=-1, keepdims=True)
    log_total = top + jnp.log(jnp.sum(jnp.exp(scores - top), axis=-1, keepdims=True))
    probs = jnp.exp(scores - log_total)
    probs_low = probs.astype(BF16)
    attended = jnp.einsum("rhqk,rkhd->rqhd", probs_low, value, preferred_element_type=F32)
    attended = attended.reshape(4 * toks, cols).astype(BF16)
    partial = dot(attended, out_w).reshape(2, 2, toks, width)
    across = swap_core(partial[:, 1].astype(BF16))
    partial = partial[:, 0] + across.astype(F32)
    across = swap_pair(partial[1].astype(BF16))
    x = own_tokens.astype(F32)
    middle = x + (partial[0] + across.astype(F32))

    inverse_two = rms_inverse(middle)
    unit_two = middle * inverse_two
    normed_two = (unit_two * gain_second).astype(BF16)
    router_probs = jax.nn.softmax(dot(normed_two, router_w), axis=-1)
    route_ids = routes.reshape(toks)
    chosen = route_ids[:, None] == jnp.arange(experts, dtype=jnp.int32)[None, :]
    chosen_float = chosen.astype(F32)
    tok = jnp.arange(toks, dtype=jnp.int32)
    earlier = (route_ids[:, None] == route_ids[None, :]) & (tok[:, None] > tok[None, :])
    slot = jnp.sum(earlier.astype(jnp.int32), axis=1)
    slot_at = jnp.where(slot < capacity, route_ids * capacity + slot, -1)
    dispatch = (slot_at[:, None] == jnp.arange(slots, dtype=jnp.int32)[None, :]).astype(BF16)
    gate = jnp.sum(router_probs * chosen_float, axis=-1, keepdims=True)
    outgoing = dot(dispatch, normed_two, ((0,), (0,))).astype(BF16)
    g_low = out_grad.reshape(toks, width)
    outgoing_grad = dot(dispatch, g_low, ((0,), (0,))).astype(BF16)
    incoming = exchange(outgoing.reshape(experts, capacity, width)).reshape(slots, width)
    incoming_grad = exchange(outgoing_grad.reshape(experts, capacity, width)).reshape(slots, width)

    inner, outer = w_inner[0], w_outer[0]
    buffers = jnp.concatenate([incoming, swap_core(incoming)], axis=0)
    slot_g = jnp.concatenate([incoming_grad, swap_core(incoming_grad)], axis=0).astype(F32)
    slot_probs = jax.nn.softmax(dot(buffers, router_w), axis=-1)
    mine = (jnp.arange(experts, dtype=jnp.int32) == place).astype(F32)[None]
    slot_gate = jnp.sum(slot_probs * mine, axis=-1, keepdims=True)
    slot_grad = (slot_gate * slot_g).astype(BF16)
    pre = dot(buffers, inner)
    cdf = 0.5 * (1.0 + lax.erf(pre * (0.5**0.5)))
    hidden = (pre * cdf).astype(BF16)
    slope = cdf + pre * jnp.exp(-0.5 * pre * pre) * 0.3989422804014327
    grad_hidden = dot(slot_grad, outer, ((1,), (1,)))
    grad_pre = (grad_hidden * slope).astype(BF16)
    result_part = dot(hidden, outer)
    back_part = dot(grad_pre, inner, ((1,), (1,)))
    grad_outer = dot(hidden, slot_grad, ((0,), (0,)))
    grad_inner = dot(buffers, grad_pre, ((0,), (0,)))
    parts = jnp.stack([result_part, back_part])
    across = swap_core(parts[:, slots:].astype(BF16))
    parts = (parts[:, :slots] + across.astype(F32)).astype(BF16)
    result, back = parts[0], parts[1]
    grad_gate = jnp.sum(slot_g[:slots] * result.astype(F32), axis=-1, keepdims=True)
    grad_logits = (grad_gate * slot_gate[:slots] * (mine - slot_probs[:slots])).astype(BF16)
    grad_router = dot(incoming, grad_logits, ((0,), (0,)))
    back = (back.astype(F32) + dot(grad_logits, router_w, ((1,), (1,)))).astype(BF16)
    back = exchange(back.reshape(sources, capacity, width)).reshape(slots, width)
    result = exchange(result.reshape(sources, capacity, width)).reshape(slots, width)

    final = middle + gate * dot(dispatch, result)
    grad_normed_two = dot(dispatch, back)
    grad_gain_two = jnp.sum(grad_normed_two * unit_two, axis=0)
    grad_middle = g_low.astype(F32) + norm_backward(
        grad_normed_two, unit_two, inverse_two, gain_second
    )
    grad_attn = grad_middle.astype(BF16)
    pair_grad = swap_pair(grad_attn)
    two = jnp.stack([grad_attn, pair_grad])
    group_grad = jnp.stack([two, swap_core(two)], axis=1).reshape(4 * toks, width)

    grad_out = dot(attended, group_grad, ((0,), (0,))).astype(BF16)
    grad_out = lax.dynamic_update_slice(
        jnp.zeros((half, width), BF16), grad_out, (member * cols, 0)
    )
    grad_out = jnp.sum(exchange(grad_out.reshape(sources, rows, width)).astype(F32), axis=0)

    grad_attended = dot(group_grad, out_w, ((1,), (1,))).astype(BF16)
    grad_attended = grad_attended.reshape(2, length, own_heads, head_dim)
    grad_probs = jnp.einsum("rqhd,rkhd->rhqk", grad_attended, value, preferred_element_type=F32)
    row_dot = jnp.sum(probs * grad_probs, axis=-1, keepdims=True)
    grad_scores = (probs * (grad_probs - row_dot)).astype(BF16)
    grad_table = jnp.einsum(
        "qkb,rhqk->bh", onehot, grad_scores.astype(F32), precision=lax.Precision.HIGHEST,
        preferred_element_type=F32,
    )
    grad_query = jnp.einsum("rhqk,rkhd->rqhd", grad_scores, key, preferred_element_type=F32) * scale
    grad_key = jnp.einsum("rhqk,rqhd->rkhd", grad_scores, query, preferred_element_type=F32) * scale
    grad_value = jnp.einsum(
        "rhqk,rqhd->rkhd", probs_low, grad_attended, preferred_element_type=F32
    )
    grad_qkv = jnp.stack([grad_query, grad_key, grad_value], axis=2).astype(BF16)
    grad_qkv = grad_qkv.reshape(4 * toks, 3 * cols)
    grad_weights = dot(normed_all, grad_qkv, ((0,), (0,)))
    grad_normed = dot(grad_qkv, qkv_w, ((1,), (1,)))
    grad_gain_one = jnp.sum(grad_normed * unit_all, axis=0)

    table_cols = own_heads * buckets // (2 * rows) if own_heads * buckets >= 2 * rows else 1
    table_rows = own_heads * buckets // table_cols
    table_part = jnp.zeros((2 * rows, table_cols), F32)
    table_part = table_part.at[:table_rows].set(grad_table.reshape(table_rows, table_cols))
    narrow = jnp.stack([grad_gain_one, grad_gain_two], axis=1)
    narrow = jnp.concatenate([grad_weights, grad_router, narrow], axis=1)
    spread = narrow.shape[1]
    narrow = narrow.reshape(2, sources, rows, spread).transpose(1, 0, 2, 3)
    narrow = narrow.reshape(sources, 2 * rows, spread)
    table_part = jnp.broadcast_to(table_part[None], (sources, 2 * rows, table_cols))
    message = jnp.concatenate([narrow, table_part], axis=2).astype(BF16)
    arrived = exchange(message).astype(F32)
    summed = jnp.sum(arrived.reshape(sources // 2, 2, 2 * rows, -1), axis=0)
    by_member = summed[:, :, : 3 * cols].reshape(2, 2, rows, 3, cols)
    smalls = jnp.sum(summed[:, :, 3 * cols : spread], axis=0).reshape(2, rows, spread - 3 * cols)
    tables = summed[:, :table_rows, spread:].reshape(2, buckets, own_heads)
    tables = tables.transpose(1, 0, 2).reshape(buckets, 2 * own_heads)
    mine_w = jnp.where(first_core, by_member[:, 0], by_member[:, 1])
    away_w = jnp.where(first_core, by_member[:, 1], by_member[:, 0])
    mine_s = jnp.where(first_core, smalls[0], smalls[1])
    away_s = jnp.where(first_core, smalls[1], smalls[0])
    came_w = swap_core(away_w.astype(BF16)).astype(F32)
    came_s = swap_core(away_s)
    came_t = swap_core(tables)
    full = jnp.where(first_core, jnp.stack([mine_w, came_w]), jnp.stack([came_w, mine_w]))
    full = full.transpose(3, 2, 0, 1, 4).reshape(3, rows, width)
    smalls = mine_s + came_s
    table_sum = jnp.where(
        first_core,
        jnp.concatenate([tables, came_t], axis=1),
        jnp.concatenate([came_t, tables], axis=1),
    )

    partial = grad_normed.reshape(2, 2, toks, width)
    across = swap_core(partial[:, 1].astype(BF16))
    partial = partial[:, 0] + across.astype(F32)
    across = swap_pair(partial[1].astype(BF16))
    grad_normed_one = partial[0] + across.astype(F32)
    inverse_one = rms_inverse(x)
    grad_input = grad_middle + norm_backward(grad_normed_one, x * inverse_one, inverse_one, gain_first)
    return (
        final.astype(BF16).reshape(tokens.shape),
        grad_input.astype(BF16).reshape(tokens.shape),
        smalls[:, experts],
        full[0],
        full[1],
        full[2],
        grad_out,
        table_sum,
        smalls[:, experts + 1],
        smalls[:, :experts],
        grad_inner[None],
        grad_outer[None],
    )


def solution(mesh):
    both = ("dp", "expert")
    return jax.shard_map(
        local,
        mesh=mesh,
        in_specs=(
            P("expert", "dp", None),
            P(both),
            P(both, None),
            P(both, None),
            P(both, None),
            P(both, None),
            P(),
            P(both),
            P(both, None),
            P("expert", None, "dp"),
            P("expert", "dp", None),
            P("expert", None),
            P("expert", "dp", None),
            P("expert", "dp", None),
        ),
        out_specs=(
            P("expert", "dp", None),
            P("expert", "dp", None),
            P(both),
            P(both, None),
            P(both, None),
            P(both, None),
            P(both, None),
            P(),
            P(both),
            P(both, None),
            P("expert", None, "dp"),
            P("expert", "dp", None),
        ),
        check_vma=False,
    )
```

```python
import functools

import jax
import jax.numpy as jnp
from jax import lax
from jax.experimental import pallas as pl
from jax.experimental.pallas import tpu as pltpu
from jax.sharding import PartitionSpec as P

EPSILON = 1e-06
MASKED = -1000000000.0
BUCKET_EDGES = (1, 2, 3, 4, 5, 6, 7, 8, 12, 16, 23, 32, 46, 64, 91)
F32 = jnp.float32
BF16 = jnp.bfloat16
PAIR_BIT = 2
PAIR = 1 << PAIR_BIT
VMEM_BYTES = 48 * 1024 * 1024


def dot(left, right, dims=((1,), (0,))):
    return lax.dot_general(left, right, (dims, ((), ())), preferred_element_type=F32)


def rms_inverse(values):
    return lax.rsqrt(jnp.mean(values * values, axis=-1, keepdims=True) + EPSILON)


def norm_backward(grad_normed, unit_values, inverse, gain_values):
    grad_unit = grad_normed * gain_values
    projected = jnp.mean(grad_unit * unit_values, axis=-1, keepdims=True)
    return inverse * (grad_unit - unit_values * projected)


def swap_core(value):
    return lax.ppermute(value, "dp", [(0, 1), (1, 0)])


def swap_pair(value):
    n = lax.axis_size("expert")
    return lax.ppermute(value, "expert", [(i, i ^ PAIR) for i in range(n)])


def exchange(value):
    return lax.all_to_all(value, "expert", split_axis=0, concat_axis=0, tiled=True)


def bucket_of(offset, total):
    distance = jnp.abs(offset)
    bucket = jnp.zeros(offset.shape, jnp.int32)
    for border in BUCKET_EDGES:
        bucket = bucket + (distance >= border).astype(jnp.int32)
    return bucket + total // 2 * (offset > 0).astype(jnp.int32)


def iota(shape, axis):
    return lax.broadcasted_iota(jnp.int32, shape, axis)


def kernel_call(body, outs, *args, scalars=0, flops=1_000_000, nbytes=1_000_000):
    specs = [pl.BlockSpec(memory_space=pltpu.SMEM)] * scalars
    specs += [pl.BlockSpec(memory_space=pltpu.VMEM)] * (len(args) - scalars)
    return pl.pallas_call(
        body,
        out_shape=[jax.ShapeDtypeStruct(shape, dtype) for shape, dtype in outs],
        in_specs=specs,
        out_specs=[pl.BlockSpec(memory_space=pltpu.VMEM)] * len(outs),
        compiler_params=pltpu.CompilerParams(vmem_limit_bytes=VMEM_BYTES),
        cost_estimate=pl.CostEstimate(flops=flops, bytes_accessed=nbytes, transcendentals=0),
    )(*args)


def pack_weights(q_ref, k_ref, v_ref, router_ref, gains_ref, out_ref):
    rows, width = q_ref.shape
    experts = router_ref.shape[1]
    out_ref[:, :width] = q_ref[...]
    out_ref[:, width : 2 * width] = k_ref[...]
    out_ref[:, 2 * width : 3 * width] = v_ref[...]
    eye = iota((rows, rows), 0) == iota((rows, rows), 1)
    columns = [
        jnp.sum(jnp.where(eye, gains_ref[i : i + 1, :].astype(F32), 0.0), axis=1, keepdims=True)
        for i in range(2)
    ]
    pad = out_ref.shape[1] - 3 * width - experts - 2
    small = jnp.concatenate(
        [router_ref[...].astype(F32)] + columns + [jnp.zeros((rows, pad), F32)], axis=1
    )
    out_ref[:, 3 * width :] = small.astype(BF16)


def spread_weights(cols, core_ref, own_ref, other_ref, out_ref):
    sources, _, wide = out_ref.shape
    width = 4 * cols
    half = 2 * cols
    first = core_ref[0] == 0
    own = own_ref[...]
    other = other_ref[...]
    both = jnp.concatenate(
        [jnp.where(first, own, other), jnp.where(first, other, own)], axis=0
    )
    for variant in range(2):
        at = variant * cols
        parts = []
        for k in range(3):
            low = k * width + at
            high = low + half
            parts.append(jnp.where(first, both[:, low : low + cols], both[:, high : high + cols]))
        parts.append(both[:, 3 * width : 3 * width + wide - 3 * cols])
        value = jnp.concatenate(parts, axis=1)
        for dest in range(sources):
            if (dest >> PAIR_BIT) & 1 == variant:
                out_ref[dest] = value


def prepare(capacity, pad, core_ref, group_ref, table_ref, docs_ref, routes_ref, bias_ref,
            spread_ref, gather_ref, send_ref):
    buckets = table_ref.shape[0]
    own_heads = bias_ref.shape[1]
    length = docs_ref.shape[1]
    toks = length // 2
    group = group_ref[0]
    spot = iota((1, length), 1)
    offset = jnp.where(spot >= toks, spot - length, spot)
    bucket = bucket_of(offset, buckets)
    vectors = []
    for h in range(own_heads):
        vector = jnp.zeros((1, length), F32)
        for b in range(buckets):
            vector = jnp.where(bucket == b, table_ref[b, group * own_heads + h], vector)
        full = jnp.broadcast_to(vector, (length, length))
        vectors.append(pltpu.roll(full, 0, 1, stride=1, stride_axis=0))
    for r in range(2):
        across = jnp.broadcast_to(docs_ref[r : r + 1, :].astype(F32), (length, length))
        same = across == jnp.transpose(across)
        for h in range(own_heads):
            bias_ref[r, h] = jnp.where(same, vectors[h], MASKED)
    experts = spread_ref.shape[1] // pad
    route = routes_ref[...]
    chosen = route == iota((toks, experts), 1)
    lower = (iota((toks, toks), 0) > iota((toks, toks), 1)).astype(BF16)
    counts = dot(lower, chosen.astype(BF16))
    slot = jnp.sum(jnp.where(chosen, counts, 0.0), axis=1, keepdims=True).astype(jnp.int32)
    kept = slot < capacity
    place = jnp.where(kept, route * pad + slot, -1)
    spread = (place == iota((toks, experts * pad), 1)).astype(F32)
    spread_ref[...] = spread.astype(BF16)
    wide = send_ref.shape[0] // experts
    place = jnp.where(kept, route * wide + slot, -1)
    later = jnp.where(kept, route * wide + capacity + slot, -1)
    across = iota((toks, experts * wide), 1)
    send_ref[:, :toks] = jnp.transpose((place == across).astype(F32)).astype(BF16)
    send_ref[:, toks:] = jnp.transpose((later == across).astype(F32)).astype(BF16)
    gather_ref[...] = chosen.astype(F32)


def attend(scale, head_dim, experts, w_ref, own_ref, across_ref, bias_ref, wout_ref, qkv_ref,
           normed_ref, probs_ref, att_ref, keep_ref, send_ref, gains_ref):
    own_heads = bias_ref.shape[1]
    cols = own_heads * head_dim
    toks = own_ref.shape[1]
    small = w_ref[:, 3 * cols :]
    pick = (iota((8, small.shape[1]), 1) == iota((8, small.shape[1]), 0) + experts).astype(BF16)
    gains = dot(pick, small, ((1,), (1,)))
    gains_ref[...] = gains
    for r in range(2):
        x = jnp.concatenate([own_ref[r], across_ref[r]], axis=0).astype(F32)
        normed = (x * rms_inverse(x) * gains[0:1]).astype(BF16)
        normed_ref[r] = normed
        qkv = dot(normed, w_ref[:, : 3 * cols]).astype(BF16)
        qkv_ref[r] = qkv
        parts = []
        for h in range(own_heads):
            at = h * head_dim
            q = qkv[:, at : at + head_dim]
            k = qkv[:, cols + at : cols + at + head_dim]
            v = qkv[:, 2 * cols + at : 2 * cols + at + head_dim]
            scores = dot(q, k, ((1,), (1,))) * scale + bias_ref[r, h]
            top = jnp.max(scores, axis=1, keepdims=True)
            raised = jnp.exp(scores - top)
            probs = raised * (1.0 / jnp.sum(raised, axis=1, keepdims=True))
            probs_ref[r, h] = probs
            parts.append(dot(probs.astype(BF16), v))
        attended = jnp.concatenate(parts, axis=1).astype(BF16)
        att_ref[r] = attended
        partial = dot(attended, wout_ref[...])
        keep_ref[r] = partial[:toks]
        send_ref[r] = partial[toks:].astype(BF16)


def route_tokens(experts, x_ref, keep_ref, came_ref, gains_ref, w_ref, chosen_ref, send_ref,
                 g_ref, middle_ref, gate_ref, out_ref):
    middle = x_ref[...].astype(F32) + (keep_ref[...] + came_ref[...].astype(F32))
    middle_ref[...] = middle
    normed = (middle * rms_inverse(middle) * gains_ref[1:2]).astype(BF16)
    both = jnp.concatenate([normed, g_ref[...]], axis=0)
    out_ref[...] = dot(send_ref[...], both).astype(BF16)
    probs = jax.nn.softmax(dot(normed, w_ref[...]), axis=-1)
    gate_ref[...] = jnp.sum(probs * chosen_ref[...], axis=1, keepdims=True)


def run_expert(capacity, place_ref, own_ref, other_ref, router_ref, inner_ref, outer_ref,
               buf_ref, dslot_ref, g_ref, probs_ref, gate_ref, hidden_ref, dpre_ref, keep_ref,
               send_ref, acc_ref):
    step = pl.program_id(0)
    slots = buf_ref.shape[0] // 2
    experts = router_ref.shape[1]
    pad = own_ref.shape[0] // (slots // capacity)

    @pl.when(step == 0)
    def _():
        shape = (slots, own_ref.shape[0])
        row = iota(shape, 0)
        source = row // capacity
        wanted = source * pad + (row - source * capacity)
        first = (iota(shape, 1) == wanted).astype(BF16)
        second = (iota(shape, 1) == wanted + capacity).astype(BF16)
        mine = (iota((1, experts), 1) == place_ref[0]).astype(F32)
        for side, ref in enumerate((own_ref, other_ref)):
            at = side * slots
            rows = ref[...]
            buffers = dot(first, rows).astype(BF16)
            buf_ref[at : at + slots] = buffers
            g = dot(second, rows)
            probs = jax.nn.softmax(dot(buffers, router_ref[...]), axis=-1)
            gate = jnp.sum(probs * mine, axis=1, keepdims=True)
            dslot_ref[at : at + slots] = (gate * g).astype(BF16)
            if side == 0:
                g_ref[...] = g.astype(BF16)
                probs_ref[...] = probs
                gate_ref[...] = gate
        acc_ref[...] = jnp.zeros_like(acc_ref)

    inner = inner_ref[...]
    outer = outer_ref[...]
    pre = dot(buf_ref[...], inner)
    cdf = 0.5 * (1.0 + lax.erf(pre * (0.5**0.5)))
    hidden = (pre * cdf).astype(BF16)
    hidden_ref[...] = hidden
    slope = cdf + pre * jnp.exp(-0.5 * pre * pre) * 0.3989422804014327
    dpre = (dot(dslot_ref[...], outer, ((1,), (1,))) * slope).astype(BF16)
    dpre_ref[...] = dpre
    acc_ref[0] += dot(hidden, outer)
    acc_ref[1] += dot(dpre, inner, ((1,), (1,)))

    @pl.when(step == pl.num_programs(0) - 1)
    def _():
        keep_ref[...] = acc_ref[:, :slots]
        send_ref[...] = acc_ref[:, slots:].astype(BF16)


def finish_expert(capacity, place_ref, keep_ref, came_ref, buf_ref, g_ref, probs_ref, gate_ref,
                  router_ref, result_ref, back_ref, grad_ref):
    slots = g_ref.shape[0]
    experts = router_ref.shape[1]
    pad = result_ref.shape[0] // (slots // capacity)
    total = (keep_ref[...] + came_ref[...].astype(F32)).astype(BF16)
    result = total[0]
    mine = (iota((1, experts), 1) == place_ref[0]).astype(F32)
    grad_gate = jnp.sum(g_ref[...].astype(F32) * result.astype(F32), axis=1, keepdims=True)
    grad_logits = (grad_gate * gate_ref[...] * (mine - probs_ref[...])).astype(BF16)
    grad_ref[...] = dot(buf_ref[...], grad_logits, ((0,), (0,))).astype(BF16)
    back = total[1].astype(F32) + dot(grad_logits, router_ref[...], ((1,), (1,)))
    shape = (result_ref.shape[0], slots)
    row = iota(shape, 0)
    source = row // pad
    inside = row - source * pad
    wanted = jnp.where(inside < capacity, source * capacity + inside, -1)
    expand = (iota(shape, 1) == wanted).astype(BF16)
    back_ref[...] = dot(expand, back.astype(BF16)).astype(BF16)
    result_ref[...] = dot(expand, result).astype(BF16)


def norm_two_backward(back_ref, spread_ref, middle_ref, gains_ref, g_ref, dmiddle_ref, da_ref,
                      gain_ref):
    middle = middle_ref[...]
    inverse = rms_inverse(middle)
    unit = middle * inverse
    grad_normed = dot(spread_ref[...], back_ref[...])
    gain_ref[...] = jnp.sum(grad_normed * unit, axis=0, keepdims=True)
    dmiddle = g_ref[...].astype(F32) + norm_backward(grad_normed, unit, inverse, gains_ref[1:2])
    dmiddle_ref[...] = dmiddle
    da_ref[...] = dmiddle.astype(BF16)


def finish_layer(result_ref, spread_ref, middle_ref, gate_ref, out_ref):
    combined = dot(spread_ref[...], result_ref[...])
    out_ref[...] = (middle_ref[...] + gate_ref[...] * combined).astype(BF16)


def attend_backward(scale, head_dim, buckets, own_ref, across_ref, wout_ref, att_ref, qkv_ref,
                    probs_ref, normed_ref, w_ref, x_own_ref, x_across_ref, gout_ref, gw_ref,
                    keep_ref, send_ref, gain_ref, table_ref):
    own_heads = probs_ref.shape[1]
    cols = own_heads * head_dim
    toks = own_ref.shape[1]
    length = 2 * toks
    width = own_ref.shape[2]
    flip = (iota((length, length), 0) + iota((length, length), 1) == length - 1).astype(BF16)
    wout = wout_ref[...]
    grads = []
    diagonals = [jnp.zeros((length, length), F32)] * own_heads
    for r in range(2):
        da = jnp.concatenate([own_ref[r], across_ref[r]], axis=0)
        grads.append(da)
        grad_att = dot(da, wout, ((1,), (1,))).astype(BF16)
        qkv = qkv_ref[r]
        parts = [[], [], []]
        for h in range(own_heads):
            at = h * head_dim
            q = qkv[:, at : at + head_dim]
            k = qkv[:, cols + at : cols + at + head_dim]
            v = qkv[:, 2 * cols + at : 2 * cols + at + head_dim]
            gh = grad_att[:, at : at + head_dim]
            probs = probs_ref[r, h]
            grad_probs = dot(gh, v, ((1,), (1,)))
            row_dot = jnp.sum(probs * grad_probs, axis=1, keepdims=True)
            ds = (probs * (grad_probs - row_dot)).astype(BF16)
            diagonals[h] = diagonals[h] + dot(flip, ds)
            parts[0].append(dot(ds, k) * scale)
            parts[1].append(dot(ds, q, ((0,), (0,))) * scale)
            parts[2].append(dot(probs.astype(BF16), gh, ((0,), (0,))))
        grad_qkv = jnp.concatenate(parts[0] + parts[1] + parts[2], axis=1).astype(BF16)
        weights = dot(normed_ref[r], grad_qkv, ((0,), (0,)))
        outs = dot(att_ref[r], da, ((0,), (0,)))
        grad_normed = dot(grad_qkv, w_ref[:, : 3 * cols], ((1,), (1,)))
        x = jnp.concatenate([x_own_ref[r], x_across_ref[r]], axis=0).astype(F32)
        gain = jnp.sum(grad_normed * (x * rms_inverse(x)), axis=0, keepdims=True)
        keep_ref[r] = grad_normed[:toks]
        send_ref[r] = grad_normed[toks:].astype(BF16)
        if r == 0:
            total, total_out, total_gain = weights, outs, gain
        else:
            total, total_out, total_gain = total + weights, total_out + outs, total_gain + gain
    gw_ref[...] = total.astype(BF16)
    gout_ref[...] = total_out.astype(BF16)
    gain_ref[...] = total_gain
    spot = iota((1, length), 1)
    offset = jnp.where(spot >= toks, spot - length, spot)
    bucket = bucket_of(offset, buckets)
    belongs = iota((buckets, length), 0) == bucket
    sums = []
    for h in range(own_heads):
        turned = pltpu.roll(diagonals[h], 1, 1, stride=1, stride_axis=0)
        by_offset = jnp.sum(turned, axis=0, keepdims=True)
        sums.append(jnp.sum(jnp.where(belongs, by_offset, 0.0), axis=1, keepdims=True))
    table_ref[...] = jnp.concatenate(sums, axis=1)


def gather_rows(w_out, place, sources):
    top = sources.bit_length() - 2
    if top != PAIR_BIT:
        w_out = lax.ppermute(w_out, "expert", swap_bits(sources))
    for level in range(top):
        bit = top if level == PAIR_BIT else level
        came = lax.ppermute(w_out, "expert", [(i, i ^ (1 << bit)) for i in range(sources)])
        low = (place >> bit) & 1 == 0
        w_out = jnp.where(
            low, jnp.concatenate([w_out, came], axis=0), jnp.concatenate([came, w_out], axis=0)
        )
    return w_out


def scatter_rows(grad, place, sources):
    top = sources.bit_length() - 2
    for level in reversed(range(top)):
        bit = top if level == PAIR_BIT else level
        middle = grad.shape[0] // 2
        low = (place >> bit) & 1 == 0
        away = jnp.where(low, grad[middle:], grad[:middle])
        came = lax.ppermute(
            away.astype(BF16), "expert", [(i, i ^ (1 << bit)) for i in range(sources)]
        )
        grad = jnp.where(low, grad[:middle], grad[middle:]).astype(F32) + came.astype(F32)
    if top != PAIR_BIT:
        grad = lax.ppermute(grad.astype(BF16), "expert", swap_bits(sources))
    return grad.astype(F32)


def swap_bits(sources):
    top = sources.bit_length() - 2
    pairs = []
    for i in range(sources):
        high, low = (i >> top) & 1, (i >> PAIR_BIT) & 1
        rest = i & ~((1 << top) | (1 << PAIR_BIT))
        pairs.append((i, rest | (low << top) | (high << PAIR_BIT)))
    return pairs


def local(
    tokens,
    gain_one,
    w_query,
    w_key,
    w_value,
    w_out,
    bias_table,
    gain_two,
    w_router,
    w_inner,
    w_outer,
    segment_ids,
    routes,
    out_grad,
):
    toks = tokens.shape[1]
    width = tokens.shape[2]
    heads = bias_table.shape[1]
    buckets = bias_table.shape[0]
    head_dim = width // heads
    own_heads = heads // 4
    cols = own_heads * head_dim
    length = 2 * toks
    scale = head_dim ** (-0.5)
    sources = lax.axis_size("expert")
    experts = sources
    capacity = (5 * toks + 4 * experts - 1) // (4 * experts)
    slots = experts * capacity
    pad = -(-capacity // 8) * 8
    pad_two = -(-2 * capacity // 8) * 8
    rows = w_query.shape[0]
    core = lax.axis_index("dp")
    place = lax.axis_index("expert")
    member = (place >> PAIR_BIT) & 1
    first_core = core == 0
    core_at = core.reshape(1).astype(jnp.int32)
    place_at = place.reshape(1).astype(jnp.int32)
    group_at = (2 * core + member).reshape(1).astype(jnp.int32)
    wide = -(-(3 * cols + experts + 2) // 128) * 128
    small = -(-(experts + 2) // 128) * 128

    gains = jnp.stack([gain_one, gain_two])
    (packed,) = kernel_call(
        pack_weights, [((rows, 3 * width + small), BF16)], w_query, w_key, w_value, w_router, gains
    )
    (message,) = kernel_call(
        functools.partial(spread_weights, cols),
        [((sources, 2 * rows, wide), BF16)],
        core_at, packed, swap_core(packed), scalars=1,
    )
    weights = exchange(message)
    weights = (
        weights.reshape(sources, 2, rows, wide).transpose(1, 0, 2, 3).reshape(width, wide)
    )
    router_w = weights[:, 3 * cols : 3 * cols + experts]
    out_w = gather_rows(w_out, place, sources)

    own_tokens = tokens.reshape(toks, width)
    x_own = jnp.stack([own_tokens, swap_pair(own_tokens)])
    x_across = swap_core(x_own)
    docs_two = jnp.concatenate([segment_ids, swap_pair(segment_ids)], axis=0)
    docs = jnp.where(first_core, docs_two, jnp.roll(docs_two, toks, axis=1))
    bias, spread, chosen, send = kernel_call(
        functools.partial(prepare, capacity, pad),
        [
            ((2, own_heads, length, length), F32),
            ((toks, experts * pad), BF16),
            ((toks, experts), F32),
            ((experts * pad_two, 2 * toks), BF16),
        ],
        core_at, group_at, bias_table, docs, routes.reshape(toks, 1), scalars=3,
    )
    g_low = out_grad.reshape(toks, width)

    qkv, normed, probs, attended, keep, away, gain_rows = kernel_call(
        functools.partial(attend, scale, head_dim, experts),
        [
            ((2, length, 3 * cols), BF16),
            ((2, length, width), BF16),
            ((2, own_heads, length, length), F32),
            ((2, length, cols), BF16),
            ((2, toks, width), F32),
            ((2, toks, width), BF16),
            ((8, width), F32),
        ],
        weights, x_own, x_across, bias, out_w,
    )
    keep = keep + swap_core(away).astype(F32)
    middle, gate, outgoing = kernel_call(
        functools.partial(route_tokens, experts),
        [((toks, width), F32), ((toks, 1), F32), ((experts * pad_two, width), BF16)],
        own_tokens, keep[0], swap_pair(keep[1].astype(BF16)), gain_rows, router_w, chosen, send,
        g_low,
    )
    incoming = exchange(outgoing.reshape(experts, pad_two, width)).reshape(-1, width)

    inner, outer = w_inner[0], w_outer[0]
    units = inner.shape[1]
    chunk = units // 3
    fixed = lambda shape: pl.BlockSpec(shape, lambda i: (0,) * len(shape))
    outs = [
        ((2 * slots, width), BF16, None),
        ((2 * slots, width), BF16, None),
        ((slots, width), BF16, None),
        ((slots, experts), F32, None),
        ((slots, 1), F32, None),
        ((2 * slots, units), BF16, pl.BlockSpec((2 * slots, chunk), lambda i: (0, i))),
        ((2 * slots, units), BF16, pl.BlockSpec((2 * slots, chunk), lambda i: (0, i))),
        ((2, slots, width), F32, None),
        ((2, slots, width), BF16, None),
    ]
    buffers, dslot, slot_g, slot_probs, slot_gate, hidden, dpre, keep, away = pl.pallas_call(
        functools.partial(run_expert, capacity),
        grid=(units // chunk,),
        out_shape=[jax.ShapeDtypeStruct(shape, dtype) for shape, dtype, _ in outs],
        in_specs=[
            pl.BlockSpec(memory_space=pltpu.SMEM),
            fixed((experts * pad_two, width)),
            fixed((experts * pad_two, width)),
            fixed((width, experts)),
            pl.BlockSpec((width, chunk), lambda i: (0, i)),
            pl.BlockSpec((chunk, width), lambda i: (i, 0)),
        ],
        out_specs=[spec or fixed(shape) for shape, _, spec in outs],
        scratch_shapes=[pltpu.VMEM((2, 2 * slots, width), F32)],
        compiler_params=pltpu.CompilerParams(vmem_limit_bytes=VMEM_BYTES),
    )(place_at, incoming, swap_core(incoming), router_w, inner, outer)
    grad_outer = dot(hidden, dslot, ((0,), (0,)))
    grad_inner = dot(buffers, dpre, ((0,), (0,)))
    result, back, grad_router = kernel_call(
        functools.partial(finish_expert, capacity),
        [
            ((sources * pad, width), BF16),
            ((sources * pad, width), BF16),
            ((width, experts), BF16),
        ],
        place_at, keep, swap_core(away), buffers[:slots], slot_g, slot_probs, slot_gate, router_w,
        scalars=1,
    )
    back = exchange(back.reshape(sources, pad, width)).reshape(-1, width)
    result = exchange(result.reshape(sources, pad, width)).reshape(-1, width)

    grad_middle, grad_attn, grad_gain_two = kernel_call(
        norm_two_backward,
        [((toks, width), F32), ((toks, width), BF16), ((1, width), F32)],
        back, spread, middle, gain_rows, g_low,
    )
    g_own = jnp.stack([grad_attn, swap_pair(grad_attn)])
    grad_out, grad_weights, keep, away, grad_gain_one, grad_table = kernel_call(
        functools.partial(attend_backward, scale, head_dim, buckets),
        [
            ((cols, width), BF16),
            ((width, 3 * cols), BF16),
            ((2, toks, width), F32),
            ((2, toks, width), BF16),
            ((1, width), F32),
            ((buckets, own_heads), F32),
        ],
        g_own, swap_core(g_own), out_w, attended, qkv, probs, normed, weights, x_own, x_across,
    )
    (final,) = kernel_call(
        finish_layer, [((toks, width), BF16)], result, spread, middle, gate
    )
    grad_out = scatter_rows(grad_out, place, sources)

    table_cols = max(1, own_heads * buckets // (2 * rows))
    table_rows = own_heads * buckets // table_cols
    table_part = jnp.zeros((2 * rows, table_cols), F32)
    table_part = table_part.at[:table_rows].set(grad_table.reshape(table_rows, table_cols))
    narrow = jnp.concatenate([grad_gain_one, grad_gain_two], axis=0).T.astype(BF16)
    narrow = jnp.concatenate([grad_weights, grad_router, narrow], axis=1)
    spread_cols = narrow.shape[1]
    narrow = narrow.reshape(2, sources, rows, spread_cols).transpose(1, 0, 2, 3)
    narrow = narrow.reshape(sources, 2 * rows, spread_cols)
    table_part = jnp.broadcast_to(
        table_part[None].astype(BF16), (sources, 2 * rows, table_cols)
    )
    message = jnp.concatenate([narrow, table_part], axis=2)
    arrived = exchange(message).astype(F32)
    by_parity = arrived.reshape(sources >> (PAIR_BIT + 1), 2, PAIR, 2 * rows, -1)
    summed = jnp.sum(by_parity, axis=(0, 2))
    by_member = summed[:, :, : 3 * cols].reshape(2, 2, rows, 3, cols)
    smalls = jnp.sum(summed[:, :, 3 * cols : spread_cols], axis=0)
    smalls = smalls.reshape(2, rows, spread_cols - 3 * cols)
    tables = summed[:, :table_rows, spread_cols:].reshape(2, buckets, own_heads)
    tables = tables.transpose(1, 0, 2).reshape(buckets, 2 * own_heads)
    mine_w = jnp.where(first_core, by_member[:, 0], by_member[:, 1])
    away_w = jnp.where(first_core, by_member[:, 1], by_member[:, 0])
    mine_s = jnp.where(first_core, smalls[0], smalls[1])
    away_s = jnp.where(first_core, smalls[1], smalls[0])
    came_w = swap_core(away_w.astype(BF16)).astype(F32)
    came_s = swap_core(away_s)
    came_t = swap_core(tables)
    full = jnp.where(first_core, jnp.stack([mine_w, came_w]), jnp.stack([came_w, mine_w]))
    full = full.transpose(3, 2, 0, 1, 4).reshape(3, rows, width)
    smalls = mine_s + came_s
    table_sum = jnp.where(
        first_core,
        jnp.concatenate([tables, came_t], axis=1),
        jnp.concatenate([came_t, tables], axis=1),
    )

    keep = keep + swap_core(away).astype(F32)
    grad_normed_one = keep[0] + swap_pair(keep[1].astype(BF16)).astype(F32)
    x = own_tokens.astype(F32)
    inverse_one = rms_inverse(x)
    grad_input = grad_middle + norm_backward(
        grad_normed_one, x * inverse_one, inverse_one, gain_rows[0:1]
    )
    return (
        final.reshape(tokens.shape),
        grad_input.astype(BF16).reshape(tokens.shape),
        smalls[:, experts],
        full[0],
        full[1],
        full[2],
        grad_out,
        table_sum,
        smalls[:, experts + 1],
        smalls[:, :experts],
        grad_inner[None],
        grad_outer[None],
    )


def solution(mesh):
    both = ("dp", "expert")
    return jax.shard_map(
        local,
        mesh=mesh,
        in_specs=(
            P("expert", "dp", None),
            P(both),
            P(both, None),
            P(both, None),
            P(both, None),
            P(both, None),
            P(),
            P(both),
            P(both, None),
            P("expert", None, "dp"),
            P("expert", "dp", None),
            P("expert", None),
            P("expert", "dp", None),
            P("expert", "dp", None),
        ),
        out_specs=(
            P("expert", "dp", None),
            P("expert", "dp", None),
            P(both),
            P(both, None),
            P(both, None),
            P(both, None),
            P(both, None),
            P(),
            P(both),
            P(both, None),
            P("expert", None, "dp"),
            P("expert", "dp", None),
        ),
        check_vma=False,
    )
```

```python
import functools

import jax
import jax.numpy as jnp
from jax import lax
from jax.experimental import pallas as pl
from jax.experimental.pallas import tpu as pltpu
from jax.sharding import PartitionSpec as P

EPSILON = 1e-06
MASKED = -1000000000.0
BUCKET_EDGES = (1, 2, 3, 4, 5, 6, 7, 8, 12, 16, 23, 32, 46, 64, 91)
F32 = jnp.float32
BF16 = jnp.bfloat16
VMEM_BYTES = 24 * 1024 * 1024


def dot(left, right, dims=((1,), (0,))):
    return lax.dot_general(left, right, (dims, ((), ())), preferred_element_type=F32)


def rms_inverse(values):
    return lax.rsqrt(jnp.mean(values * values, axis=-1, keepdims=True) + EPSILON)


def norm_backward(grad_normed, unit_values, inverse, gain_values):
    grad_unit = grad_normed * gain_values
    projected = jnp.mean(grad_unit * unit_values, axis=-1, keepdims=True)
    return inverse * (grad_unit - unit_values * projected)


def swap_core(value):
    return lax.ppermute(value, "dp", [(0, 1), (1, 0)])


def swap_pair(value):
    n = lax.axis_size("expert")
    other = 3 * n // 4
    return lax.ppermute(value, "expert", [(i, i ^ other) for i in range(n)])


def exchange(value):
    return lax.all_to_all(value, "expert", split_axis=0, concat_axis=0, tiled=True)


def exchange_half(value):
    half = lax.axis_size("expert") // 2
    groups = [[q * half + s for s in range(half)] for q in range(2)]
    return lax.all_to_all(
        value, "expert", split_axis=0, concat_axis=0, tiled=True, axis_index_groups=groups
    )


def bucket_of(offset, total):
    distance = jnp.abs(offset)
    bucket = jnp.zeros(offset.shape, jnp.int32)
    for border in BUCKET_EDGES:
        bucket = bucket + (distance >= border).astype(jnp.int32)
    return bucket + total // 2 * (offset > 0).astype(jnp.int32)


def iota(shape, axis):
    return lax.broadcasted_iota(jnp.int32, shape, axis)


def kernel_call(body, outs, *args, scalars=0, flops=1_000_000, nbytes=1_000_000):
    specs = [pl.BlockSpec(memory_space=pltpu.SMEM)] * scalars
    specs += [pl.BlockSpec(memory_space=pltpu.VMEM)] * (len(args) - scalars)
    return pl.pallas_call(
        body,
        out_shape=[jax.ShapeDtypeStruct(shape, dtype) for shape, dtype in outs],
        in_specs=specs,
        out_specs=[pl.BlockSpec(memory_space=pltpu.VMEM)] * len(outs),
        compiler_params=pltpu.CompilerParams(vmem_limit_bytes=VMEM_BYTES),
        cost_estimate=pl.CostEstimate(flops=flops, bytes_accessed=nbytes, transcendentals=0),
    )(*args)


def choose(index, values):
    picked = values[0]
    for i in range(1, len(values)):
        picked = jnp.where(index == i, values[i], picked)
    return picked


def pack_weights(group_ref, q_ref, k_ref, v_ref, router_ref, gains_ref, *out_refs):
    rows, width = q_ref.shape
    experts = router_ref.shape[1]
    cols = width // 4
    eye = iota((rows, rows), 0) == iota((rows, rows), 1)
    columns = [
        jnp.sum(jnp.where(eye, gains_ref[i : i + 1, :].astype(F32), 0.0), axis=1, keepdims=True)
        for i in range(2)
    ]
    pad = out_refs[0].shape[1] - 3 * cols - experts - 2
    small = jnp.concatenate(
        [router_ref[...].astype(F32)] + columns + [jnp.zeros((rows, pad), F32)], axis=1
    ).astype(BF16)
    pieces = [
        jnp.concatenate(
            [ref[:, j * cols : (j + 1) * cols] for ref in (q_ref, k_ref, v_ref)] + [small], axis=1
        )
        for j in range(4)
    ]
    for d, out_ref in enumerate(out_refs):
        out_ref[...] = choose(group_ref[0] ^ d, pieces)


def spread_weights(group_ref, p0_ref, p1_ref, p2_ref, p3_ref, wout_ref, out_ref):
    dests, _, wide = out_ref.shape
    rows, used = p0_ref.shape
    pieces = [ref[...] for ref in (p0_ref, p1_ref, p2_ref, p3_ref)]
    value = jnp.concatenate([choose(group_ref[0] ^ j, pieces) for j in range(4)], axis=0)
    if wide > used:
        value = jnp.concatenate([value, jnp.zeros((4 * rows, wide - used), BF16)], axis=1)
    last = wout_ref[...]
    if wide > last.shape[1]:
        last = jnp.concatenate([last, jnp.zeros((rows, wide - last.shape[1]), BF16)], axis=1)
    value = jnp.concatenate([value, last], axis=0)
    for dest in range(dests):
        out_ref[dest] = value


def prepare(capacity, pad_two, group_ref, table_ref, docs_ref, routes_ref, own_bias_ref,
            pair_bias_ref, spread_ref, later_ref, gather_ref, send_ref):
    buckets = table_ref.shape[0]
    own_heads = own_bias_ref.shape[0]
    length = docs_ref.shape[1]
    toks = length // 2
    group = group_ref[0]
    spot = iota((1, length), 1)
    offset = jnp.where(spot >= toks, spot - length, spot)
    bucket = bucket_of(offset, buckets)
    vectors = []
    for h in range(own_heads):
        vector = jnp.zeros((1, length), F32)
        for b in range(buckets):
            vector = jnp.where(bucket == b, table_ref[b, group * own_heads + h], vector)
        full = jnp.broadcast_to(vector, (length, length))
        vectors.append(pltpu.roll(full, 0, 1, stride=1, stride_axis=0))
    for r, bias_ref in enumerate((own_bias_ref, pair_bias_ref)):
        across = jnp.broadcast_to(docs_ref[r : r + 1, :].astype(F32), (length, length))
        same = across == jnp.transpose(across)
        for h in range(own_heads):
            bias_ref[h] = jnp.where(same, vectors[h], MASKED)
    experts = spread_ref.shape[1] // pad_two
    route = routes_ref[...]
    chosen = route == iota((toks, experts), 1)
    lower = (iota((toks, toks), 0) > iota((toks, toks), 1)).astype(BF16)
    counts = dot(lower, chosen.astype(BF16))
    slot = jnp.sum(jnp.where(chosen, counts, 0.0), axis=1, keepdims=True).astype(jnp.int32)
    kept = slot < capacity
    place = jnp.where(kept, route * pad_two + slot, -1)
    later = jnp.where(kept, route * pad_two + capacity + slot, -1)
    across = iota((toks, experts * pad_two), 1)
    first = (place == across).astype(F32)
    second = (later == across).astype(F32)
    spread_ref[...] = first.astype(BF16)
    later_ref[...] = second.astype(BF16)
    send_ref[:, :toks] = jnp.transpose(first).astype(BF16)
    send_ref[:, toks:] = jnp.transpose(second).astype(BF16)
    gather_ref[...] = chosen.astype(F32)


def place_weights(arrived_ref, w_ref, wout_ref):
    sources, total, _ = arrived_ref.shape
    rows = total // 5
    used = w_ref.shape[1]
    width = wout_ref.shape[1]
    block = sources * rows
    for s in range(sources):
        for j in range(4):
            w_ref[j * block + s * rows : j * block + (s + 1) * rows] = arrived_ref[
                s, j * rows : (j + 1) * rows, :used
            ]
        wout_ref[s * rows : (s + 1) * rows] = arrived_ref[s, 4 * rows :, :width]


def gain_rows(experts, cols, w_ref, gains_ref):
    small = w_ref[:, 3 * cols :]
    pick = (iota((8, small.shape[1]), 1) == iota((8, small.shape[1]), 0) + experts).astype(BF16)
    gains_ref[...] = dot(pick, small, ((1,), (1,)))


def attend(scale, head_dim, w_ref, wout_ref, gains_ref, own_ref, across_ref, bias_ref, qkv_ref,
           probs_ref, att_ref, keep_ref, send_ref):
    own_heads = bias_ref.shape[0]
    cols = own_heads * head_dim
    toks = own_ref.shape[0]
    x = jnp.concatenate([own_ref[...], across_ref[...]], axis=0).astype(F32)
    normed = (x * rms_inverse(x) * gains_ref[0:1]).astype(BF16)
    qkv = dot(normed, w_ref[:, : 3 * cols]).astype(BF16)
    qkv_ref[...] = qkv
    parts = []
    for h in range(own_heads):
        at = h * head_dim
        q = qkv[:, at : at + head_dim]
        k = qkv[:, cols + at : cols + at + head_dim]
        v = qkv[:, 2 * cols + at : 2 * cols + at + head_dim]
        scores = dot(q, k, ((1,), (1,))) * scale + bias_ref[h]
        top = jnp.max(scores, axis=1, keepdims=True)
        raised = jnp.exp(scores - top)
        probs = raised * (1.0 / jnp.sum(raised, axis=1, keepdims=True))
        probs_ref[h] = probs
        parts.append(dot(probs.astype(BF16), v))
    attended = jnp.concatenate(parts, axis=1).astype(BF16)
    att_ref[...] = attended
    partial = dot(attended, wout_ref[...])
    keep_ref[...] = partial[:toks]
    send_ref[...] = partial[toks:].astype(BF16)


def attend_first(scale, head_dim, experts, arrived_ref, own_ref, across_ref, bias_ref, w_ref,
                 wout_ref, gains_ref, *out_refs):
    place_weights(arrived_ref, w_ref, wout_ref)
    gain_rows(experts, bias_ref.shape[0] * head_dim, w_ref, gains_ref)
    attend(scale, head_dim, w_ref, wout_ref, gains_ref, own_ref, across_ref, bias_ref, *out_refs)


def attend_first_placed(scale, head_dim, experts, w_ref, wout_ref, own_ref, across_ref, bias_ref,
                        gains_ref, *out_refs):
    gain_rows(experts, bias_ref.shape[0] * head_dim, w_ref, gains_ref)
    attend(scale, head_dim, w_ref, wout_ref, gains_ref, own_ref, across_ref, bias_ref, *out_refs)


def route_tokens(x_ref, keep_ref, core_ref, came_ref, gains_ref, w_ref, chosen_ref, send_ref,
                 g_ref, middle_ref, gate_ref, out_ref):
    middle = x_ref[...].astype(F32) + (
        (keep_ref[...] + core_ref[...].astype(F32)) + came_ref[...].astype(F32)
    )
    middle_ref[...] = middle
    normed = (middle * rms_inverse(middle) * gains_ref[1:2]).astype(BF16)
    both = jnp.concatenate([normed, g_ref[...]], axis=0)
    out_ref[...] = dot(send_ref[...], both).astype(BF16)
    probs = jax.nn.softmax(dot(normed, w_ref[...]), axis=-1)
    gate_ref[...] = jnp.sum(probs * chosen_ref[...], axis=1, keepdims=True)


def run_expert(capacity, place_ref, own_ref, other_ref, router_ref, inner_ref, outer_ref,
               buf_ref, dslot_ref, g_ref, probs_ref, gate_ref, hidden_ref, dpre_ref, keep_ref,
               send_ref, acc_ref):
    step = pl.program_id(0)
    slots = buf_ref.shape[0] // 2
    experts = router_ref.shape[1]
    pad = own_ref.shape[0] // (slots // capacity)

    @pl.when(step == 0)
    def _():
        shape = (slots, own_ref.shape[0])
        row = iota(shape, 0)
        source = row // capacity
        wanted = source * pad + (row - source * capacity)
        first = (iota(shape, 1) == wanted).astype(BF16)
        second = (iota(shape, 1) == wanted + capacity).astype(BF16)
        mine = (iota((1, experts), 1) == place_ref[0]).astype(F32)
        for side, ref in enumerate((own_ref, other_ref)):
            at = side * slots
            rows = ref[...]
            buffers = dot(first, rows).astype(BF16)
            buf_ref[at : at + slots] = buffers
            g = dot(second, rows)
            probs = jax.nn.softmax(dot(buffers, router_ref[...]), axis=-1)
            gate = jnp.sum(probs * mine, axis=1, keepdims=True)
            dslot_ref[at : at + slots] = (gate * g).astype(BF16)
            if side == 0:
                g_ref[...] = g.astype(BF16)
                probs_ref[...] = probs
                gate_ref[...] = gate
        acc_ref[...] = jnp.zeros_like(acc_ref)

    inner = inner_ref[...]
    outer = outer_ref[...]
    pre = dot(buf_ref[...], inner)
    cdf = 0.5 * (1.0 + lax.erf(pre * (0.5**0.5)))
    hidden = (pre * cdf).astype(BF16)
    hidden_ref[...] = hidden
    slope = cdf + pre * jnp.exp(-0.5 * pre * pre) * 0.3989422804014327
    dpre = (dot(dslot_ref[...], outer, ((1,), (1,))) * slope).astype(BF16)
    dpre_ref[...] = dpre
    acc_ref[0] += dot(hidden, outer)
    acc_ref[1] += dot(dpre, inner, ((1,), (1,)))

    @pl.when(step == pl.num_programs(0) - 1)
    def _():
        keep_ref[...] = acc_ref[:, :slots]
        send_ref[...] = acc_ref[:, slots:].astype(BF16)


def finish_expert(capacity, place_ref, keep_ref, came_ref, buf_ref, g_ref, probs_ref, gate_ref,
                  router_ref, out_ref, grad_ref):
    slots = g_ref.shape[0]
    experts = router_ref.shape[1]
    pad = out_ref.shape[0] // (slots // capacity)
    total = (keep_ref[...] + came_ref[...].astype(F32)).astype(BF16)
    result = total[0]
    mine = (iota((1, experts), 1) == place_ref[0]).astype(F32)
    grad_gate = jnp.sum(g_ref[...].astype(F32) * result.astype(F32), axis=1, keepdims=True)
    grad_logits = (grad_gate * gate_ref[...] * (mine - probs_ref[...])).astype(BF16)
    grad_ref[...] = dot(buf_ref[...], grad_logits, ((0,), (0,))).astype(BF16)
    back = total[1].astype(F32) + dot(grad_logits, router_ref[...], ((1,), (1,)))
    shape = (out_ref.shape[0], 2 * slots)
    row = iota(shape, 0)
    source = row // pad
    inside = row - source * pad
    wanted = jnp.where(
        inside < capacity,
        source * capacity + inside,
        jnp.where(inside < 2 * capacity, slots + source * capacity + inside - capacity, -1),
    )
    expand = (iota(shape, 1) == wanted).astype(BF16)
    both = jnp.concatenate([back.astype(BF16), result], axis=0)
    out_ref[...] = dot(expand, both).astype(BF16)


def norm_two_backward(back_ref, spread_ref, middle_ref, gains_ref, g_ref, dmiddle_ref, da_ref,
                      gain_ref):
    middle = middle_ref[...]
    inverse = rms_inverse(middle)
    unit = middle * inverse
    grad_normed = dot(spread_ref[...], back_ref[...])
    gain_ref[...] = jnp.sum(grad_normed * unit, axis=0, keepdims=True)
    dmiddle = g_ref[...].astype(F32) + norm_backward(grad_normed, unit, inverse, gains_ref[1:2])
    dmiddle_ref[...] = dmiddle
    da_ref[...] = dmiddle.astype(BF16)


def finish_layer(result_ref, spread_ref, middle_ref, gate_ref, out_ref):
    combined = dot(spread_ref[...], result_ref[...])
    out_ref[...] = (middle_ref[...] + gate_ref[...] * combined).astype(BF16)


def attend_backward(scale, head_dim, own_ref, across_ref, wout_ref, att_ref, qkv_ref, probs_ref,
                    gains_ref, w_ref, x_own_ref, x_across_ref):
    own_heads = probs_ref.shape[0]
    cols = own_heads * head_dim
    length = 2 * own_ref.shape[0]
    flip = (iota((length, length), 0) + iota((length, length), 1) == length - 1).astype(BF16)
    da = jnp.concatenate([own_ref[...], across_ref[...]], axis=0)
    grad_att = dot(da, wout_ref[...], ((1,), (1,))).astype(BF16)
    qkv = qkv_ref[...]
    parts = [[], [], []]
    offsets = []
    for h in range(own_heads):
        at = h * head_dim
        q = qkv[:, at : at + head_dim]
        k = qkv[:, cols + at : cols + at + head_dim]
        v = qkv[:, 2 * cols + at : 2 * cols + at + head_dim]
        gh = grad_att[:, at : at + head_dim]
        probs = probs_ref[h]
        grad_probs = dot(gh, v, ((1,), (1,)))
        row_dot = jnp.sum(probs * grad_probs, axis=1, keepdims=True)
        ds = (probs * (grad_probs - row_dot)).astype(BF16)
        turned = pltpu.roll(dot(flip, ds), 1, 1, stride=1, stride_axis=0)
        offsets.append(jnp.sum(turned, axis=0, keepdims=True))
        parts[0].append(dot(ds, k) * scale)
        parts[1].append(dot(ds, q, ((0,), (0,))) * scale)
        parts[2].append(dot(probs.astype(BF16), gh, ((0,), (0,))))
    grad_qkv = jnp.concatenate(parts[0] + parts[1] + parts[2], axis=1).astype(BF16)
    x = jnp.concatenate([x_own_ref[...], x_across_ref[...]], axis=0).astype(F32)
    unit = x * rms_inverse(x)
    normed = (unit * gains_ref[0:1]).astype(BF16)
    weights = dot(normed, grad_qkv, ((0,), (0,)))
    outs = dot(att_ref[...], da, ((0,), (0,)))
    grad_normed = dot(grad_qkv, w_ref[:, : 3 * cols], ((1,), (1,)))
    gain = jnp.sum(grad_normed * unit, axis=0, keepdims=True)
    return weights, outs, grad_normed, gain, offsets


def backward_own(scale, head_dim, *refs):
    gw_ref, gout_ref, keep_ref, gain_ref, offsets_ref = refs[10:]
    weights, outs, grad_normed, gain, offsets = attend_backward(scale, head_dim, *refs[:10])
    gw_ref[...] = weights
    gout_ref[...] = outs
    keep_ref[...] = grad_normed
    gain_ref[...] = gain
    for h, value in enumerate(offsets):
        offsets_ref[h : h + 1] = value


def backward_pair(scale, head_dim, buckets, table_cols, *refs):
    gw_ref, gout_ref, gain_ref, offsets_ref, gain_two_ref, router_ref = refs[10:16]
    send_ref, full_ref, out_ref = refs[16:]
    weights, outs, grad_normed, gain, offsets = attend_backward(scale, head_dim, *refs[:10])
    own_heads = offsets_ref.shape[0]
    width, experts = router_ref.shape
    length = offsets_ref.shape[1]
    toks = length // 2
    send_ref[...] = grad_normed.astype(BF16)
    rows = own_heads * buckets // table_cols
    spot = iota((1, length), 1)
    offset = jnp.where(spot >= toks, spot - length, spot)
    bucket = bucket_of(offset, buckets)
    table = []
    for t in range(table_cols):
        column = jnp.zeros((rows, 1), F32)
        for h in range(own_heads):
            belongs = iota((rows, length), 0) * table_cols + t == bucket * own_heads + h
            value = offsets[h] + offsets_ref[h : h + 1]
            column = column + jnp.sum(jnp.where(belongs, value, 0.0), axis=1, keepdims=True)
        table.append(column)
    table = jnp.concatenate([jnp.concatenate(table, axis=1)] * (width // rows), axis=0)
    narrow = jnp.concatenate(
        [gain_ref[...] + gain, gain_two_ref[...], jnp.zeros((6, width), F32)], axis=0
    )
    narrow = jnp.transpose(narrow)[:, :2]
    weights = weights + gw_ref[...]
    pieces = [weights, router_ref[...].astype(F32), narrow, table]
    spare = full_ref.shape[-1] - sum(p.shape[1] for p in pieces)
    if len(full_ref.shape) == 2:
        full_ref[...] = jnp.concatenate(
            pieces + [jnp.zeros((width, spare), F32)], axis=1
        ).astype(BF16)
        out_ref[...] = (outs + gout_ref[...]).astype(BF16)


def backward_pair_message(scale, head_dim, buckets, table_cols, *refs):
    *rest, send_ref, message_ref, full_ref, out_ref = refs
    backward_pair(scale, head_dim, buckets, table_cols, *rest, send_ref, full_ref, out_ref)
    dests, total, wide = message_ref.shape
    rows = total // 5
    used = full_ref.shape[1]
    block = dests * rows
    for s in range(dests):
        for j in range(4):
            at = j * block + s * rows
            message_ref[s, j * rows : (j + 1) * rows, :used] = full_ref[at : at + rows]
            if wide > used:
                message_ref[s, j * rows : (j + 1) * rows, used:] = jnp.zeros(
                    (rows, wide - used), BF16
                )
        width = out_ref.shape[1]
        message_ref[s, 4 * rows :, :width] = out_ref[s * rows : (s + 1) * rows]
        if wide > width:
            message_ref[s, 4 * rows :, width:] = jnp.zeros((rows, wide - width), BF16)


def sum_arrived(group_ref, arrived_ref, out_ref, own_ref, *send_refs):
    rows, used = own_ref.shape
    total = arrived_ref[0].astype(F32)
    for s in range(1, arrived_ref.shape[0]):
        total = total + arrived_ref[s].astype(F32)
    out_ref[...] = total[4 * rows :, : out_ref.shape[1]]
    pieces = [total[j * rows : (j + 1) * rows, :used] for j in range(4)]
    own_ref[...] = choose(group_ref[0], pieces)
    for d, ref in enumerate(send_refs):
        ref[...] = choose(group_ref[0] ^ (d + 1), pieces).astype(BF16)


def finish_weights(own_heads, buckets, table_cols, group_ref, p0_ref, p1_ref, p2_ref, p3_ref,
                   q_ref, k_ref, v_ref, router_ref, gains_ref, table_ref):
    rows, width = q_ref.shape
    experts = router_ref.shape[1]
    cols = width // 4
    pieces = [ref[...].astype(F32) for ref in (p0_ref, p1_ref, p2_ref, p3_ref)]
    ordered = [choose(group_ref[0] ^ j, pieces) for j in range(4)]
    for n, ref in enumerate((q_ref, k_ref, v_ref)):
        ref[...] = jnp.concatenate([p[:, n * cols : (n + 1) * cols] for p in ordered], axis=1)
    at = 3 * cols
    small = sum(p[:, at : at + experts + 2] for p in pieces)
    router_ref[...] = small[:, :experts]
    eye = iota((rows, rows), 0) == iota((rows, rows), 1)
    for i in range(2):
        column = small[:, experts + i : experts + i + 1]
        gains_ref[i : i + 1] = jnp.sum(jnp.where(eye, column, 0.0), axis=0, keepdims=True)
    at += experts + 2
    lines = []
    lane = iota((rows, 128), 1)
    for p in ordered:
        for h in range(own_heads):
            line = jnp.zeros((1, 128), F32)
            for t in range(table_cols):
                belongs = iota((rows, 128), 0) * table_cols + t == lane * own_heads + h
                value = jnp.where(belongs & (lane < buckets), p[:, at + t : at + t + 1], 0.0)
                line = line + jnp.sum(value, axis=0, keepdims=True)
            lines.append(line)
    heads = len(lines)
    padded = jnp.concatenate(lines + [jnp.zeros((128 - heads, 128), F32)], axis=0)
    table_ref[...] = jnp.transpose(padded)[:buckets, :heads]


def local(
    tokens,
    gain_one,
    w_query,
    w_key,
    w_value,
    w_out,
    bias_table,
    gain_two,
    w_router,
    w_inner,
    w_outer,
    segment_ids,
    routes,
    out_grad,
):
    toks = tokens.shape[1]
    width = tokens.shape[2]
    heads = bias_table.shape[1]
    buckets = bias_table.shape[0]
    head_dim = width // heads
    own_heads = heads // 4
    cols = own_heads * head_dim
    length = 2 * toks
    scale = head_dim ** (-0.5)
    sources = lax.axis_size("expert")
    experts = sources
    capacity = (5 * toks + 4 * experts - 1) // (4 * experts)
    slots = experts * capacity
    pad_two = -(-2 * capacity // 8) * 8
    rows = w_query.shape[0]
    core = lax.axis_index("dp")
    place = lax.axis_index("expert")
    half = sources // 2
    member = place // half
    first_core = core == 0
    place_at = place.reshape(1).astype(jnp.int32)
    group_at = (2 * core + member).reshape(1).astype(jnp.int32)
    table_cols = max(1, own_heads * buckets // rows)
    used = -(-(3 * cols + experts + 2 + table_cols) // 128) * 128
    wide = max(used, width)
    aligned = rows % 8 == 0

    def across_group(pieces):
        return [
            lax.ppermute(
                piece,
                ("dp", "expert"),
                [
                    (c * sources + e, (c ^ (d >> 1)) * sources + (e ^ (half * (d & 1))))
                    for c in range(2)
                    for e in range(sources)
                ],
            )
            for d, piece in enumerate(pieces, 1)
        ]

    own_tokens = tokens.reshape(toks, width)
    pair_tokens = swap_pair(own_tokens)
    pair_docs = swap_pair(segment_ids)

    own_piece, *pieces = kernel_call(
        pack_weights, [((rows, used), BF16)] * 4,
        group_at, w_query, w_key, w_value, w_router, jnp.stack([gain_one, gain_two]), scalars=1,
    )
    pieces = across_group(pieces)
    pair_tokens, pair_docs, own_piece, *pieces = lax.optimization_barrier(
        (pair_tokens, pair_docs, own_piece, *pieces)
    )
    (message,) = kernel_call(
        spread_weights, [((half, 5 * rows, wide), BF16)],
        group_at, own_piece, *pieces, w_out, scalars=1,
    )
    arrived = exchange_half(message)

    own_across = swap_core(own_tokens)
    pair_across = swap_core(pair_tokens)
    docs_two = jnp.concatenate([segment_ids, pair_docs], axis=0)
    docs = jnp.where(first_core, docs_two, jnp.roll(docs_two, toks, axis=1))
    own_bias, pair_bias, spread, later, chosen, send = kernel_call(
        functools.partial(prepare, capacity, pad_two),
        [
            ((own_heads, length, length), F32),
            ((own_heads, length, length), F32),
            ((toks, experts * pad_two), BF16),
            ((toks, experts * pad_two), BF16),
            ((toks, experts), F32),
            ((experts * pad_two, 2 * toks), BF16),
        ],
        group_at, bias_table, docs, routes.reshape(toks, 1), scalars=2,
    )
    g_low = out_grad.reshape(toks, width)

    row_outs = [
        ((length, 3 * cols), BF16),
        ((own_heads, length, length), F32),
        ((length, cols), BF16),
        ((toks, width), F32),
        ((toks, width), BF16),
    ]
    placed = [((width, used), BF16), ((cols, width), BF16)]
    if aligned:
        weights, out_w, gains, *pair_kept = kernel_call(
            functools.partial(attend_first, scale, head_dim, experts),
            placed + [((8, width), F32)] + row_outs,
            arrived, pair_tokens, pair_across, pair_bias,
        )
    else:
        weights = arrived[:, : 4 * rows, :used].reshape(half, 2, 2, rows, used)
        weights = weights.transpose(1, 2, 0, 3, 4).reshape(width, used)
        out_w = arrived[:, 4 * rows :, :width].reshape(cols, width)
        gains, *pair_kept = kernel_call(
            functools.partial(attend_first_placed, scale, head_dim, experts),
            [((8, width), F32)] + row_outs,
            weights, out_w, pair_tokens, pair_across, pair_bias,
        )
    pair_qkv, pair_probs, pair_att, keep, away = pair_kept
    pair_sum = (keep + swap_core(away).astype(F32)).astype(BF16)
    pair_sum = swap_pair(pair_sum)
    own_qkv, own_probs, own_att, keep, away = kernel_call(
        functools.partial(attend, scale, head_dim), row_outs,
        weights, out_w, gains, own_tokens, own_across, own_bias,
    )
    router_w = weights[:, 3 * cols : 3 * cols + experts]
    middle, gate, outgoing = kernel_call(
        route_tokens,
        [((toks, width), F32), ((toks, 1), F32), ((experts * pad_two, width), BF16)],
        own_tokens, keep, swap_core(away), pair_sum, gains, router_w, chosen, send, g_low,
    )
    incoming = exchange(outgoing.reshape(experts, pad_two, width)).reshape(-1, width)

    inner, outer = w_inner[0], w_outer[0]
    units = inner.shape[1]
    chunk = units // 3
    fixed = lambda shape: pl.BlockSpec(shape, lambda i: (0,) * len(shape))
    outs = [
        ((2 * slots, width), BF16, None),
        ((2 * slots, width), BF16, None),
        ((slots, width), BF16, None),
        ((slots, experts), F32, None),
        ((slots, 1), F32, None),
        ((2 * slots, units), BF16, pl.BlockSpec((2 * slots, chunk), lambda i: (0, i))),
        ((2 * slots, units), BF16, pl.BlockSpec((2 * slots, chunk), lambda i: (0, i))),
        ((2, slots, width), F32, None),
        ((2, slots, width), BF16, None),
    ]
    buffers, dslot, slot_g, slot_probs, slot_gate, hidden, dpre, keep, away = pl.pallas_call(
        functools.partial(run_expert, capacity),
        grid=(units // chunk,),
        out_shape=[jax.ShapeDtypeStruct(shape, dtype) for shape, dtype, _ in outs],
        in_specs=[
            pl.BlockSpec(memory_space=pltpu.SMEM),
            fixed((experts * pad_two, width)),
            fixed((experts * pad_two, width)),
            fixed((width, experts)),
            pl.BlockSpec((width, chunk), lambda i: (0, i)),
            pl.BlockSpec((chunk, width), lambda i: (i, 0)),
        ],
        out_specs=[spec or fixed(shape) for shape, _, spec in outs],
        scratch_shapes=[pltpu.VMEM((2, 2 * slots, width), F32)],
        compiler_params=pltpu.CompilerParams(vmem_limit_bytes=VMEM_BYTES),
    )(place_at, incoming, swap_core(incoming), router_w, inner, outer)
    grad_outer = dot(hidden, dslot, ((0,), (0,)))
    grad_inner = dot(buffers, dpre, ((0,), (0,)))
    back, grad_router = kernel_call(
        functools.partial(finish_expert, capacity),
        [((sources * pad_two, width), BF16), ((width, experts), BF16)],
        place_at, keep, swap_core(away), buffers[:slots], slot_g, slot_probs, slot_gate, router_w,
        scalars=1,
    )
    back = exchange(back.reshape(sources, pad_two, width)).reshape(-1, width)

    grad_middle, grad_attn, grad_gain_two = kernel_call(
        norm_two_backward,
        [((toks, width), F32), ((toks, width), BF16), ((1, width), F32)],
        back, spread, middle, gains, g_low,
    )
    pair_grad = swap_pair(grad_attn)
    shared = (gains, weights)
    grad_w, grad_out, grad_normed, gain_part, offsets = kernel_call(
        functools.partial(backward_own, scale, head_dim),
        [
            ((width, 3 * cols), F32),
            ((cols, width), F32),
            ((length, width), F32),
            ((1, width), F32),
            ((own_heads, length), F32),
        ],
        grad_attn, swap_core(grad_attn), out_w, own_att, own_qkv, own_probs, *shared,
        own_tokens, own_across,
    )
    last = (
        pair_grad, swap_core(pair_grad), out_w, pair_att, pair_qkv, pair_probs, *shared,
        pair_tokens, pair_across, grad_w, grad_out, gain_part, offsets, grad_gain_two, grad_router,
    )
    outs = [((length, width), BF16), ((width, used), BF16), ((cols, width), BF16)]
    options = (scale, head_dim, buckets, table_cols)
    if aligned:
        away, message, _, _ = kernel_call(
            functools.partial(backward_pair_message, *options),
            [outs[0], ((half, 5 * rows, wide), BF16), *outs[1:]], *last,
        )
    else:
        away, full, grad_out = kernel_call(functools.partial(backward_pair, *options), outs, *last)
        full = full.reshape(2, 2, half, rows, used).transpose(2, 0, 1, 3, 4)
        full = full.reshape(half, 4 * rows, used)
        grad_out = grad_out.reshape(half, rows, width)
        message = jnp.concatenate(
            [
                jnp.pad(full, ((0, 0), (0, 0), (0, wide - used))),
                jnp.pad(grad_out, ((0, 0), (0, 0), (0, wide - width))),
            ],
            axis=1,
        )
    came = swap_pair(away)
    arrived = exchange_half(message)
    (final,) = kernel_call(finish_layer, [((toks, width), BF16)], back, later, middle, gate)

    out_grad_w, own_piece, *pieces = kernel_call(
        sum_arrived, [((rows, width), F32), ((rows, used), F32)] + [((rows, used), BF16)] * 3,
        group_at, arrived, scalars=1,
    )
    pieces = across_group(pieces)
    query_grad, key_grad, value_grad, router_grad, gain_grads, table_grad = kernel_call(
        functools.partial(finish_weights, own_heads, buckets, table_cols),
        [((rows, width), F32)] * 3
        + [((rows, experts), F32), ((2, rows), F32), ((buckets, heads), F32)],
        group_at, own_piece, *pieces, scalars=1,
    )

    grad_normed = grad_normed + came.astype(F32)
    across = swap_core(grad_normed[toks:].astype(BF16)).astype(F32)
    x = own_tokens.astype(F32)
    inverse_one = rms_inverse(x)
    grad_input = grad_middle + norm_backward(
        grad_normed[:toks] + across, x * inverse_one, inverse_one, gains[0:1]
    )
    return (
        final.reshape(tokens.shape),
        grad_input.astype(BF16).reshape(tokens.shape),
        gain_grads[0],
        query_grad,
        key_grad,
        value_grad,
        out_grad_w,
        table_grad,
        gain_grads[1],
        router_grad,
        grad_inner[None],
        grad_outer[None],
    )


def solution(mesh):
    both = ("dp", "expert")
    return jax.shard_map(
        local,
        mesh=mesh,
        in_specs=(
            P("expert", "dp", None),
            P(both),
            P(both, None),
            P(both, None),
            P(both, None),
            P(both, None),
            P(),
            P(both),
            P(both, None),
            P("expert", None, "dp"),
            P("expert", "dp", None),
            P("expert", None),
            P("expert", "dp", None),
            P("expert", "dp", None),
        ),
        out_specs=(
            P("expert", "dp", None),
            P("expert", "dp", None),
            P(both),
            P(both, None),
            P(both, None),
            P(both, None),
            P(both, None),
            P(),
            P(both),
            P(both, None),
            P("expert", None, "dp"),
            P("expert", "dp", None),
        ),
        check_vma=False,
    )
```

```python
import functools

import jax
import jax.numpy as jnp
from jax import lax
from jax.experimental import pallas as pl
from jax.experimental.pallas import tpu as pltpu
from jax.sharding import PartitionSpec as P

EPSILON = 1e-06
MASKED = -1000000000.0
BUCKET_EDGES = (1, 2, 3, 4, 5, 6, 7, 8, 12, 16, 23, 32, 46, 64, 91)
F32 = jnp.float32
BF16 = jnp.bfloat16
VMEM_BYTES = 24 * 1024 * 1024


def dot(left, right, dims=((1,), (0,))):
    return lax.dot_general(left, right, (dims, ((), ())), preferred_element_type=F32)


def rms_inverse(values):
    return lax.rsqrt(jnp.mean(values * values, axis=-1, keepdims=True) + EPSILON)


def norm_backward(grad_normed, unit_values, inverse, gain_values):
    grad_unit = grad_normed * gain_values
    projected = jnp.mean(grad_unit * unit_values, axis=-1, keepdims=True)
    return inverse * (grad_unit - unit_values * projected)


def swap_core(value):
    return lax.ppermute(value, "dp", [(0, 1), (1, 0)])


def swap_pair(value):
    n = lax.axis_size("expert")
    other = 3 * n // 4
    return lax.ppermute(value, "expert", [(i, i ^ other) for i in range(n)])


def exchange(value):
    return lax.all_to_all(value, "expert", split_axis=0, concat_axis=0, tiled=True)


def exchange_half(value):
    half = lax.axis_size("expert") // 2
    groups = [[q * half + s for s in range(half)] for q in range(2)]
    return lax.all_to_all(
        value, "expert", split_axis=0, concat_axis=0, tiled=True, axis_index_groups=groups
    )


def bucket_of(offset, total):
    distance = jnp.abs(offset)
    bucket = jnp.zeros(offset.shape, jnp.int32)
    for border in BUCKET_EDGES:
        bucket = bucket + (distance >= border).astype(jnp.int32)
    return bucket + total // 2 * (offset > 0).astype(jnp.int32)


def iota(shape, axis):
    return lax.broadcasted_iota(jnp.int32, shape, axis)


class LateRef:
    def __init__(self, source, target, sem):
        self.copy = pltpu.make_async_copy(source, target, sem)
        self.target = target
        self.shape = target.shape
        self.pending = True
        self.copy.start()

    def wait(self):
        if self.pending:
            self.copy.wait()
            self.pending = False

    def __getitem__(self, index):
        self.wait()
        return self.target[index]


def kernel_call(body, outs, *args, scalars=0, late=(), limit=VMEM_BYTES):
    count = len(args)
    late = sorted(late)

    def run(*refs):
        ins = list(refs[:count])
        out_refs = refs[count : count + len(outs)]
        scratch = refs[count + len(outs) :]
        for n, i in enumerate(late):
            ins[i] = LateRef(ins[i], scratch[n], scratch[-1].at[n])
        body(*ins, *out_refs)
        for i in late:
            ins[i].wait()

    spaces = [pltpu.SMEM if i < scalars else pltpu.VMEM for i in range(count)]
    for i in late:
        spaces[i] = pltpu.HBM
    scratch = [pltpu.VMEM(args[i].shape, args[i].dtype) for i in late]
    if late:
        scratch.append(pltpu.SemaphoreType.DMA((len(late),)))
    return pl.pallas_call(
        run,
        out_shape=[jax.ShapeDtypeStruct(shape, dtype) for shape, dtype in outs],
        in_specs=[pl.BlockSpec(memory_space=space) for space in spaces],
        out_specs=[pl.BlockSpec(memory_space=pltpu.VMEM)] * len(outs),
        scratch_shapes=scratch,
        compiler_params=pltpu.CompilerParams(vmem_limit_bytes=limit),
        cost_estimate=pl.CostEstimate(
            flops=1_000_000, bytes_accessed=1_000_000, transcendentals=0
        ),
    )(*args)


def choose(index, values):
    picked = values[0]
    for i in range(1, len(values)):
        picked = jnp.where(index == i, values[i], picked)
    return picked


def pack_weights(group_ref, q_ref, k_ref, v_ref, router_ref, one_ref, two_ref, wout_ref, docs_ref,
                 *refs):
    *out_refs, keep_ref = refs
    rows, width = q_ref.shape
    experts = router_ref.shape[0]
    cols = width // 4
    eye = iota((rows, rows), 0) == iota((rows, rows), 1)
    router = dot(eye.astype(F32).astype(BF16), router_ref[...], ((1,), (1,)))
    columns = [
        jnp.sum(jnp.where(eye, ref[...].astype(F32), 0.0), axis=1, keepdims=True)
        for ref in (one_ref, two_ref)
    ]
    docs = docs_ref[...].astype(F32)
    length = docs.shape[1]
    doc_cols = -(-length // rows)
    for t in range(doc_cols):
        belongs = iota((rows, length), 1) == iota((rows, length), 0) * doc_cols + t
        columns.append(jnp.sum(jnp.where(belongs, docs, 0.0), axis=1, keepdims=True))
    pad = out_refs[0].shape[1] - 3 * cols - experts - 2 - doc_cols
    small = jnp.concatenate(
        [router] + columns + [jnp.zeros((rows, pad), F32)], axis=1
    ).astype(BF16)
    weights = [ref[...] for ref in (q_ref, k_ref, v_ref)]
    pieces = [
        jnp.concatenate([w[:, j * cols : (j + 1) * cols] for w in weights] + [small], axis=1)
        for j in range(4)
    ]
    for d, out_ref in enumerate(out_refs):
        out_ref[...] = choose(group_ref[0] ^ d, pieces)
    keep_ref[...] = wout_ref[...]


def spread_weights(group_ref, p0_ref, p1_ref, p2_ref, p3_ref, wout_ref, out_ref):
    dests, _, wide = out_ref.shape
    rows, used = p0_ref.shape
    pieces = [ref[...] for ref in (p0_ref, p1_ref, p2_ref, p3_ref)]
    value = jnp.concatenate([choose(group_ref[0] ^ j, pieces) for j in range(4)], axis=0)
    if wide > used:
        value = jnp.concatenate([value, jnp.zeros((4 * rows, wide - used), BF16)], axis=1)
    last = wout_ref[...]
    if wide > last.shape[1]:
        last = jnp.concatenate([last, jnp.zeros((rows, wide - last.shape[1]), BF16)], axis=1)
    value = jnp.concatenate([value, last], axis=0)
    for dest in range(dests):
        out_ref[dest] = value


def prepare(capacity, pad_two, group_ref, table_ref, routes_ref, vector_ref, spread_ref, later_ref,
            gather_ref, send_ref):
    buckets = table_ref.shape[0]
    own_heads, length = vector_ref.shape
    toks = length // 2
    group = group_ref[0]
    spot = iota((1, length), 1)
    offset = jnp.where(spot >= toks, spot - length, spot)
    bucket = bucket_of(offset, buckets)
    for h in range(own_heads):
        vector = jnp.zeros((1, length), F32)
        for b in range(buckets):
            vector = jnp.where(bucket == b, table_ref[b, group * own_heads + h], vector)
        vector_ref[h : h + 1] = vector
    experts = spread_ref.shape[1] // pad_two
    route = routes_ref[...]
    chosen = route == iota((toks, experts), 1)
    lower = (iota((toks, toks), 0) > iota((toks, toks), 1)).astype(BF16)
    counts = dot(lower, chosen.astype(BF16))
    slot = jnp.sum(jnp.where(chosen, counts, 0.0), axis=1, keepdims=True).astype(jnp.int32)
    kept = slot < capacity
    place = jnp.where(kept, route * pad_two + slot, -1)
    later = jnp.where(kept, route * pad_two + capacity + slot, -1)
    across = iota((toks, experts * pad_two), 1)
    first = (place == across).astype(F32)
    second = (later == across).astype(F32)
    spread_ref[...] = first.astype(BF16)
    later_ref[...] = second.astype(BF16)
    send_ref[:, :toks] = jnp.transpose(first).astype(BF16)
    send_ref[:, toks:] = jnp.transpose(second).astype(BF16)
    gather_ref[...] = chosen.astype(F32)


def place_weights(arrived_ref, w_ref, wout_ref):
    sources, total, _ = arrived_ref.shape
    rows = total // 5
    used = w_ref.shape[1]
    width = wout_ref.shape[1]
    block = sources * rows
    for s in range(sources):
        for j in range(4):
            w_ref[j * block + s * rows : j * block + (s + 1) * rows] = arrived_ref[
                s, j * rows : (j + 1) * rows, :used
            ]
        wout_ref[s * rows : (s + 1) * rows] = arrived_ref[s, 4 * rows :, :width]


def gain_rows(experts, cols, w_ref, gains_ref):
    small = w_ref[:, 3 * cols :]
    pick = (iota((8, small.shape[1]), 1) == iota((8, small.shape[1]), 0) + experts).astype(BF16)
    gains_ref[...] = dot(pick, small, ((1,), (1,)))


def attend(scale, head_dim, docs, group_ref, w_ref, wout_ref, gains_ref, own_ref, across_ref,
           vector_ref, qkv_ref, probs_ref, att_ref, keep_ref, send_ref):
    own_heads, length = vector_ref.shape
    cols = own_heads * head_dim
    toks = own_ref.shape[0]
    vectors = vector_ref[...]
    turned = jnp.concatenate([docs[:, toks:], docs[:, :toks]], axis=1)
    across = jnp.broadcast_to(jnp.where(group_ref[0] < 2, docs, turned), (length, length))
    same = across == jnp.transpose(across)
    x = jnp.concatenate([own_ref[...], across_ref[...]], axis=0).astype(F32)
    normed = (x * rms_inverse(x) * gains_ref[0:1]).astype(BF16)
    qkv = dot(normed, w_ref[:, : 3 * cols]).astype(BF16)
    qkv_ref[...] = qkv
    parts = []
    for h in range(own_heads):
        at = h * head_dim
        q = qkv[:, at : at + head_dim]
        k = qkv[:, cols + at : cols + at + head_dim]
        v = qkv[:, 2 * cols + at : 2 * cols + at + head_dim]
        full = jnp.broadcast_to(vectors[h : h + 1], (length, length))
        bias = pltpu.roll(full, 0, 1, stride=1, stride_axis=0)
        scores = jnp.where(same, dot(q, k, ((1,), (1,))) * scale + bias, MASKED)
        top = jnp.max(scores, axis=1, keepdims=True)
        raised = jnp.exp(scores - top)
        probs = raised * (1.0 / jnp.sum(raised, axis=1, keepdims=True))
        probs_ref[h] = probs
        parts.append(dot(probs.astype(BF16), v))
    attended = jnp.concatenate(parts, axis=1).astype(BF16)
    att_ref[...] = attended
    partial = dot(attended, wout_ref[...])
    keep_ref[...] = partial[:toks]
    send_ref[...] = partial[toks:].astype(BF16)


def docs_of_pair(at, length, group_ref, place_ref, arrived_ref):
    sources, total, _ = arrived_ref.shape
    rows = total // 5
    doc_cols = -(-length // rows)
    held = arrived_ref[(place_ref[0] % sources) ^ (sources // 2)]
    blocks = [held[j * rows : (j + 1) * rows, at : at + doc_cols].astype(F32) for j in range(4)]
    block = choose(group_ref[0] ^ 1, blocks)
    docs = jnp.zeros((1, length), F32)
    for t in range(doc_cols):
        belongs = iota((rows, length), 1) == iota((rows, length), 0) * doc_cols + t
        docs = docs + jnp.sum(jnp.where(belongs, block[:, t : t + 1], 0.0), axis=0, keepdims=True)
    return docs


def attend_own(scale, head_dim, group_ref, docs_ref, *refs):
    attend(scale, head_dim, docs_ref[...].astype(F32), group_ref, *refs)


def attend_first(scale, head_dim, experts, group_ref, place_ref, arrived_ref, own_ref, across_ref,
                 vector_ref, w_ref, wout_ref, gains_ref, *outs):
    place_weights(arrived_ref, w_ref, wout_ref)
    cols = wout_ref.shape[0]
    gain_rows(experts, cols, w_ref, gains_ref)
    docs = docs_of_pair(3 * cols + experts + 2, vector_ref.shape[1], group_ref, place_ref, arrived_ref)
    attend(scale, head_dim, docs, group_ref, w_ref, wout_ref, gains_ref, own_ref, across_ref,
           vector_ref, *outs)


def attend_first_placed(scale, head_dim, experts, group_ref, place_ref, arrived_ref, w_ref, wout_ref,
                        own_ref, across_ref, vector_ref, gains_ref, *outs):
    cols = wout_ref.shape[0]
    gain_rows(experts, cols, w_ref, gains_ref)
    docs = docs_of_pair(3 * cols + experts + 2, vector_ref.shape[1], group_ref, place_ref, arrived_ref)
    attend(scale, head_dim, docs, group_ref, w_ref, wout_ref, gains_ref, own_ref, across_ref,
           vector_ref, *outs)


def route_tokens(x_ref, keep_ref, core_ref, came_ref, gains_ref, w_ref, chosen_ref, send_ref,
                 g_ref, middle_ref, gate_ref, out_ref):
    middle = x_ref[...].astype(F32) + (
        (keep_ref[...] + core_ref[...].astype(F32)) + came_ref[...].astype(F32)
    )
    middle_ref[...] = middle
    normed = (middle * rms_inverse(middle) * gains_ref[1:2]).astype(BF16)
    both = jnp.concatenate([normed, g_ref[...]], axis=0)
    out_ref[...] = dot(send_ref[...], both).astype(BF16)
    probs = jax.nn.softmax(dot(normed, w_ref[...]), axis=-1)
    gate_ref[...] = jnp.sum(probs * chosen_ref[...], axis=1, keepdims=True)


def run_expert(capacity, place_ref, own_ref, other_ref, router_ref, inner_ref, outer_ref,
               buf_ref, dslot_ref, g_ref, probs_ref, gate_ref, hidden_ref, dpre_ref, keep_ref,
               send_ref, acc_ref):
    step = pl.program_id(0)
    slots = buf_ref.shape[0] // 2
    experts = router_ref.shape[1]
    pad = own_ref.shape[0] // (slots // capacity)

    @pl.when(step == 0)
    def _():
        shape = (slots, own_ref.shape[0])
        row = iota(shape, 0)
        source = row // capacity
        wanted = source * pad + (row - source * capacity)
        first = (iota(shape, 1) == wanted).astype(BF16)
        second = (iota(shape, 1) == wanted + capacity).astype(BF16)
        mine = (iota((1, experts), 1) == place_ref[0]).astype(F32)
        for side, ref in enumerate((own_ref, other_ref)):
            at = side * slots
            rows = ref[...]
            buffers = dot(first, rows).astype(BF16)
            buf_ref[at : at + slots] = buffers
            g = dot(second, rows)
            probs = jax.nn.softmax(dot(buffers, router_ref[...]), axis=-1)
            gate = jnp.sum(probs * mine, axis=1, keepdims=True)
            dslot_ref[at : at + slots] = (gate * g).astype(BF16)
            if side == 0:
                g_ref[...] = g.astype(BF16)
                probs_ref[...] = probs
                gate_ref[...] = gate
        acc_ref[...] = jnp.zeros_like(acc_ref)

    inner = inner_ref[...]
    outer = outer_ref[...]
    pre = dot(buf_ref[...], inner)
    cdf = 0.5 * (1.0 + lax.erf(pre * (0.5**0.5)))
    hidden = (pre * cdf).astype(BF16)
    hidden_ref[...] = hidden
    slope = cdf + pre * jnp.exp(-0.5 * pre * pre) * 0.3989422804014327
    dpre = (dot(dslot_ref[...], outer, ((1,), (1,))) * slope).astype(BF16)
    dpre_ref[...] = dpre
    acc_ref[0] += dot(hidden, outer)
    acc_ref[1] += dot(dpre, inner, ((1,), (1,)))

    @pl.when(step == pl.num_programs(0) - 1)
    def _():
        keep_ref[...] = acc_ref[:, :slots]
        send_ref[...] = acc_ref[:, slots:].astype(BF16)


def finish_expert(capacity, place_ref, keep_ref, came_ref, buf_ref, g_ref, probs_ref, gate_ref,
                  router_ref, out_ref, grad_ref):
    slots = g_ref.shape[0]
    experts = router_ref.shape[1]
    pad = out_ref.shape[0] // (slots // capacity)
    total = (keep_ref[...] + came_ref[...].astype(F32)).astype(BF16)
    result = total[0]
    mine = (iota((1, experts), 1) == place_ref[0]).astype(F32)
    grad_gate = jnp.sum(g_ref[...].astype(F32) * result.astype(F32), axis=1, keepdims=True)
    grad_logits = (grad_gate * gate_ref[...] * (mine - probs_ref[...])).astype(BF16)
    grad_ref[...] = dot(buf_ref[...], grad_logits, ((0,), (0,))).astype(BF16)
    back = total[1].astype(F32) + dot(grad_logits, router_ref[...], ((1,), (1,)))
    shape = (out_ref.shape[0], 2 * slots)
    row = iota(shape, 0)
    source = row // pad
    inside = row - source * pad
    wanted = jnp.where(
        inside < capacity,
        source * capacity + inside,
        jnp.where(inside < 2 * capacity, slots + source * capacity + inside - capacity, -1),
    )
    expand = (iota(shape, 1) == wanted).astype(BF16)
    both = jnp.concatenate([back.astype(BF16), result], axis=0)
    out_ref[...] = dot(expand, both).astype(BF16)


def norm_two_backward(back_ref, spread_ref, middle_ref, gains_ref, g_ref, dmiddle_ref, da_ref,
                      gain_ref):
    middle = middle_ref[...]
    inverse = rms_inverse(middle)
    unit = middle * inverse
    grad_normed = dot(spread_ref[...], back_ref[...])
    gain_ref[...] = jnp.sum(grad_normed * unit, axis=0, keepdims=True)
    dmiddle = g_ref[...].astype(F32) + norm_backward(grad_normed, unit, inverse, gains_ref[1:2])
    dmiddle_ref[...] = dmiddle
    da_ref[...] = dmiddle.astype(BF16)


def finish_layer(result_ref, spread_ref, middle_ref, gate_ref, out_ref):
    combined = dot(spread_ref[...], result_ref[...])
    out_ref[...] = (middle_ref[...] + gate_ref[...] * combined).astype(BF16)


def attend_backward(scale, head_dim, own_ref, across_ref, wout_ref, att_ref, qkv_ref, probs_ref,
                    gains_ref, w_ref, x_own_ref, x_across_ref):
    own_heads = probs_ref.shape[0]
    cols = own_heads * head_dim
    length = 2 * own_ref.shape[0]
    flip = (iota((length, length), 0) + iota((length, length), 1) == length - 1).astype(BF16)
    da = jnp.concatenate([own_ref[...], across_ref[...]], axis=0)
    grad_att = dot(da, wout_ref[...], ((1,), (1,))).astype(BF16)
    qkv = qkv_ref[...]
    parts = [[], [], []]
    offsets = []
    for h in range(own_heads):
        at = h * head_dim
        q = qkv[:, at : at + head_dim]
        k = qkv[:, cols + at : cols + at + head_dim]
        v = qkv[:, 2 * cols + at : 2 * cols + at + head_dim]
        gh = grad_att[:, at : at + head_dim]
        probs = probs_ref[h]
        grad_probs = dot(gh, v, ((1,), (1,)))
        row_dot = jnp.sum(probs * grad_probs, axis=1, keepdims=True)
        ds = (probs * (grad_probs - row_dot)).astype(BF16)
        turned = pltpu.roll(dot(flip, ds), 1, 1, stride=1, stride_axis=0)
        offsets.append(jnp.sum(turned, axis=0, keepdims=True))
        parts[0].append(dot(ds, k) * scale)
        parts[1].append(dot(ds, q, ((0,), (0,))) * scale)
        parts[2].append(dot(probs.astype(BF16), gh, ((0,), (0,))))
    grad_qkv = jnp.concatenate(parts[0] + parts[1] + parts[2], axis=1).astype(BF16)
    x = jnp.concatenate([x_own_ref[...], x_across_ref[...]], axis=0).astype(F32)
    unit = x * rms_inverse(x)
    normed = (unit * gains_ref[0:1]).astype(BF16)
    weights = dot(normed, grad_qkv, ((0,), (0,)))
    outs = dot(att_ref[...], da, ((0,), (0,)))
    grad_normed = dot(grad_qkv, w_ref[:, : 3 * cols], ((1,), (1,)))
    gain = jnp.sum(grad_normed * unit, axis=0, keepdims=True)
    return weights, outs, grad_normed, gain, offsets


def backward_own(scale, head_dim, *refs):
    gw_ref, gout_ref, keep_ref, send_ref, gain_ref, offsets_ref = refs[10:]
    toks = keep_ref.shape[0]
    weights, outs, grad_normed, gain, offsets = attend_backward(scale, head_dim, *refs[:10])
    gw_ref[...] = weights
    gout_ref[...] = outs
    keep_ref[...] = grad_normed[:toks]
    send_ref[...] = grad_normed[toks:].astype(BF16)
    gain_ref[...] = gain
    for h, value in enumerate(offsets):
        offsets_ref[h : h + 1] = value


def backward_pair(scale, head_dim, buckets, table_cols, *refs):
    gw_ref, gout_ref, gain_ref, offsets_ref, gain_two_ref, router_ref = refs[10:16]
    keep_ref, send_ref, full_ref, out_ref = refs[16:]
    weights, outs, grad_normed, gain, offsets = attend_backward(scale, head_dim, *refs[:10])
    own_heads = offsets_ref.shape[0]
    width, experts = router_ref.shape
    length = offsets_ref.shape[1]
    toks = length // 2
    keep_ref[...] = grad_normed[:toks]
    send_ref[...] = grad_normed[toks:].astype(BF16)
    rows = own_heads * buckets // table_cols
    spot = iota((1, length), 1)
    offset = jnp.where(spot >= toks, spot - length, spot)
    bucket = bucket_of(offset, buckets)
    table = []
    for t in range(table_cols):
        column = jnp.zeros((rows, 1), F32)
        for h in range(own_heads):
            belongs = iota((rows, length), 0) * table_cols + t == bucket * own_heads + h
            value = offsets[h] + offsets_ref[h : h + 1]
            column = column + jnp.sum(jnp.where(belongs, value, 0.0), axis=1, keepdims=True)
        table.append(column)
    table = jnp.concatenate([jnp.concatenate(table, axis=1)] * (width // rows), axis=0)
    narrow = jnp.concatenate(
        [gain_ref[...] + gain, gain_two_ref[...], jnp.zeros((6, width), F32)], axis=0
    )
    narrow = jnp.transpose(narrow)[:, :2]
    weights = weights + gw_ref[...]
    pieces = [weights, router_ref[...].astype(F32), narrow, table]
    spare = full_ref.shape[-1] - sum(p.shape[1] for p in pieces)
    full_ref[...] = jnp.concatenate(pieces + [jnp.zeros((width, spare), F32)], axis=1).astype(BF16)
    out_ref[...] = (outs + gout_ref[...]).astype(BF16)


def backward_pair_message(scale, head_dim, buckets, table_cols, *refs):
    *rest, message_ref, full_ref, out_ref = refs
    backward_pair(scale, head_dim, buckets, table_cols, *rest, full_ref, out_ref)
    dests, total, wide = message_ref.shape
    rows = total // 5
    used = full_ref.shape[1]
    block = dests * rows
    for s in range(dests):
        for j in range(4):
            at = j * block + s * rows
            message_ref[s, j * rows : (j + 1) * rows, :used] = full_ref[at : at + rows]
            if wide > used:
                message_ref[s, j * rows : (j + 1) * rows, used:] = jnp.zeros(
                    (rows, wide - used), BF16
                )
        width = out_ref.shape[1]
        message_ref[s, 4 * rows :, :width] = out_ref[s * rows : (s + 1) * rows]
        if wide > width:
            message_ref[s, 4 * rows :, width:] = jnp.zeros((rows, wide - width), BF16)


def sum_arrived(group_ref, arrived_ref, out_ref, own_ref, *send_refs):
    rows, used = own_ref.shape
    total = arrived_ref[0].astype(F32)
    for s in range(1, arrived_ref.shape[0]):
        total = total + arrived_ref[s].astype(F32)
    out_ref[...] = total[4 * rows :, : out_ref.shape[1]]
    pieces = [total[j * rows : (j + 1) * rows, :used] for j in range(4)]
    own_ref[...] = choose(group_ref[0], pieces)
    for d, ref in enumerate(send_refs):
        ref[...] = choose(group_ref[0] ^ (d + 1), pieces).astype(BF16)


def finish_weights(own_heads, buckets, table_cols, group_ref, p0_ref, p1_ref, p2_ref, p3_ref,
                   q_ref, k_ref, v_ref, router_ref, one_ref, two_ref, table_ref):
    rows, width = q_ref.shape
    experts = router_ref.shape[0]
    cols = width // 4
    pieces = [ref[...].astype(F32) for ref in (p0_ref, p1_ref, p2_ref, p3_ref)]
    ordered = [choose(group_ref[0] ^ j, pieces) for j in range(4)]
    for n, ref in enumerate((q_ref, k_ref, v_ref)):
        ref[...] = jnp.concatenate([p[:, n * cols : (n + 1) * cols] for p in ordered], axis=1)
    at = 3 * cols
    small = sum(p[:, at : at + experts + 2] for p in pieces)
    square = -(-max(rows, experts) // 128) * 128
    padded = small[:, :experts]
    if square > experts:
        padded = jnp.concatenate([padded, jnp.zeros((rows, square - experts), F32)], axis=1)
    padded = jnp.concatenate([padded, jnp.zeros((square - rows, square), F32)], axis=0)
    router_ref[...] = jnp.transpose(padded)[:experts, :rows]
    eye = iota((rows, rows), 0) == iota((rows, rows), 1)
    for i, ref in enumerate((one_ref, two_ref)):
        column = small[:, experts + i : experts + i + 1]
        ref[...] = jnp.sum(jnp.where(eye, column, 0.0), axis=0, keepdims=True)
    at += experts + 2
    lines = []
    lane = iota((rows, 128), 1)
    for p in ordered:
        for h in range(own_heads):
            line = jnp.zeros((1, 128), F32)
            for t in range(table_cols):
                belongs = iota((rows, 128), 0) * table_cols + t == lane * own_heads + h
                value = jnp.where(belongs & (lane < buckets), p[:, at + t : at + t + 1], 0.0)
                line = line + jnp.sum(value, axis=0, keepdims=True)
            lines.append(line)
    table_ref[...] = jnp.concatenate(lines, axis=0)[:, :buckets]


def local(
    tokens,
    gain_one,
    w_query,
    w_key,
    w_value,
    w_out,
    bias_table,
    gain_two,
    w_router,
    w_inner,
    w_outer,
    segment_ids,
    routes,
    out_grad,
):
    toks = tokens.shape[1]
    width = tokens.shape[2]
    heads = bias_table.shape[1]
    buckets = bias_table.shape[0]
    head_dim = width // heads
    own_heads = heads // 4
    cols = own_heads * head_dim
    length = 2 * toks
    scale = head_dim ** (-0.5)
    sources = lax.axis_size("expert")
    experts = sources
    capacity = (5 * toks + 4 * experts - 1) // (4 * experts)
    slots = experts * capacity
    pad_two = -(-2 * capacity // 8) * 8
    rows = w_query.shape[0]
    core = lax.axis_index("dp")
    place = lax.axis_index("expert")
    half = sources // 2
    member = place // half
    first_core = core == 0
    place_at = place.reshape(1).astype(jnp.int32)
    group_at = (2 * core + member).reshape(1).astype(jnp.int32)
    table_cols = max(1, own_heads * buckets // rows)
    extra = max(table_cols, -(-length // rows))
    used = -(-(3 * cols + experts + 2 + extra) // 128) * 128
    wide = max(used, width)
    aligned = rows % 8 == 0

    def across_group(pieces):
        return [
            lax.ppermute(
                piece,
                ("dp", "expert"),
                [
                    (c * sources + e, (c ^ (d >> 1)) * sources + (e ^ (half * (d & 1))))
                    for c in range(2)
                    for e in range(sources)
                ],
            )
            for d, piece in enumerate(pieces, 1)
        ]

    own_tokens = tokens.reshape(toks, width)
    pair_tokens = swap_pair(own_tokens)

    own_piece, *pieces, out_rows = kernel_call(
        pack_weights, [((rows, used), BF16)] * 4 + [((rows, width), BF16)],
        group_at, w_query, w_key, w_value, w_router.T, gain_one.reshape(1, rows),
        gain_two.reshape(1, rows), w_out, segment_ids, scalars=1, late=range(1, 9),
        limit=60 * 1024 * 1024,
    )
    pieces = across_group(pieces)
    pair_tokens, own_piece, *pieces = lax.optimization_barrier((pair_tokens, own_piece, *pieces))
    (message,) = kernel_call(
        spread_weights, [((half, 5 * rows, wide), BF16)],
        group_at, own_piece, *pieces, out_rows, scalars=1,
    )
    arrived = exchange_half(message)

    own_across = swap_core(own_tokens)
    pair_across = swap_core(pair_tokens)
    vectors, spread, later, chosen, send = kernel_call(
        functools.partial(prepare, capacity, pad_two),
        [
            ((own_heads, length), F32),
            ((toks, experts * pad_two), BF16),
            ((toks, experts * pad_two), BF16),
            ((toks, experts), F32),
            ((experts * pad_two, 2 * toks), BF16),
        ],
        group_at, bias_table, routes.reshape(toks, 1), scalars=2,
    )
    g_low = out_grad.reshape(toks, width)

    row_outs = [
        ((length, 3 * cols), BF16),
        ((own_heads, length, length), F32),
        ((length, cols), BF16),
        ((toks, width), F32),
        ((toks, width), BF16),
    ]
    placed = [((width, used), BF16), ((cols, width), BF16)]
    if aligned:
        weights, out_w, gains, *pair_kept = kernel_call(
            functools.partial(attend_first, scale, head_dim, experts),
            placed + [((8, width), F32)] + row_outs,
            group_at, place_at, arrived, pair_tokens, pair_across, vectors, scalars=2,
        )
    else:
        weights = arrived[:, : 4 * rows, :used].reshape(half, 2, 2, rows, used)
        weights = weights.transpose(1, 2, 0, 3, 4).reshape(width, used)
        out_w = arrived[:, 4 * rows :, :width].reshape(cols, width)
        gains, *pair_kept = kernel_call(
            functools.partial(attend_first_placed, scale, head_dim, experts),
            [((8, width), F32)] + row_outs,
            group_at, place_at, arrived, weights, out_w, pair_tokens, pair_across, vectors, scalars=2,
        )
    pair_qkv, pair_probs, pair_att, keep, away = pair_kept
    pair_sum = (keep + swap_core(away).astype(F32)).astype(BF16)
    pair_sum = swap_pair(pair_sum)
    own_qkv, own_probs, own_att, keep, away = kernel_call(
        functools.partial(attend_own, scale, head_dim), row_outs,
        group_at, segment_ids, weights, out_w, gains, own_tokens, own_across, vectors, scalars=1,
    )
    router_w = weights[:, 3 * cols : 3 * cols + experts]
    middle, gate, outgoing = kernel_call(
        route_tokens,
        [((toks, width), F32), ((toks, 1), F32), ((experts * pad_two, width), BF16)],
        own_tokens, keep, swap_core(away), pair_sum, gains, router_w, chosen, send, g_low,
    )
    incoming = exchange(outgoing.reshape(experts, pad_two, width)).reshape(-1, width)

    inner, outer = w_inner[0], w_outer[0]
    units = inner.shape[1]
    chunk = units // 3
    fixed = lambda shape: pl.BlockSpec(shape, lambda i: (0,) * len(shape))
    outs = [
        ((2 * slots, width), BF16, None),
        ((2 * slots, width), BF16, None),
        ((slots, width), BF16, None),
        ((slots, experts), F32, None),
        ((slots, 1), F32, None),
        ((2 * slots, units), BF16, pl.BlockSpec((2 * slots, chunk), lambda i: (0, i))),
        ((2 * slots, units), BF16, pl.BlockSpec((2 * slots, chunk), lambda i: (0, i))),
        ((2, slots, width), F32, None),
        ((2, slots, width), BF16, None),
    ]
    buffers, dslot, slot_g, slot_probs, slot_gate, hidden, dpre, keep, away = pl.pallas_call(
        functools.partial(run_expert, capacity),
        grid=(units // chunk,),
        out_shape=[jax.ShapeDtypeStruct(shape, dtype) for shape, dtype, _ in outs],
        in_specs=[
            pl.BlockSpec(memory_space=pltpu.SMEM),
            fixed((experts * pad_two, width)),
            fixed((experts * pad_two, width)),
            fixed((width, experts)),
            pl.BlockSpec((width, chunk), lambda i: (0, i)),
            pl.BlockSpec((chunk, width), lambda i: (i, 0)),
        ],
        out_specs=[spec or fixed(shape) for shape, _, spec in outs],
        scratch_shapes=[pltpu.VMEM((2, 2 * slots, width), F32)],
        compiler_params=pltpu.CompilerParams(vmem_limit_bytes=VMEM_BYTES),
    )(place_at, incoming, swap_core(incoming), router_w, inner, outer)
    grad_outer = dot(hidden, dslot, ((0,), (0,)))
    grad_inner = dot(buffers, dpre, ((0,), (0,)))
    back, grad_router = kernel_call(
        functools.partial(finish_expert, capacity),
        [((sources * pad_two, width), BF16), ((width, experts), BF16)],
        place_at, keep, swap_core(away), buffers[:slots], slot_g, slot_probs, slot_gate, router_w,
        scalars=1,
    )
    back = exchange(back.reshape(sources, pad_two, width)).reshape(-1, width)

    grad_middle, grad_attn, grad_gain_two = kernel_call(
        norm_two_backward,
        [((toks, width), F32), ((toks, width), BF16), ((1, width), F32)],
        back, spread, middle, gains, g_low,
    )
    pair_grad = swap_pair(grad_attn)
    shared = (gains, weights)
    grad_w, grad_out, grad_normed, away, gain_part, offsets = kernel_call(
        functools.partial(backward_own, scale, head_dim),
        [
            ((width, 3 * cols), F32),
            ((cols, width), F32),
            ((toks, width), F32),
            ((toks, width), BF16),
            ((1, width), F32),
            ((own_heads, length), F32),
        ],
        grad_attn, swap_core(grad_attn), out_w, own_att, own_qkv, own_probs, *shared,
        own_tokens, own_across,
    )
    grad_normed = grad_normed + swap_core(away).astype(F32)
    last = (
        pair_grad, swap_core(pair_grad), out_w, pair_att, pair_qkv, pair_probs, *shared,
        pair_tokens, pair_across, grad_w, grad_out, gain_part, offsets, grad_gain_two, grad_router,
    )
    outs = [((toks, width), F32), ((toks, width), BF16)]
    flat = [((width, used), BF16), ((cols, width), BF16)]
    options = (scale, head_dim, buckets, table_cols)
    if aligned:
        keep, away, message, _, _ = kernel_call(
            functools.partial(backward_pair_message, *options),
            [*outs, ((half, 5 * rows, wide), BF16), *flat], *last,
        )
    else:
        keep, away, full, grad_out = kernel_call(
            functools.partial(backward_pair, *options), outs + flat, *last
        )
        full = full.reshape(2, 2, half, rows, used).transpose(2, 0, 1, 3, 4)
        full = full.reshape(half, 4 * rows, used)
        grad_out = grad_out.reshape(half, rows, width)
        message = jnp.concatenate(
            [
                jnp.pad(full, ((0, 0), (0, 0), (0, wide - used))),
                jnp.pad(grad_out, ((0, 0), (0, 0), (0, wide - width))),
            ],
            axis=1,
        )
    message, away, keep = lax.optimization_barrier((message, away, keep))
    arrived = exchange_half(message)
    came = swap_pair((keep + swap_core(away).astype(F32)).astype(BF16)).astype(F32)
    (final,) = kernel_call(finish_layer, [((toks, width), BF16)], back, later, middle, gate
    )

    out_grad_w, own_piece, *pieces = kernel_call(
        sum_arrived, [((rows, width), F32), ((rows, used), F32)] + [((rows, used), BF16)] * 3,
        group_at, arrived, scalars=1,
    )
    pieces = across_group(pieces)
    query_grad, key_grad, value_grad, router_grad, one_grad, two_grad, table_grad = kernel_call(
        functools.partial(finish_weights, own_heads, buckets, table_cols),
        [((rows, width), F32)] * 3
        + [((experts, rows), F32), ((1, rows), F32), ((1, rows), F32), ((heads, buckets), F32)],
        group_at, own_piece, *pieces, scalars=1,
    )

    x = own_tokens.astype(F32)
    inverse_one = rms_inverse(x)
    grad_input = grad_middle + norm_backward(
        grad_normed + came, x * inverse_one, inverse_one, gains[0:1]
    )
    return (
        final.reshape(tokens.shape),
        grad_input.astype(BF16).reshape(tokens.shape),
        one_grad.reshape(rows),
        query_grad,
        key_grad,
        value_grad,
        out_grad_w,
        table_grad.T,
        two_grad.reshape(rows),
        router_grad.T,
        grad_inner[None],
        grad_outer[None],
    )


def solution(mesh):
    both = ("dp", "expert")
    return jax.shard_map(
        local,
        mesh=mesh,
        in_specs=(
            P("expert", "dp", None),
            P(both),
            P(both, None),
            P(both, None),
            P(both, None),
            P(both, None),
            P(),
            P(both),
            P(both, None),
            P("expert", None, "dp"),
            P("expert", "dp", None),
            P("expert", None),
            P("expert", "dp", None),
            P("expert", "dp", None),
        ),
        out_specs=(
            P("expert", "dp", None),
            P("expert", "dp", None),
            P(both),
            P(both, None),
            P(both, None),
            P(both, None),
            P(both, None),
            P(),
            P(both),
            P(both, None),
            P("expert", None, "dp"),
            P("expert", "dp", None),
        ),
        check_vma=False,
    )
```

```python
import functools

import jax
import jax.numpy as jnp
from jax import lax
from jax.experimental import pallas as pl
from jax.experimental.pallas import tpu as pltpu
from jax.sharding import PartitionSpec as P

EPSILON = 1e-06
MASKED = -1000000000.0
BUCKET_EDGES = (1, 2, 3, 4, 5, 6, 7, 8, 12, 16, 23, 32, 46, 64, 91)
F32 = jnp.float32
BF16 = jnp.bfloat16
VMEM_BYTES = 24 * 1024 * 1024


def dot(left, right, dims=((1,), (0,))):
    return lax.dot_general(left, right, (dims, ((), ())), preferred_element_type=F32)


def rms_inverse(values):
    return lax.rsqrt(jnp.mean(values * values, axis=-1, keepdims=True) + EPSILON)


def norm_backward(grad_normed, unit_values, inverse, gain_values):
    grad_unit = grad_normed * gain_values
    projected = jnp.mean(grad_unit * unit_values, axis=-1, keepdims=True)
    return inverse * (grad_unit - unit_values * projected)


def swap_core(value):
    return lax.ppermute(value, "dp", [(0, 1), (1, 0)])


def swap_pair(value):
    n = lax.axis_size("expert")
    other = 3 * n // 4
    return lax.ppermute(value, "expert", [(i, i ^ other) for i in range(n)])


def exchange(value):
    return lax.all_to_all(value, "expert", split_axis=0, concat_axis=0, tiled=True)


def exchange_half(value):
    half = lax.axis_size("expert") // 2
    groups = [[q * half + s for s in range(half)] for q in range(2)]
    return lax.all_to_all(
        value, "expert", split_axis=0, concat_axis=0, tiled=True, axis_index_groups=groups
    )


def bucket_of(offset, total):
    distance = jnp.abs(offset)
    bucket = jnp.zeros(offset.shape, jnp.int32)
    for border in BUCKET_EDGES:
        bucket = bucket + (distance >= border).astype(jnp.int32)
    return bucket + total // 2 * (offset > 0).astype(jnp.int32)


def iota(shape, axis):
    return lax.broadcasted_iota(jnp.int32, shape, axis)


class LateRef:
    def __init__(self, source, target, sem):
        self.copy = pltpu.make_async_copy(source, target, sem)
        self.target = target
        self.shape = target.shape
        self.pending = True
        self.copy.start()

    def wait(self):
        if self.pending:
            self.copy.wait()
            self.pending = False

    def __getitem__(self, index):
        self.wait()
        return self.target[index]


def kernel_call(body, outs, *args, scalars=0, late=(), limit=VMEM_BYTES):
    count = len(args)
    late = sorted(late)

    def run(*refs):
        ins = list(refs[:count])
        out_refs = refs[count : count + len(outs)]
        scratch = refs[count + len(outs) :]
        for n, i in enumerate(late):
            ins[i] = LateRef(ins[i], scratch[n], scratch[-1].at[n])
        body(*ins, *out_refs)
        for i in late:
            ins[i].wait()

    spaces = [pltpu.SMEM if i < scalars else pltpu.VMEM for i in range(count)]
    for i in late:
        spaces[i] = pltpu.HBM
    scratch = [pltpu.VMEM(args[i].shape, args[i].dtype) for i in late]
    if late:
        scratch.append(pltpu.SemaphoreType.DMA((len(late),)))
    return pl.pallas_call(
        run,
        out_shape=[jax.ShapeDtypeStruct(shape, dtype) for shape, dtype in outs],
        in_specs=[pl.BlockSpec(memory_space=space) for space in spaces],
        out_specs=[pl.BlockSpec(memory_space=pltpu.VMEM)] * len(outs),
        scratch_shapes=scratch,
        compiler_params=pltpu.CompilerParams(vmem_limit_bytes=limit),
        cost_estimate=pl.CostEstimate(
            flops=1_000_000, bytes_accessed=1_000_000, transcendentals=0
        ),
    )(*args)


def choose(index, values):
    picked = values[0]
    for i in range(1, len(values)):
        picked = jnp.where(index == i, values[i], picked)
    return picked


def pack_weights(group_ref, q_ref, k_ref, v_ref, router_ref, one_ref, two_ref, wout_ref, docs_ref,
                 *refs):
    *out_refs, keep_ref = refs
    rows, width = q_ref.shape
    experts = router_ref.shape[0]
    cols = width // 4
    eye = iota((rows, rows), 0) == iota((rows, rows), 1)
    router = dot(eye.astype(F32).astype(BF16), router_ref[...], ((1,), (1,)))
    columns = [
        jnp.sum(jnp.where(eye, ref[...].astype(F32), 0.0), axis=1, keepdims=True)
        for ref in (one_ref, two_ref)
    ]
    docs = docs_ref[...].astype(F32)
    length = docs.shape[1]
    doc_cols = -(-length // rows)
    for t in range(doc_cols):
        belongs = iota((rows, length), 1) == iota((rows, length), 0) * doc_cols + t
        columns.append(jnp.sum(jnp.where(belongs, docs, 0.0), axis=1, keepdims=True))
    pad = out_refs[0].shape[1] - 3 * cols - experts - 2 - doc_cols
    small = jnp.concatenate(
        [router] + columns + [jnp.zeros((rows, pad), F32)], axis=1
    ).astype(BF16)
    weights = [ref[...] for ref in (q_ref, k_ref, v_ref)]
    pieces = [
        jnp.concatenate([w[:, j * cols : (j + 1) * cols] for w in weights] + [small], axis=1)
        for j in range(4)
    ]
    for d, out_ref in enumerate(out_refs):
        out_ref[...] = choose(group_ref[0] ^ d, pieces)
    keep_ref[...] = wout_ref[...]


def put_rows(ref, dest, value):
    rows, width = value.shape
    wide = ref.shape[2]
    if wide >= width:
        ref[dest, 4 * rows :, :width] = value
        if wide > width:
            ref[dest, 4 * rows :, width:] = jnp.zeros((rows, wide - width), BF16)
        return
    over = width - wide
    blocks = rows // 8
    ref[dest, 4 * rows : 5 * rows] = value[:, :wide]
    for b in range(blocks):
        ref[dest, 5 * rows :, b * over : (b + 1) * over] = value[b * 8 : (b + 1) * 8, wide:]
    ref[dest, 5 * rows :, blocks * over :] = jnp.zeros((8, wide - blocks * over), BF16)


def take_rows(held, rows, width):
    wide = held.shape[1]
    if wide >= width:
        return held[4 * rows :, :width]
    over = width - wide
    tail = [held[5 * rows :, b * over : (b + 1) * over] for b in range(rows // 8)]
    return jnp.concatenate([held[4 * rows : 5 * rows], jnp.concatenate(tail, axis=0)], axis=1)


def spread_weights(group_ref, p0_ref, p1_ref, p2_ref, p3_ref, wout_ref, out_ref):
    dests, _, wide = out_ref.shape
    rows, used = p0_ref.shape
    pieces = [ref[...] for ref in (p0_ref, p1_ref, p2_ref, p3_ref)]
    value = jnp.concatenate([choose(group_ref[0] ^ j, pieces) for j in range(4)], axis=0)
    if wide > used:
        value = jnp.concatenate([value, jnp.zeros((4 * rows, wide - used), BF16)], axis=1)
    last = wout_ref[...]
    for dest in range(dests):
        out_ref[dest, : 4 * rows] = value
        put_rows(out_ref, dest, last)


def prepare(capacity, pad, group_ref, table_ref, routes_ref, vector_ref, spread_ref, later_ref,
            gather_ref, send_ref):
    buckets = table_ref.shape[0]
    own_heads, length = vector_ref.shape
    toks = length // 2
    group = group_ref[0]
    spot = iota((1, length), 1)
    offset = jnp.where(spot >= toks, spot - length, spot)
    bucket = bucket_of(offset, buckets)
    for h in range(own_heads):
        vector = jnp.zeros((1, length), F32)
        for b in range(buckets):
            vector = jnp.where(bucket == b, table_ref[b, group * own_heads + h], vector)
        vector_ref[h : h + 1] = vector
    experts = gather_ref.shape[1]
    route = routes_ref[...]
    chosen = route == iota((toks, experts), 1)
    gather_ref[...] = chosen.astype(F32)
    lower = (iota((toks, toks), 0) > iota((toks, toks), 1)).astype(BF16)
    counts = dot(lower, chosen.astype(BF16))
    slot = jnp.sum(jnp.where(chosen, counts, 0.0), axis=1, keepdims=True).astype(jnp.int32)
    across = iota((toks, experts * pad), 1)
    for i in range(4):
        place = jnp.where(slot < capacity, route * pad + i * capacity + slot, -1)
        spread = (place == across).astype(F32)
        target = (spread_ref, later_ref)[i % 2]
        target[i // 2] = spread.astype(BF16)
        send_ref[:, i * toks : (i + 1) * toks] = jnp.transpose(spread).astype(BF16)


def place_weights(arrived_ref, w_ref, wout_ref):
    sources = arrived_ref.shape[0]
    rows = wout_ref.shape[0] // sources
    used = w_ref.shape[1]
    width = wout_ref.shape[1]
    block = sources * rows
    for s in range(sources):
        for j in range(4):
            w_ref[j * block + s * rows : j * block + (s + 1) * rows] = arrived_ref[
                s, j * rows : (j + 1) * rows, :used
            ]
        wout_ref[s * rows : (s + 1) * rows] = take_rows(arrived_ref[s], rows, width)


def gain_rows(experts, cols, w_ref, gains_ref):
    small = w_ref[:, 3 * cols :]
    pick = (iota((8, small.shape[1]), 1) == iota((8, small.shape[1]), 0) + experts).astype(BF16)
    gains_ref[...] = dot(pick, small, ((1,), (1,)))


def attend(scale, head_dim, docs, group_ref, w_ref, wout_ref, gains_ref, own_ref, across_ref,
           vector_ref, qkv_ref, probs_ref, att_ref, keep_ref, send_ref):
    own_heads, length = vector_ref.shape
    cols = own_heads * head_dim
    toks = own_ref.shape[0]
    vectors = vector_ref[...]
    turned = jnp.concatenate([docs[:, toks:], docs[:, :toks]], axis=1)
    across = jnp.broadcast_to(jnp.where(group_ref[0] < 2, docs, turned), (length, length))
    same = across == jnp.transpose(across)
    x = jnp.concatenate([own_ref[...], across_ref[...]], axis=0).astype(F32)
    normed = (x * rms_inverse(x) * gains_ref[0:1]).astype(BF16)
    qkv = dot(normed, w_ref[:, : 3 * cols]).astype(BF16)
    qkv_ref[...] = qkv
    parts = []
    for h in range(own_heads):
        at = h * head_dim
        q = qkv[:, at : at + head_dim]
        k = qkv[:, cols + at : cols + at + head_dim]
        v = qkv[:, 2 * cols + at : 2 * cols + at + head_dim]
        full = jnp.broadcast_to(vectors[h : h + 1], (length, length))
        bias = pltpu.roll(full, 0, 1, stride=1, stride_axis=0)
        scores = jnp.where(same, dot(q, k, ((1,), (1,))) * scale + bias, MASKED)
        top = jnp.max(scores, axis=1, keepdims=True)
        raised = jnp.exp(scores - top)
        probs = raised * (1.0 / jnp.sum(raised, axis=1, keepdims=True))
        probs_ref[h] = probs
        parts.append(dot(probs.astype(BF16), v))
    attended = jnp.concatenate(parts, axis=1).astype(BF16)
    att_ref[...] = attended
    partial = dot(attended, wout_ref[...])
    keep_ref[...] = partial[:toks]
    send_ref[...] = partial[toks:].astype(BF16)


def docs_of_pair(at, length, rows, group_ref, place_ref, arrived_ref):
    sources = arrived_ref.shape[0]
    doc_cols = -(-length // rows)
    held = arrived_ref[(place_ref[0] % sources) ^ (sources // 2)]
    blocks = [held[j * rows : (j + 1) * rows, at : at + doc_cols].astype(F32) for j in range(4)]
    block = choose(group_ref[0] ^ 1, blocks)
    docs = jnp.zeros((1, length), F32)
    for t in range(doc_cols):
        belongs = iota((rows, length), 1) == iota((rows, length), 0) * doc_cols + t
        docs = docs + jnp.sum(jnp.where(belongs, block[:, t : t + 1], 0.0), axis=0, keepdims=True)
    return docs


def attend_own(scale, head_dim, group_ref, docs_ref, *refs):
    attend(scale, head_dim, docs_ref[...].astype(F32), group_ref, *refs)


def attend_first(scale, head_dim, experts, group_ref, place_ref, arrived_ref, own_ref, across_ref,
                 vector_ref, w_ref, wout_ref, gains_ref, *outs):
    place_weights(arrived_ref, w_ref, wout_ref)
    cols = wout_ref.shape[0]
    gain_rows(experts, cols, w_ref, gains_ref)
    docs = docs_of_pair(
        3 * cols + experts + 2, vector_ref.shape[1], cols // arrived_ref.shape[0], group_ref, place_ref,
        arrived_ref,
    )
    attend(scale, head_dim, docs, group_ref, w_ref, wout_ref, gains_ref, own_ref, across_ref,
           vector_ref, *outs)


def attend_first_placed(scale, head_dim, experts, group_ref, place_ref, arrived_ref, w_ref, wout_ref,
                        own_ref, across_ref, vector_ref, gains_ref, *outs):
    cols = wout_ref.shape[0]
    gain_rows(experts, cols, w_ref, gains_ref)
    docs = docs_of_pair(
        3 * cols + experts + 2, vector_ref.shape[1], cols // arrived_ref.shape[0], group_ref, place_ref,
        arrived_ref,
    )
    attend(scale, head_dim, docs, group_ref, w_ref, wout_ref, gains_ref, own_ref, across_ref,
           vector_ref, *outs)


def route_tokens(x_ref, keep_ref, core_ref, came_ref, gains_ref, w_ref, chosen_ref, send_ref,
                 g_ref, middle_ref, gate_ref, out_ref):
    middle = x_ref[...].astype(F32) + (
        (keep_ref[...] + core_ref[...].astype(F32)) + came_ref[...].astype(F32)
    )
    middle_ref[...] = middle
    normed = (middle * rms_inverse(middle) * gains_ref[1:2]).astype(BF16)
    g = g_ref[...]
    half = g.shape[1] // 2
    both = jnp.concatenate([normed[:, :half], g[:, :half], normed[:, half:], g[:, half:]], axis=0)
    out_ref[...] = dot(send_ref[...], both).astype(BF16)
    probs = jax.nn.softmax(dot(normed, w_ref[...]), axis=-1)
    gate_ref[...] = jnp.sum(probs * chosen_ref[...], axis=1, keepdims=True)


def run_expert(capacity, place_ref, own_ref, other_ref, router_ref, inner_ref, outer_ref,
               buf_ref, dslot_ref, g_ref, probs_ref, gate_ref, hidden_ref, dpre_ref, keep_ref,
               send_ref, acc_ref):
    step = pl.program_id(0)
    slots = buf_ref.shape[0] // 2
    experts = router_ref.shape[1]
    pad = own_ref.shape[0] // (slots // capacity)

    @pl.when(step == 0)
    def _():
        shape = (slots, own_ref.shape[0])
        row = iota(shape, 0)
        source = row // capacity
        wanted = source * pad + (row - source * capacity)
        select = [(iota(shape, 1) == wanted + i * capacity).astype(BF16) for i in range(4)]
        mine = (iota((1, experts), 1) == place_ref[0]).astype(F32)
        for side, ref in enumerate((own_ref, other_ref)):
            at = side * slots
            rows = ref[...]
            buffers, g = [
                jnp.concatenate([dot(select[i], rows), dot(select[i + 2], rows)], axis=1)
                for i in range(2)
            ]
            buffers = buffers.astype(BF16)
            buf_ref[at : at + slots] = buffers
            probs = jax.nn.softmax(dot(buffers, router_ref[...]), axis=-1)
            gate = jnp.sum(probs * mine, axis=1, keepdims=True)
            dslot_ref[at : at + slots] = (gate * g).astype(BF16)
            if side == 0:
                g_ref[...] = g.astype(BF16)
                probs_ref[...] = probs
                gate_ref[...] = gate
        acc_ref[...] = jnp.zeros_like(acc_ref)

    inner = inner_ref[...]
    outer = outer_ref[...]
    pre = dot(buf_ref[...], inner)
    cdf = 0.5 * (1.0 + lax.erf(pre * (0.5**0.5)))
    hidden = (pre * cdf).astype(BF16)
    hidden_ref[...] = hidden
    slope = cdf + pre * jnp.exp(-0.5 * pre * pre) * 0.3989422804014327
    dpre = (dot(dslot_ref[...], outer, ((1,), (1,))) * slope).astype(BF16)
    dpre_ref[...] = dpre
    acc_ref[0] += dot(hidden, outer)
    acc_ref[1] += dot(dpre, inner, ((1,), (1,)))

    @pl.when(step == pl.num_programs(0) - 1)
    def _():
        keep_ref[...] = acc_ref[:, :slots]
        send_ref[...] = acc_ref[:, slots:].astype(BF16)


def finish_expert(capacity, place_ref, keep_ref, came_ref, buf_ref, g_ref, probs_ref, gate_ref,
                  router_ref, out_ref, grad_ref):
    slots = g_ref.shape[0]
    experts = router_ref.shape[1]
    pad = out_ref.shape[0] // (slots // capacity)
    total = (keep_ref[...] + came_ref[...].astype(F32)).astype(BF16)
    result = total[0]
    mine = (iota((1, experts), 1) == place_ref[0]).astype(F32)
    grad_gate = jnp.sum(g_ref[...].astype(F32) * result.astype(F32), axis=1, keepdims=True)
    grad_logits = (grad_gate * gate_ref[...] * (mine - probs_ref[...])).astype(BF16)
    grad_ref[...] = dot(buf_ref[...], grad_logits, ((0,), (0,))).astype(BF16)
    back = total[1].astype(F32) + dot(grad_logits, router_ref[...], ((1,), (1,)))
    shape = (out_ref.shape[0], 4 * slots)
    row = iota(shape, 0)
    source = row // pad
    inside = row - source * pad
    part = inside // capacity
    wanted = jnp.where(part < 4, part * slots + source * capacity + inside - part * capacity, -1)
    expand = (iota(shape, 1) == wanted).astype(BF16)
    back = back.astype(BF16)
    half = back.shape[1] // 2
    both = jnp.concatenate([back[:, :half], result[:, :half], back[:, half:], result[:, half:]], axis=0)
    out_ref[...] = dot(expand, both).astype(BF16)


def norm_two_backward(back_ref, spread_ref, middle_ref, gains_ref, g_ref, dmiddle_ref, da_ref,
                      gain_ref):
    middle = middle_ref[...]
    inverse = rms_inverse(middle)
    unit = middle * inverse
    rows = back_ref[...]
    grad_normed = jnp.concatenate([dot(spread_ref[i], rows) for i in range(2)], axis=1)
    gain_ref[...] = jnp.sum(grad_normed * unit, axis=0, keepdims=True)
    dmiddle = g_ref[...].astype(F32) + norm_backward(grad_normed, unit, inverse, gains_ref[1:2])
    dmiddle_ref[...] = dmiddle
    da_ref[...] = dmiddle.astype(BF16)


def finish_layer(result_ref, spread_ref, middle_ref, gate_ref, out_ref):
    rows = result_ref[...]
    combined = jnp.concatenate([dot(spread_ref[i], rows) for i in range(2)], axis=1)
    out_ref[...] = (middle_ref[...] + gate_ref[...] * combined).astype(BF16)


def attend_backward(scale, head_dim, own_ref, across_ref, wout_ref, qkv_ref, probs_ref, gains_ref,
                    w_ref, x_own_ref, x_across_ref, keep_ref, send_ref, grad_ref, gain_ref,
                    offsets_ref):
    own_heads = probs_ref.shape[0]
    cols = own_heads * head_dim
    toks = own_ref.shape[0]
    length = 2 * toks
    flip = (iota((length, length), 0) + iota((length, length), 1) == length - 1).astype(BF16)
    da = jnp.concatenate([own_ref[...], across_ref[...]], axis=0)
    grad_att = dot(da, wout_ref[...], ((1,), (1,))).astype(BF16)
    qkv = qkv_ref[...]
    parts = [[], [], []]
    for h in range(own_heads):
        at = h * head_dim
        q = qkv[:, at : at + head_dim]
        k = qkv[:, cols + at : cols + at + head_dim]
        v = qkv[:, 2 * cols + at : 2 * cols + at + head_dim]
        gh = grad_att[:, at : at + head_dim]
        probs = probs_ref[h]
        grad_probs = dot(gh, v, ((1,), (1,)))
        row_dot = jnp.sum(probs * grad_probs, axis=1, keepdims=True)
        ds = (probs * (grad_probs - row_dot)).astype(BF16)
        turned = pltpu.roll(dot(flip, ds), 1, 1, stride=1, stride_axis=0)
        offsets_ref[h : h + 1] = jnp.sum(turned, axis=0, keepdims=True)
        parts[0].append(dot(ds, k) * scale)
        parts[1].append(dot(ds, q, ((0,), (0,))) * scale)
        parts[2].append(dot(probs.astype(BF16), gh, ((0,), (0,))))
    grad_qkv = jnp.concatenate(parts[0] + parts[1] + parts[2], axis=1).astype(BF16)
    grad_ref[...] = grad_qkv
    grad_normed = dot(grad_qkv, w_ref[:, : 3 * cols], ((1,), (1,)))
    keep_ref[...] = grad_normed[:toks]
    send_ref[...] = grad_normed[toks:].astype(BF16)
    x = jnp.concatenate([x_own_ref[...], x_across_ref[...]], axis=0).astype(F32)
    gain_ref[...] = jnp.sum(grad_normed * (x * rms_inverse(x)), axis=0, keepdims=True)


def row_weights(own_ref, across_ref, att_ref, grad_ref, gains_ref, x_own_ref, x_across_ref):
    x = jnp.concatenate([x_own_ref[...], x_across_ref[...]], axis=0).astype(F32)
    normed = (x * rms_inverse(x) * gains_ref[0:1]).astype(BF16)
    da = jnp.concatenate([own_ref[...], across_ref[...]], axis=0)
    weights = dot(normed, grad_ref[...], ((0,), (0,)))
    return weights, dot(att_ref[...], da, ((0,), (0,)))


def backward_own(scale, head_dim, own_ref, across_ref, wout_ref, att_ref, qkv_ref, probs_ref,
                 gains_ref, w_ref, x_own_ref, x_across_ref, gw_ref, gout_ref, keep_ref, send_ref,
                 grad_ref, gain_ref, offsets_ref):
    attend_backward(
        scale, head_dim, own_ref, across_ref, wout_ref, qkv_ref, probs_ref, gains_ref, w_ref,
        x_own_ref, x_across_ref, keep_ref, send_ref, grad_ref, gain_ref, offsets_ref,
    )
    gw_ref[...], gout_ref[...] = row_weights(
        own_ref, across_ref, att_ref, grad_ref, gains_ref, x_own_ref, x_across_ref
    )


def sum_weights(buckets, table_cols, *refs):
    gw_ref, gout_ref, own_gain_ref, own_offsets_ref, gain_ref, offsets_ref = refs[7:13]
    gain_two_ref, router_ref, full_ref, out_ref = refs[13:]
    weights, outs = row_weights(*refs[:7])
    own_heads, length = offsets_ref.shape
    width, experts = router_ref.shape
    toks = length // 2
    rows = own_heads * buckets // table_cols
    spot = iota((1, length), 1)
    offset = jnp.where(spot >= toks, spot - length, spot)
    bucket = bucket_of(offset, buckets)
    table = []
    for t in range(table_cols):
        column = jnp.zeros((rows, 1), F32)
        for h in range(own_heads):
            belongs = iota((rows, length), 0) * table_cols + t == bucket * own_heads + h
            value = own_offsets_ref[h : h + 1] + offsets_ref[h : h + 1]
            column = column + jnp.sum(jnp.where(belongs, value, 0.0), axis=1, keepdims=True)
        table.append(column)
    table = jnp.concatenate([jnp.concatenate(table, axis=1)] * (width // rows), axis=0)
    narrow = jnp.concatenate(
        [own_gain_ref[...] + gain_ref[...], gain_two_ref[...], jnp.zeros((6, width), F32)], axis=0
    )
    narrow = jnp.transpose(narrow)[:, :2]
    weights = weights + gw_ref[...]
    pieces = [weights, router_ref[...].astype(F32), narrow, table]
    spare = full_ref.shape[-1] - sum(p.shape[1] for p in pieces)
    full_ref[...] = jnp.concatenate(pieces + [jnp.zeros((width, spare), F32)], axis=1).astype(BF16)
    out_ref[...] = (outs + gout_ref[...]).astype(BF16)


def sum_weights_message(buckets, table_cols, *refs):
    *rest, message_ref, full_ref, out_ref = refs
    sum_weights(buckets, table_cols, *rest, full_ref, out_ref)
    dests, _, wide = message_ref.shape
    rows = out_ref.shape[0] // dests
    used = full_ref.shape[1]
    block = dests * rows
    for s in range(dests):
        for j in range(4):
            at = j * block + s * rows
            message_ref[s, j * rows : (j + 1) * rows, :used] = full_ref[at : at + rows]
            if wide > used:
                message_ref[s, j * rows : (j + 1) * rows, used:] = jnp.zeros(
                    (rows, wide - used), BF16
                )
        put_rows(message_ref, s, out_ref[s * rows : (s + 1) * rows])


def sum_arrived(group_ref, arrived_ref, out_ref, own_ref, *send_refs):
    rows, used = own_ref.shape
    total = arrived_ref[0].astype(F32)
    for s in range(1, arrived_ref.shape[0]):
        total = total + arrived_ref[s].astype(F32)
    out_ref[...] = take_rows(total, rows, out_ref.shape[1])
    pieces = [total[j * rows : (j + 1) * rows, :used] for j in range(4)]
    own_ref[...] = choose(group_ref[0], pieces)
    for d, ref in enumerate(send_refs):
        ref[...] = choose(group_ref[0] ^ (d + 1), pieces).astype(BF16)


def finish_weights(own_heads, buckets, table_cols, group_ref, p0_ref, p1_ref, p2_ref, p3_ref,
                   q_ref, k_ref, v_ref, router_ref, one_ref, two_ref, table_ref):
    rows, width = q_ref.shape
    experts = router_ref.shape[0]
    cols = width // 4
    pieces = [ref[...].astype(F32) for ref in (p0_ref, p1_ref, p2_ref, p3_ref)]
    ordered = [choose(group_ref[0] ^ j, pieces) for j in range(4)]
    for n, ref in enumerate((q_ref, k_ref, v_ref)):
        ref[...] = jnp.concatenate([p[:, n * cols : (n + 1) * cols] for p in ordered], axis=1)
    at = 3 * cols
    small = sum(p[:, at : at + experts + 2] for p in pieces)
    square = -(-max(rows, experts) // 128) * 128
    padded = small[:, :experts]
    if square > experts:
        padded = jnp.concatenate([padded, jnp.zeros((rows, square - experts), F32)], axis=1)
    padded = jnp.concatenate([padded, jnp.zeros((square - rows, square), F32)], axis=0)
    router_ref[...] = jnp.transpose(padded)[:experts, :rows]
    eye = iota((rows, rows), 0) == iota((rows, rows), 1)
    for i, ref in enumerate((one_ref, two_ref)):
        column = small[:, experts + i : experts + i + 1]
        ref[...] = jnp.sum(jnp.where(eye, column, 0.0), axis=0, keepdims=True)
    at += experts + 2
    lines = []
    lane = iota((rows, 128), 1)
    for p in ordered:
        for h in range(own_heads):
            line = jnp.zeros((1, 128), F32)
            for t in range(table_cols):
                belongs = iota((rows, 128), 0) * table_cols + t == lane * own_heads + h
                value = jnp.where(belongs & (lane < buckets), p[:, at + t : at + t + 1], 0.0)
                line = line + jnp.sum(value, axis=0, keepdims=True)
            lines.append(line)
    table_ref[...] = jnp.concatenate(lines, axis=0)[:, :buckets]


def local(
    tokens,
    gain_one,
    w_query,
    w_key,
    w_value,
    w_out,
    bias_table,
    gain_two,
    w_router,
    w_inner,
    w_outer,
    segment_ids,
    routes,
    out_grad,
):
    toks = tokens.shape[1]
    width = tokens.shape[2]
    heads = bias_table.shape[1]
    buckets = bias_table.shape[0]
    head_dim = width // heads
    own_heads = heads // 4
    cols = own_heads * head_dim
    length = 2 * toks
    scale = head_dim ** (-0.5)
    sources = lax.axis_size("expert")
    experts = sources
    capacity = (5 * toks + 4 * experts - 1) // (4 * experts)
    slots = experts * capacity
    pad = -(-4 * capacity // 8) * 8
    rows = w_query.shape[0]
    core = lax.axis_index("dp")
    place = lax.axis_index("expert")
    half = sources // 2
    member = place // half
    first_core = core == 0
    place_at = place.reshape(1).astype(jnp.int32)
    group_at = (2 * core + member).reshape(1).astype(jnp.int32)
    table_cols = max(1, own_heads * buckets // rows)
    extra = max(table_cols, -(-length // rows))
    used = -(-(3 * cols + experts + 2 + extra) // 128) * 128
    aligned = rows % 8 == 0
    if aligned and used < width and (width - used) * (rows // 8) <= used:
        wide, total = used, 5 * rows + 8
    else:
        wide, total = max(used, width), 5 * rows

    def across_group(pieces):
        return [
            lax.ppermute(
                piece,
                ("dp", "expert"),
                [
                    (c * sources + e, (c ^ (d >> 1)) * sources + (e ^ (half * (d & 1))))
                    for c in range(2)
                    for e in range(sources)
                ],
            )
            for d, piece in enumerate(pieces, 1)
        ]

    own_tokens = tokens.reshape(toks, width)
    pair_tokens = swap_pair(own_tokens)

    own_piece, *pieces, out_rows = kernel_call(
        pack_weights, [((rows, used), BF16)] * 4 + [((rows, width), BF16)],
        group_at, w_query, w_key, w_value, w_router.T, gain_one.reshape(1, rows),
        gain_two.reshape(1, rows), w_out, segment_ids, scalars=1, late=range(1, 9),
        limit=60 * 1024 * 1024,
    )
    pieces = across_group(pieces)
    pair_tokens, own_piece, *pieces = lax.optimization_barrier((pair_tokens, own_piece, *pieces))
    (message,) = kernel_call(
        spread_weights, [((half, total, wide), BF16)],
        group_at, own_piece, *pieces, out_rows, scalars=1,
    )
    arrived = exchange_half(message)

    own_across = swap_core(own_tokens)
    pair_across = swap_core(pair_tokens)
    vectors, spread, later, chosen, send = kernel_call(
        functools.partial(prepare, capacity, pad),
        [
            ((own_heads, length), F32),
            ((2, toks, experts * pad), BF16),
            ((2, toks, experts * pad), BF16),
            ((toks, experts), F32),
            ((experts * pad, 4 * toks), BF16),
        ],
        group_at, bias_table, routes.reshape(toks, 1), scalars=2,
    )
    g_low = out_grad.reshape(toks, width)

    row_outs = [
        ((length, 3 * cols), BF16),
        ((own_heads, length, length), F32),
        ((length, cols), BF16),
        ((toks, width), F32),
        ((toks, width), BF16),
    ]
    placed = [((width, used), BF16), ((cols, width), BF16)]
    if aligned:
        weights, out_w, gains, *pair_kept = kernel_call(
            functools.partial(attend_first, scale, head_dim, experts),
            placed + [((8, width), F32)] + row_outs,
            group_at, place_at, arrived, pair_tokens, pair_across, vectors, scalars=2,
        )
    else:
        weights = arrived[:, : 4 * rows, :used].reshape(half, 2, 2, rows, used)
        weights = weights.transpose(1, 2, 0, 3, 4).reshape(width, used)
        out_w = arrived[:, 4 * rows :, :width].reshape(cols, width)
        gains, *pair_kept = kernel_call(
            functools.partial(attend_first_placed, scale, head_dim, experts),
            [((8, width), F32)] + row_outs,
            group_at, place_at, arrived, weights, out_w, pair_tokens, pair_across, vectors, scalars=2,
        )
    pair_qkv, pair_probs, pair_att, keep, away = pair_kept
    pair_sum = (keep + swap_core(away).astype(F32)).astype(BF16)
    pair_sum, out_w, gains = lax.optimization_barrier((pair_sum, out_w, gains))
    pair_sum = swap_pair(pair_sum)
    own_qkv, own_probs, own_att, keep, away = kernel_call(
        functools.partial(attend_own, scale, head_dim), row_outs,
        group_at, segment_ids, weights, out_w, gains, own_tokens, own_across, vectors, scalars=1,
    )
    router_w = weights[:, 3 * cols : 3 * cols + experts]
    middle, gate, outgoing = kernel_call(
        route_tokens,
        [((toks, width), F32), ((toks, 1), F32), ((experts * pad, width // 2), BF16)],
        own_tokens, keep, swap_core(away), pair_sum, gains, router_w, chosen, send, g_low,
    )
    incoming = exchange(outgoing.reshape(experts, pad, width // 2)).reshape(-1, width // 2)

    inner, outer = w_inner[0], w_outer[0]
    units = inner.shape[1]
    chunk = units // 3
    fixed = lambda shape: pl.BlockSpec(shape, lambda i: (0,) * len(shape))
    outs = [
        ((2 * slots, width), BF16, None),
        ((2 * slots, width), BF16, None),
        ((slots, width), BF16, None),
        ((slots, experts), F32, None),
        ((slots, 1), F32, None),
        ((2 * slots, units), BF16, pl.BlockSpec((2 * slots, chunk), lambda i: (0, i))),
        ((2 * slots, units), BF16, pl.BlockSpec((2 * slots, chunk), lambda i: (0, i))),
        ((2, slots, width), F32, None),
        ((2, slots, width), BF16, None),
    ]
    buffers, dslot, slot_g, slot_probs, slot_gate, hidden, dpre, keep, away = pl.pallas_call(
        functools.partial(run_expert, capacity),
        grid=(units // chunk,),
        out_shape=[jax.ShapeDtypeStruct(shape, dtype) for shape, dtype, _ in outs],
        in_specs=[
            pl.BlockSpec(memory_space=pltpu.SMEM),
            fixed((experts * pad, width // 2)),
            fixed((experts * pad, width // 2)),
            fixed((width, experts)),
            pl.BlockSpec((width, chunk), lambda i: (0, i)),
            pl.BlockSpec((chunk, width), lambda i: (i, 0)),
        ],
        out_specs=[spec or fixed(shape) for shape, _, spec in outs],
        scratch_shapes=[pltpu.VMEM((2, 2 * slots, width), F32)],
        compiler_params=pltpu.CompilerParams(vmem_limit_bytes=VMEM_BYTES),
    )(place_at, incoming, swap_core(incoming), router_w, inner, outer)
    grad_outer = dot(hidden, dslot, ((0,), (0,)))
    grad_inner = dot(buffers, dpre, ((0,), (0,)))
    back, grad_router = kernel_call(
        functools.partial(finish_expert, capacity),
        [((sources * pad, width // 2), BF16), ((width, experts), BF16)],
        place_at, keep, swap_core(away), buffers[:slots], slot_g, slot_probs, slot_gate, router_w,
        scalars=1,
    )
    back = exchange(back.reshape(sources, pad, width // 2)).reshape(-1, width // 2)

    grad_middle, grad_attn, grad_gain_two = kernel_call(
        norm_two_backward,
        [((toks, width), F32), ((toks, width), BF16), ((1, width), F32)],
        back, spread, middle, gains, g_low,
    )
    pair_grad = swap_pair(grad_attn)
    shared = (gains, weights)
    back_outs = [
        ((toks, width), F32),
        ((toks, width), BF16),
        ((length, 3 * cols), BF16),
        ((1, width), F32),
        ((own_heads, length), F32),
    ]
    grad_w, grad_out, grad_normed, away, _, own_gain, own_offsets = kernel_call(
        functools.partial(backward_own, scale, head_dim),
        [((width, 3 * cols), F32), ((cols, width), F32)] + back_outs,
        grad_attn, swap_core(grad_attn), out_w, own_att, own_qkv, own_probs, *shared,
        own_tokens, own_across,
    )
    pair_grad, grad_w, own_away = lax.optimization_barrier((pair_grad, grad_w, away))
    grad_normed = grad_normed + swap_core(own_away).astype(F32)
    pair_grads = (pair_grad, swap_core(pair_grad))
    keep, away, grad_qkv, pair_gain, pair_offsets = kernel_call(
        functools.partial(attend_backward, scale, head_dim), back_outs,
        *pair_grads, out_w, pair_qkv, pair_probs, *shared, pair_tokens, pair_across,
    )
    to_pair = (keep + swap_core(away).astype(F32)).astype(BF16)
    last = (
        *pair_grads, pair_att, grad_qkv, gains, pair_tokens, pair_across, grad_w, grad_out,
        own_gain, own_offsets, pair_gain, pair_offsets, grad_gain_two, grad_router,
    )
    flat = [((width, used), BF16), ((cols, width), BF16)]
    if aligned:
        message, _, _ = kernel_call(
            functools.partial(sum_weights_message, buckets, table_cols),
            [((half, total, wide), BF16), *flat], *last,
        )
    else:
        full, grad_out = kernel_call(
            functools.partial(sum_weights, buckets, table_cols), flat, *last
        )
        full = full.reshape(2, 2, half, rows, used).transpose(2, 0, 1, 3, 4)
        full = full.reshape(half, 4 * rows, used)
        grad_out = grad_out.reshape(half, rows, width)
        message = jnp.concatenate(
            [
                jnp.pad(full, ((0, 0), (0, 0), (0, wide - used))),
                jnp.pad(grad_out, ((0, 0), (0, 0), (0, wide - width))),
            ],
            axis=1,
        )
    message, to_pair = lax.optimization_barrier((message, to_pair))
    came = swap_pair(to_pair).astype(F32)
    arrived = exchange_half(message)
    (final,) = kernel_call(
        finish_layer, [((toks, width), BF16)], back, later, middle, gate
    )

    out_grad_w, own_piece, *pieces = kernel_call(
        sum_arrived, [((rows, width), F32), ((rows, used), F32)] + [((rows, used), BF16)] * 3,
        group_at, arrived, scalars=1,
    )
    came, own_piece = lax.optimization_barrier((came, own_piece))
    pieces = across_group(pieces)
    query_grad, key_grad, value_grad, router_grad, one_grad, two_grad, table_grad = kernel_call(
        functools.partial(finish_weights, own_heads, buckets, table_cols),
        [((rows, width), F32)] * 3
        + [((experts, rows), F32), ((1, rows), F32), ((1, rows), F32), ((heads, buckets), F32)],
        group_at, own_piece, *pieces, scalars=1,
    )

    x = own_tokens.astype(F32)
    inverse_one = rms_inverse(x)
    grad_input = grad_middle + norm_backward(
        grad_normed + came, x * inverse_one, inverse_one, gains[0:1]
    )
    return (
        final.reshape(tokens.shape),
        grad_input.astype(BF16).reshape(tokens.shape),
        one_grad.reshape(rows),
        query_grad,
        key_grad,
        value_grad,
        out_grad_w,
        table_grad.T,
        two_grad.reshape(rows),
        router_grad.T,
        grad_inner[None],
        grad_outer[None],
    )


def solution(mesh):
    both = ("dp", "expert")
    return jax.shard_map(
        local,
        mesh=mesh,
        in_specs=(
            P("expert", "dp", None),
            P(both),
            P(both, None),
            P(both, None),
            P(both, None),
            P(both, None),
            P(),
            P(both),
            P(both, None),
            P("expert", None, "dp"),
            P("expert", "dp", None),
            P("expert", None),
            P("expert", "dp", None),
            P("expert", "dp", None),
        ),
        out_specs=(
            P("expert", "dp", None),
            P("expert", "dp", None),
            P(both),
            P(both, None),
            P(both, None),
            P(both, None),
            P(both, None),
            P(),
            P(both),
            P(both, None),
            P("expert", None, "dp"),
            P("expert", "dp", None),
        ),
        check_vma=False,
    )
```

```python
import functools

import jax
import jax.numpy as jnp
from jax import lax
from jax.experimental import pallas as pl
from jax.experimental.pallas import tpu as pltpu
from jax.sharding import PartitionSpec as P

EPSILON = 1e-06
MASKED = -1000000000.0
BUCKET_EDGES = (1, 2, 3, 4, 5, 6, 7, 8, 12, 16, 23, 32, 46, 64, 91)
F32 = jnp.float32
BF16 = jnp.bfloat16
VMEM_BYTES = 24 * 1024 * 1024


def dot(left, right, dims=((1,), (0,))):
    return lax.dot_general(left, right, (dims, ((), ())), preferred_element_type=F32)


def rms_inverse(values):
    return lax.rsqrt(jnp.mean(values * values, axis=-1, keepdims=True) + EPSILON)


def norm_backward(grad_normed, unit_values, inverse, gain_values):
    grad_unit = grad_normed * gain_values
    projected = jnp.mean(grad_unit * unit_values, axis=-1, keepdims=True)
    return inverse * (grad_unit - unit_values * projected)


def swap_core(value):
    return lax.ppermute(value, "dp", [(0, 1), (1, 0)])


def swap_pair(value):
    n = lax.axis_size("expert")
    other = 3 * n // 4
    return lax.ppermute(value, "expert", [(i, i ^ other) for i in range(n)])


def exchange(value):
    return lax.all_to_all(value, "expert", split_axis=0, concat_axis=0, tiled=True)


def exchange_half(value):
    half = lax.axis_size("expert") // 2
    groups = [[q * half + s for s in range(half)] for q in range(2)]
    return lax.all_to_all(
        value, "expert", split_axis=0, concat_axis=0, tiled=True, axis_index_groups=groups
    )


def bucket_of(offset, total):
    distance = jnp.abs(offset)
    bucket = jnp.zeros(offset.shape, jnp.int32)
    for border in BUCKET_EDGES:
        bucket = bucket + (distance >= border).astype(jnp.int32)
    return bucket + total // 2 * (offset > 0).astype(jnp.int32)


def iota(shape, axis):
    return lax.broadcasted_iota(jnp.int32, shape, axis)


class LateRef:
    def __init__(self, source, target, sem):
        self.copy = pltpu.make_async_copy(source, target, sem)
        self.target = target
        self.shape = target.shape
        self.pending = True
        self.copy.start()

    def wait(self):
        if self.pending:
            self.copy.wait()
            self.pending = False

    def __getitem__(self, index):
        self.wait()
        return self.target[index]


def kernel_call(body, outs, *args, scalars=0, late=(), limit=VMEM_BYTES, held=()):
    count = len(args)
    late = sorted(late)

    def run(*refs):
        ins = list(refs[:count])
        out_refs = refs[count : count + len(outs)]
        scratch = refs[count + len(outs) :]
        for n, i in enumerate(late):
            ins[i] = LateRef(ins[i], scratch[n], scratch[-1].at[n])
        body(*ins, *out_refs, *scratch[len(late) : len(late) + len(held)])
        for i in late:
            ins[i].wait()

    spaces = [pltpu.SMEM if i < scalars else pltpu.VMEM for i in range(count)]
    for i in late:
        spaces[i] = pltpu.HBM
    scratch = [pltpu.VMEM(args[i].shape, args[i].dtype) for i in late]
    scratch += [pltpu.VMEM(shape, dtype) for shape, dtype in held]
    if late:
        scratch.append(pltpu.SemaphoreType.DMA((len(late),)))
    return pl.pallas_call(
        run,
        out_shape=[jax.ShapeDtypeStruct(shape, dtype) for shape, dtype in outs],
        in_specs=[pl.BlockSpec(memory_space=space) for space in spaces],
        out_specs=[pl.BlockSpec(memory_space=pltpu.VMEM)] * len(outs),
        scratch_shapes=scratch,
        compiler_params=pltpu.CompilerParams(vmem_limit_bytes=limit),
        cost_estimate=pl.CostEstimate(
            flops=1_000_000, bytes_accessed=1_000_000, transcendentals=0
        ),
    )(*args)


def choose(index, values):
    picked = values[0]
    for i in range(1, len(values)):
        picked = jnp.where(index == i, values[i], picked)
    return picked


def pack_weights(group_ref, q_ref, k_ref, v_ref, router_ref, one_ref, two_ref, wout_ref, docs_ref,
                 *refs):
    keep_ref, *out_refs = refs
    rows, width = q_ref.shape
    experts = router_ref.shape[0]
    cols = width // 4
    eye = iota((rows, rows), 0) == iota((rows, rows), 1)
    router = dot(eye.astype(F32).astype(BF16), router_ref[...], ((1,), (1,)))
    columns = [
        jnp.sum(jnp.where(eye, ref[...].astype(F32), 0.0), axis=1, keepdims=True)
        for ref in (one_ref, two_ref)
    ]
    docs = docs_ref[...].astype(F32)
    length = docs.shape[1]
    doc_cols = -(-length // rows)
    for t in range(doc_cols):
        belongs = iota((rows, length), 1) == iota((rows, length), 0) * doc_cols + t
        columns.append(jnp.sum(jnp.where(belongs, docs, 0.0), axis=1, keepdims=True))
    pad = out_refs[0].shape[1] - 3 * cols - experts - 2 - doc_cols
    small = jnp.concatenate(
        [router] + columns + [jnp.zeros((rows, pad), F32)], axis=1
    ).astype(BF16)
    weights = [ref[...] for ref in (q_ref, k_ref, v_ref)]
    pieces = [
        jnp.concatenate([w[:, j * cols : (j + 1) * cols] for w in weights] + [small], axis=1)
        for j in range(4)
    ]
    for d, out_ref in enumerate(out_refs, 1):
        out_ref[...] = choose(group_ref[0] ^ d, pieces)
    used = pieces[0].shape[1]
    keep_ref[:, :used] = choose(group_ref[0], pieces)
    keep_ref[:, used:] = wout_ref[...]


def put_rows(ref, dest, value):
    rows, width = value.shape
    wide = ref.shape[2]
    if wide >= width:
        ref[dest, 4 * rows :, :width] = value
        if wide > width:
            ref[dest, 4 * rows :, width:] = jnp.zeros((rows, wide - width), BF16)
        return
    over = width - wide
    blocks = rows // 8
    ref[dest, 4 * rows : 5 * rows] = value[:, :wide]
    for b in range(blocks):
        ref[dest, 5 * rows :, b * over : (b + 1) * over] = value[b * 8 : (b + 1) * 8, wide:]
    ref[dest, 5 * rows :, blocks * over :] = jnp.zeros((8, wide - blocks * over), BF16)


def take_rows(held, rows, width):
    wide = held.shape[1]
    if wide >= width:
        return held[4 * rows :, :width]
    over = width - wide
    tail = [held[5 * rows :, b * over : (b + 1) * over] for b in range(rows // 8)]
    return jnp.concatenate([held[4 * rows : 5 * rows], jnp.concatenate(tail, axis=0)], axis=1)


def spread_weights(group_ref, own_ref, p1_ref, p2_ref, p3_ref, out_ref):
    dests, _, wide = out_ref.shape
    rows, used = p1_ref.shape
    pieces = [own_ref[:, :used]] + [ref[...] for ref in (p1_ref, p2_ref, p3_ref)]
    value = jnp.concatenate([choose(group_ref[0] ^ j, pieces) for j in range(4)], axis=0)
    if wide > used:
        value = jnp.concatenate([value, jnp.zeros((4 * rows, wide - used), BF16)], axis=1)
    last = own_ref[:, used:]
    for dest in range(dests):
        out_ref[dest, : 4 * rows] = value
        put_rows(out_ref, dest, last)


def prepare(capacity, pad, group_ref, table_ref, routes_ref, vector_ref, spread_ref, later_ref,
            gather_ref, send_ref):
    buckets = table_ref.shape[0]
    own_heads, length = vector_ref.shape
    toks = length // 2
    group = group_ref[0]
    spot = iota((1, length), 1)
    offset = jnp.where(spot >= toks, spot - length, spot)
    bucket = bucket_of(offset, buckets)
    for h in range(own_heads):
        vector = jnp.zeros((1, length), F32)
        for b in range(buckets):
            vector = jnp.where(bucket == b, table_ref[b, group * own_heads + h], vector)
        vector_ref[h : h + 1] = vector
    experts = gather_ref.shape[1]
    route = routes_ref[...]
    chosen = route == iota((toks, experts), 1)
    gather_ref[...] = chosen.astype(F32)
    lower = (iota((toks, toks), 0) > iota((toks, toks), 1)).astype(BF16)
    counts = dot(lower, chosen.astype(BF16))
    slot = jnp.sum(jnp.where(chosen, counts, 0.0), axis=1, keepdims=True).astype(jnp.int32)
    across = iota((toks, experts * pad), 1)
    for i in range(4):
        place = jnp.where(slot < capacity, route * pad + i * capacity + slot, -1)
        spread = (place == across).astype(F32)
        target = (spread_ref, later_ref)[i % 2]
        target[i // 2] = spread.astype(BF16)
        send_ref[:, i * toks : (i + 1) * toks] = jnp.transpose(spread).astype(BF16)


def place_weights(arrived_ref, w_ref, wout_ref):
    sources = arrived_ref.shape[0]
    rows = wout_ref.shape[0] // sources
    used = w_ref.shape[1]
    width = wout_ref.shape[1]
    block = sources * rows
    for s in range(sources):
        for j in range(4):
            w_ref[j * block + s * rows : j * block + (s + 1) * rows] = arrived_ref[
                s, j * rows : (j + 1) * rows, :used
            ]
        wout_ref[s * rows : (s + 1) * rows] = take_rows(arrived_ref[s], rows, width)


def gain_rows(experts, cols, w_ref, gains_ref):
    small = w_ref[:, 3 * cols :]
    pick = (iota((8, small.shape[1]), 1) == iota((8, small.shape[1]), 0) + experts).astype(BF16)
    gains_ref[...] = dot(pick, small, ((1,), (1,)))


def attend(scale, head_dim, docs, group_ref, w_ref, wout_ref, gains_ref, own_ref, across_ref,
           vector_ref, qkv_ref, probs_ref, att_ref, keep_ref, send_ref):
    own_heads, length = vector_ref.shape
    cols = own_heads * head_dim
    toks = own_ref.shape[0]
    vectors = vector_ref[...]
    turned = jnp.concatenate([docs[:, toks:], docs[:, :toks]], axis=1)
    across = jnp.broadcast_to(jnp.where(group_ref[0] < 2, docs, turned), (length, length))
    same = across == jnp.transpose(across)
    x = jnp.concatenate([own_ref[...], across_ref[...]], axis=0).astype(F32)
    normed = (x * rms_inverse(x) * gains_ref[0:1]).astype(BF16)
    qkv = dot(normed, w_ref[:, : 3 * cols]).astype(BF16)
    qkv_ref[...] = qkv
    parts = []
    for h in range(own_heads):
        at = h * head_dim
        q = qkv[:, at : at + head_dim]
        k = qkv[:, cols + at : cols + at + head_dim]
        v = qkv[:, 2 * cols + at : 2 * cols + at + head_dim]
        full = jnp.broadcast_to(vectors[h : h + 1], (length, length))
        bias = pltpu.roll(full, 0, 1, stride=1, stride_axis=0)
        scores = jnp.where(same, dot(q, k, ((1,), (1,))) * scale + bias, MASKED)
        top = jnp.max(scores, axis=1, keepdims=True)
        raised = jnp.exp(scores - top)
        probs = raised * (1.0 / jnp.sum(raised, axis=1, keepdims=True))
        probs_ref[h] = probs
        parts.append(dot(probs.astype(BF16), v))
    attended = jnp.concatenate(parts, axis=1).astype(BF16)
    att_ref[...] = attended
    partial = dot(attended, wout_ref[...])
    keep_ref[...] = partial[:toks]
    send_ref[...] = partial[toks:].astype(BF16)


def docs_of_pair(at, length, rows, group_ref, place_ref, arrived_ref):
    sources = arrived_ref.shape[0]
    doc_cols = -(-length // rows)
    held = arrived_ref[(place_ref[0] % sources) ^ (sources // 2)]
    blocks = [held[j * rows : (j + 1) * rows, at : at + doc_cols].astype(F32) for j in range(4)]
    block = choose(group_ref[0] ^ 1, blocks)
    docs = jnp.zeros((1, length), F32)
    for t in range(doc_cols):
        belongs = iota((rows, length), 1) == iota((rows, length), 0) * doc_cols + t
        docs = docs + jnp.sum(jnp.where(belongs, block[:, t : t + 1], 0.0), axis=0, keepdims=True)
    return docs


def attend_own(scale, head_dim, group_ref, docs_ref, *refs):
    attend(scale, head_dim, docs_ref[...].astype(F32), group_ref, *refs)


def attend_first(scale, head_dim, experts, group_ref, place_ref, arrived_ref, own_ref, across_ref,
                 vector_ref, w_ref, wout_ref, gains_ref, *outs):
    place_weights(arrived_ref, w_ref, wout_ref)
    cols = wout_ref.shape[0]
    gain_rows(experts, cols, w_ref, gains_ref)
    docs = docs_of_pair(
        3 * cols + experts + 2, vector_ref.shape[1], cols // arrived_ref.shape[0], group_ref, place_ref,
        arrived_ref,
    )
    attend(scale, head_dim, docs, group_ref, w_ref, wout_ref, gains_ref, own_ref, across_ref,
           vector_ref, *outs)


def attend_first_placed(scale, head_dim, experts, group_ref, place_ref, arrived_ref, w_ref, wout_ref,
                        own_ref, across_ref, vector_ref, gains_ref, *outs):
    cols = wout_ref.shape[0]
    gain_rows(experts, cols, w_ref, gains_ref)
    docs = docs_of_pair(
        3 * cols + experts + 2, vector_ref.shape[1], cols // arrived_ref.shape[0], group_ref, place_ref,
        arrived_ref,
    )
    attend(scale, head_dim, docs, group_ref, w_ref, wout_ref, gains_ref, own_ref, across_ref,
           vector_ref, *outs)


def route_tokens(x_ref, keep_ref, core_ref, came_ref, gains_ref, w_ref, chosen_ref, send_ref,
                 g_ref, middle_ref, gate_ref, out_ref):
    middle = x_ref[...].astype(F32) + (
        (keep_ref[...] + core_ref[...].astype(F32)) + came_ref[...].astype(F32)
    )
    middle_ref[...] = middle
    normed = (middle * rms_inverse(middle) * gains_ref[1:2]).astype(BF16)
    g = g_ref[...]
    half = g.shape[1] // 2
    both = jnp.concatenate([normed[:, :half], g[:, :half], normed[:, half:], g[:, half:]], axis=0)
    out_ref[...] = dot(send_ref[...], both).astype(BF16)
    probs = jax.nn.softmax(dot(normed, w_ref[...]), axis=-1)
    gate_ref[...] = jnp.sum(probs * chosen_ref[...], axis=1, keepdims=True)


def run_expert(capacity, place_ref, own_ref, other_ref, router_ref, inner_ref, outer_ref, buf_ref,
               dslot_ref, g_ref, probs_ref, gate_ref, hidden_ref, dpre_ref, keep_ref, send_ref):
    slots = buf_ref.shape[0] // 2
    half = own_ref.shape[1]
    experts = router_ref.shape[1]
    pad = own_ref.shape[0] // (slots // capacity)
    shape = (4 * slots, own_ref.shape[0])
    row = iota(shape, 0)
    part = row // slots
    inside = row - part * slots
    source = inside // capacity
    wanted = source * pad + part * capacity + (inside - source * capacity)
    select = (iota(shape, 1) == wanted).astype(BF16)
    rows = dot(select, jnp.concatenate([own_ref[...], other_ref[...]], axis=1))
    mine = (iota((1, experts), 1) == place_ref[0]).astype(F32)
    for side in range(2):
        at = side * slots
        cut = rows[:, side * half : (side + 1) * half]
        buffers = jnp.concatenate([cut[:slots], cut[2 * slots : 3 * slots]], axis=1).astype(BF16)
        g = jnp.concatenate([cut[slots : 2 * slots], cut[3 * slots :]], axis=1)
        buf_ref[at : at + slots] = buffers
        probs = jax.nn.softmax(dot(buffers, router_ref[...]), axis=-1)
        gate = jnp.sum(probs * mine, axis=1, keepdims=True)
        dslot_ref[at : at + slots] = (gate * g).astype(BF16)
        if side == 0:
            g_ref[...] = g.astype(BF16)
            probs_ref[...] = probs
            gate_ref[...] = gate
    inner = inner_ref[...]
    outer = outer_ref[...]
    pre = dot(buf_ref[...], inner)
    cdf = 0.5 * (1.0 + lax.erf(pre * (0.5**0.5)))
    hidden = (pre * cdf).astype(BF16)
    hidden_ref[...] = hidden
    slope = cdf + pre * jnp.exp(-0.5 * pre * pre) * 0.3989422804014327
    dpre = (dot(dslot_ref[...], outer, ((1,), (1,))) * slope).astype(BF16)
    dpre_ref[...] = dpre
    result = dot(hidden, outer)
    keep_ref[0] = result[:slots]
    send_ref[0] = result[slots:].astype(BF16)
    back = dot(dpre, inner, ((1,), (1,)))
    keep_ref[1] = back[:slots]
    send_ref[1] = back[slots:].astype(BF16)


def finish_expert(capacity, place_ref, keep_ref, came_ref, buf_ref, g_ref, probs_ref, gate_ref,
                  router_ref, out_ref, grad_ref):
    slots = g_ref.shape[0]
    experts = router_ref.shape[1]
    pad = out_ref.shape[0] // (slots // capacity)
    total = (keep_ref[...] + came_ref[...].astype(F32)).astype(BF16)
    result = total[0]
    mine = (iota((1, experts), 1) == place_ref[0]).astype(F32)
    grad_gate = jnp.sum(g_ref[...].astype(F32) * result.astype(F32), axis=1, keepdims=True)
    grad_logits = (grad_gate * gate_ref[...] * (mine - probs_ref[...])).astype(BF16)
    grad_ref[...] = dot(buf_ref[...], grad_logits, ((0,), (0,))).astype(BF16)
    back = total[1].astype(F32) + dot(grad_logits, router_ref[...], ((1,), (1,)))
    shape = (out_ref.shape[0], 4 * slots)
    row = iota(shape, 0)
    source = row // pad
    inside = row - source * pad
    part = inside // capacity
    wanted = jnp.where(part < 4, part * slots + source * capacity + inside - part * capacity, -1)
    expand = (iota(shape, 1) == wanted).astype(BF16)
    back = back.astype(BF16)
    half = back.shape[1] // 2
    both = jnp.concatenate([back[:, :half], result[:, :half], back[:, half:], result[:, half:]], axis=0)
    out_ref[...] = dot(expand, both).astype(BF16)


def middle_backward(back_ref, spread_ref, middle_ref, gains_ref, g_ref):
    middle = middle_ref[...]
    inverse = rms_inverse(middle)
    unit = middle * inverse
    rows = back_ref[...]
    grad_normed = jnp.concatenate([dot(spread_ref[i], rows) for i in range(2)], axis=1)
    dmiddle = g_ref[...].astype(F32) + norm_backward(grad_normed, unit, inverse, gains_ref[1:2])
    return dmiddle, grad_normed * unit


def norm_two_backward(back_ref, spread_ref, middle_ref, gains_ref, g_ref, da_ref, gain_ref):
    dmiddle, scaled = middle_backward(back_ref, spread_ref, middle_ref, gains_ref, g_ref)
    gain_ref[...] = jnp.sum(scaled, axis=0, keepdims=True)
    da_ref[...] = dmiddle.astype(BF16)


def finish_layer(back_ref, spread_ref, later_ref, middle_ref, gains_ref, g_ref, gate_ref, out_ref,
                 dmiddle_ref):
    rows = back_ref[...]
    combined = jnp.concatenate([dot(later_ref[i], rows) for i in range(2)], axis=1)
    out_ref[...] = (middle_ref[...] + gate_ref[...] * combined).astype(BF16)
    dmiddle_ref[...] = middle_backward(back_ref, spread_ref, middle_ref, gains_ref, g_ref)[0]


def attend_backward(scale, head_dim, own_ref, across_ref, wout_ref, qkv_ref, probs_ref, gains_ref,
                    w_ref, x_own_ref, x_across_ref, keep_ref, send_ref, grad_ref, gain_ref,
                    offsets_ref):
    own_heads = probs_ref.shape[0]
    cols = own_heads * head_dim
    toks = own_ref.shape[0]
    length = 2 * toks
    flip = (iota((length, length), 0) + iota((length, length), 1) == length - 1).astype(BF16)
    da = jnp.concatenate([own_ref[...], across_ref[...]], axis=0)
    grad_att = dot(da, wout_ref[...], ((1,), (1,))).astype(BF16)
    qkv = qkv_ref[...]
    parts = [[], [], []]
    for h in range(own_heads):
        at = h * head_dim
        q = qkv[:, at : at + head_dim]
        k = qkv[:, cols + at : cols + at + head_dim]
        v = qkv[:, 2 * cols + at : 2 * cols + at + head_dim]
        gh = grad_att[:, at : at + head_dim]
        probs = probs_ref[h]
        grad_probs = dot(gh, v, ((1,), (1,)))
        row_dot = jnp.sum(probs * grad_probs, axis=1, keepdims=True)
        ds = (probs * (grad_probs - row_dot)).astype(BF16)
        turned = pltpu.roll(dot(flip, ds), 1, 1, stride=1, stride_axis=0)
        offsets_ref[h : h + 1] = jnp.sum(turned, axis=0, keepdims=True)
        parts[0].append(dot(ds, k) * scale)
        parts[1].append(dot(ds, q, ((0,), (0,))) * scale)
        parts[2].append(dot(probs.astype(BF16), gh, ((0,), (0,))))
    grad_qkv = jnp.concatenate(parts[0] + parts[1] + parts[2], axis=1).astype(BF16)
    grad_ref[...] = grad_qkv
    grad_normed = dot(grad_qkv, w_ref[:, : 3 * cols], ((1,), (1,)))
    keep_ref[...] = grad_normed[:toks]
    send_ref[...] = grad_normed[toks:].astype(BF16)
    x = jnp.concatenate([x_own_ref[...], x_across_ref[...]], axis=0).astype(F32)
    gain_ref[...] = jnp.sum(grad_normed * (x * rms_inverse(x)), axis=0, keepdims=True)


def row_weights(own_ref, across_ref, att_ref, grad_ref, gains_ref, x_own_ref, x_across_ref):
    x = jnp.concatenate([x_own_ref[...], x_across_ref[...]], axis=0).astype(F32)
    normed = (x * rms_inverse(x) * gains_ref[0:1]).astype(BF16)
    da = jnp.concatenate([own_ref[...], across_ref[...]], axis=0)
    weights = dot(normed, grad_ref[...], ((0,), (0,)))
    return weights, dot(att_ref[...], da, ((0,), (0,)))


def backward_own(scale, head_dim, own_ref, across_ref, wout_ref, att_ref, qkv_ref, probs_ref,
                 gains_ref, w_ref, x_own_ref, x_across_ref, gw_ref, gout_ref, keep_ref, send_ref,
                 grad_ref, gain_ref, offsets_ref):
    attend_backward(
        scale, head_dim, own_ref, across_ref, wout_ref, qkv_ref, probs_ref, gains_ref, w_ref,
        x_own_ref, x_across_ref, keep_ref, send_ref, grad_ref, gain_ref, offsets_ref,
    )
    gw_ref[...], gout_ref[...] = row_weights(
        own_ref, across_ref, att_ref, grad_ref, gains_ref, x_own_ref, x_across_ref
    )


def sum_weights(buckets, table_cols, *refs):
    gw_ref, gout_ref, own_gain_ref, own_offsets_ref, gain_ref, offsets_ref = refs[7:13]
    gain_two_ref, router_ref, full_ref, out_ref = refs[13:]
    weights, outs = row_weights(*refs[:7])
    own_heads, length = offsets_ref.shape
    width, experts = router_ref.shape
    toks = length // 2
    rows = own_heads * buckets // table_cols
    spot = iota((1, length), 1)
    offset = jnp.where(spot >= toks, spot - length, spot)
    bucket = bucket_of(offset, buckets)
    table = []
    for t in range(table_cols):
        column = jnp.zeros((rows, 1), F32)
        for h in range(own_heads):
            belongs = iota((rows, length), 0) * table_cols + t == bucket * own_heads + h
            value = own_offsets_ref[h : h + 1] + offsets_ref[h : h + 1]
            column = column + jnp.sum(jnp.where(belongs, value, 0.0), axis=1, keepdims=True)
        table.append(column)
    table = jnp.concatenate([jnp.concatenate(table, axis=1)] * (width // rows), axis=0)
    narrow = jnp.concatenate(
        [own_gain_ref[...] + gain_ref[...], gain_two_ref[...], jnp.zeros((6, width), F32)], axis=0
    )
    narrow = jnp.transpose(narrow)[:, :2]
    weights = weights + gw_ref[...]
    pieces = [weights, router_ref[...].astype(F32), narrow, table]
    spare = full_ref.shape[-1] - sum(p.shape[1] for p in pieces)
    full_ref[...] = jnp.concatenate(pieces + [jnp.zeros((width, spare), F32)], axis=1).astype(BF16)
    out_ref[...] = (outs + gout_ref[...]).astype(BF16)


def sum_weights_message(buckets, table_cols, *refs):
    *rest, message_ref, full_ref, out_ref = refs
    sum_weights(buckets, table_cols, *rest, full_ref, out_ref)
    dests, _, wide = message_ref.shape
    rows = out_ref.shape[0] // dests
    used = full_ref.shape[1]
    block = dests * rows
    for s in range(dests):
        for j in range(4):
            at = j * block + s * rows
            message_ref[s, j * rows : (j + 1) * rows, :used] = full_ref[at : at + rows]
            if wide > used:
                message_ref[s, j * rows : (j + 1) * rows, used:] = jnp.zeros(
                    (rows, wide - used), BF16
                )
        put_rows(message_ref, s, out_ref[s * rows : (s + 1) * rows])


def sum_arrived(group_ref, arrived_ref, out_ref, own_ref, *send_refs):
    rows, used = own_ref.shape
    total = arrived_ref[0].astype(F32)
    for s in range(1, arrived_ref.shape[0]):
        total = total + arrived_ref[s].astype(F32)
    out_ref[...] = take_rows(total, rows, out_ref.shape[1])
    pieces = [total[j * rows : (j + 1) * rows, :used] for j in range(4)]
    own_ref[...] = choose(group_ref[0], pieces)
    for d, ref in enumerate(send_refs):
        ref[...] = choose(group_ref[0] ^ (d + 1), pieces).astype(BF16)


def finish_weights(own_heads, buckets, table_cols, group_ref, p0_ref, p1_ref, p2_ref, p3_ref,
                   grad_ref, core_ref, came_ref, dmiddle_ref, x_ref, gains_ref, q_ref, k_ref, v_ref,
                   router_ref, one_ref, two_ref, table_ref, out_ref):
    x = x_ref[...].astype(F32)
    inverse = rms_inverse(x)
    grad_normed = grad_ref[...] + core_ref[...].astype(F32) + came_ref[...].astype(F32)
    out_ref[...] = (
        dmiddle_ref[...] + norm_backward(grad_normed, x * inverse, inverse, gains_ref[0:1])
    ).astype(BF16)
    rows, width = q_ref.shape
    experts = router_ref.shape[0]
    cols = width // 4
    pieces = [ref[...].astype(F32) for ref in (p0_ref, p1_ref, p2_ref, p3_ref)]
    ordered = [choose(group_ref[0] ^ j, pieces) for j in range(4)]
    for n, ref in enumerate((q_ref, k_ref, v_ref)):
        ref[...] = jnp.concatenate([p[:, n * cols : (n + 1) * cols] for p in ordered], axis=1)
    at = 3 * cols
    small = sum(p[:, at : at + experts + 2] for p in pieces)
    square = -(-max(rows, experts) // 128) * 128
    padded = small[:, :experts]
    if square > experts:
        padded = jnp.concatenate([padded, jnp.zeros((rows, square - experts), F32)], axis=1)
    padded = jnp.concatenate([padded, jnp.zeros((square - rows, square), F32)], axis=0)
    router_ref[...] = jnp.transpose(padded)[:experts, :rows]
    eye = iota((rows, rows), 0) == iota((rows, rows), 1)
    for i, ref in enumerate((one_ref, two_ref)):
        column = small[:, experts + i : experts + i + 1]
        ref[...] = jnp.sum(jnp.where(eye, column, 0.0), axis=0, keepdims=True)
    at += experts + 2
    lines = []
    lane = iota((rows, 128), 1)
    for p in ordered:
        for h in range(own_heads):
            line = jnp.zeros((1, 128), F32)
            for t in range(table_cols):
                belongs = iota((rows, 128), 0) * table_cols + t == lane * own_heads + h
                value = jnp.where(belongs & (lane < buckets), p[:, at + t : at + t + 1], 0.0)
                line = line + jnp.sum(value, axis=0, keepdims=True)
            lines.append(line)
    table_ref[...] = jnp.concatenate(lines, axis=0)[:, :buckets]


def local(
    tokens,
    gain_one,
    w_query,
    w_key,
    w_value,
    w_out,
    bias_table,
    gain_two,
    w_router,
    w_inner,
    w_outer,
    segment_ids,
    routes,
    out_grad,
):
    toks = tokens.shape[1]
    width = tokens.shape[2]
    heads = bias_table.shape[1]
    buckets = bias_table.shape[0]
    head_dim = width // heads
    own_heads = heads // 4
    cols = own_heads * head_dim
    length = 2 * toks
    scale = head_dim ** (-0.5)
    sources = lax.axis_size("expert")
    experts = sources
    capacity = (5 * toks + 4 * experts - 1) // (4 * experts)
    slots = experts * capacity
    pad = -(-4 * capacity // 8) * 8
    rows = w_query.shape[0]
    core = lax.axis_index("dp")
    place = lax.axis_index("expert")
    half = sources // 2
    member = place // half
    first_core = core == 0
    place_at = place.reshape(1).astype(jnp.int32)
    group_at = (2 * core + member).reshape(1).astype(jnp.int32)
    table_cols = max(1, own_heads * buckets // rows)
    extra = max(table_cols, -(-length // rows))
    used = -(-(3 * cols + experts + 2 + extra) // 128) * 128
    aligned = rows % 8 == 0
    if aligned and used < width and (width - used) * (rows // 8) <= used:
        wide, total = used, 5 * rows + 8
    else:
        wide, total = max(used, width), 5 * rows

    def across_group(pieces):
        return [
            lax.ppermute(
                piece,
                ("dp", "expert"),
                [
                    (c * sources + e, (c ^ (d >> 1)) * sources + (e ^ (half * (d & 1))))
                    for c in range(2)
                    for e in range(sources)
                ],
            )
            for d, piece in enumerate(pieces, 1)
        ]

    own_tokens = tokens.reshape(toks, width)
    pair_tokens = swap_pair(own_tokens)

    own_piece, *pieces = kernel_call(
        pack_weights, [((rows, used + width), BF16)] + [((rows, used), BF16)] * 3,
        group_at, w_query, w_key, w_value, w_router.T, gain_one.reshape(1, rows),
        gain_two.reshape(1, rows), w_out, segment_ids, scalars=1, late=range(1, 9),
        limit=60 * 1024 * 1024,
    )
    pieces = across_group(pieces)
    pair_tokens, own_piece, *pieces = lax.optimization_barrier((pair_tokens, own_piece, *pieces))
    (message,) = kernel_call(
        spread_weights, [((half, total, wide), BF16)],
        group_at, own_piece, *pieces, scalars=1,
    )
    arrived = exchange_half(message)

    own_across = swap_core(own_tokens)
    pair_across = swap_core(pair_tokens)
    vectors, spread, later, chosen, send = kernel_call(
        functools.partial(prepare, capacity, pad),
        [
            ((own_heads, length), F32),
            ((2, toks, experts * pad), BF16),
            ((2, toks, experts * pad), BF16),
            ((toks, experts), F32),
            ((experts * pad, 4 * toks), BF16),
        ],
        group_at, bias_table, routes.reshape(toks, 1), scalars=2,
    )
    g_low = out_grad.reshape(toks, width)

    row_outs = [
        ((length, 3 * cols), BF16),
        ((own_heads, length, length), F32),
        ((length, cols), BF16),
        ((toks, width), F32),
        ((toks, width), BF16),
    ]
    placed = [((width, used), BF16), ((cols, width), BF16)]
    if aligned:
        weights, out_w, gains, *pair_kept = kernel_call(
            functools.partial(attend_first, scale, head_dim, experts),
            placed + [((8, width), F32)] + row_outs,
            group_at, place_at, arrived, pair_tokens, pair_across, vectors, scalars=2,
        )
    else:
        weights = arrived[:, : 4 * rows, :used].reshape(half, 2, 2, rows, used)
        weights = weights.transpose(1, 2, 0, 3, 4).reshape(width, used)
        out_w = arrived[:, 4 * rows :, :width].reshape(cols, width)
        gains, *pair_kept = kernel_call(
            functools.partial(attend_first_placed, scale, head_dim, experts),
            [((8, width), F32)] + row_outs,
            group_at, place_at, arrived, weights, out_w, pair_tokens, pair_across, vectors, scalars=2,
        )
    pair_qkv, pair_probs, pair_att, keep, away = pair_kept
    pair_sum = (keep + swap_core(away).astype(F32)).astype(BF16)
    pair_sum, out_w, gains = lax.optimization_barrier((pair_sum, out_w, gains))
    pair_sum = swap_pair(pair_sum)
    own_qkv, own_probs, own_att, keep, away = kernel_call(
        functools.partial(attend_own, scale, head_dim), row_outs,
        group_at, segment_ids, weights, out_w, gains, own_tokens, own_across, vectors, scalars=1,
    )
    router_w = weights[:, 3 * cols : 3 * cols + experts]
    middle, gate, outgoing = kernel_call(
        route_tokens,
        [((toks, width), F32), ((toks, 1), F32), ((experts * pad, width // 2), BF16)],
        own_tokens, keep, swap_core(away), pair_sum, gains, router_w, chosen, send, g_low,
    )
    incoming = exchange(outgoing.reshape(experts, pad, width // 2)).reshape(-1, width // 2)

    inner, outer = w_inner[0], w_outer[0]
    units = inner.shape[1]
    buffers, dslot, slot_g, slot_probs, slot_gate, hidden, dpre, keep, away = kernel_call(
        functools.partial(run_expert, capacity),
        [
            ((2 * slots, width), BF16),
            ((2 * slots, width), BF16),
            ((slots, width), BF16),
            ((slots, experts), F32),
            ((slots, 1), F32),
            ((2 * slots, units), BF16),
            ((2 * slots, units), BF16),
            ((2, slots, width), F32),
            ((2, slots, width), BF16),
        ],
        place_at, incoming, swap_core(incoming), router_w, inner, outer, scalars=1,
    )
    grad_outer = dot(hidden, dslot, ((0,), (0,)))
    grad_inner = dot(buffers, dpre, ((0,), (0,)))
    back, grad_router = kernel_call(
        functools.partial(finish_expert, capacity),
        [((sources * pad, width // 2), BF16), ((width, experts), BF16)],
        place_at, keep, swap_core(away), buffers[:slots], slot_g, slot_probs, slot_gate, router_w,
        scalars=1,
    )
    back = exchange(back.reshape(sources, pad, width // 2)).reshape(-1, width // 2)

    grad_attn, grad_gain_two = kernel_call(
        norm_two_backward, [((toks, width), BF16), ((1, width), F32)],
        back, spread, middle, gains, g_low,
    )
    pair_grad = swap_pair(grad_attn)
    shared = (gains, weights)
    back_outs = [
        ((toks, width), F32),
        ((toks, width), BF16),
        ((length, 3 * cols), BF16),
        ((1, width), F32),
        ((own_heads, length), F32),
    ]
    grad_w, grad_out, grad_normed, away, _, own_gain, own_offsets = kernel_call(
        functools.partial(backward_own, scale, head_dim),
        [((width, 3 * cols), F32), ((cols, width), F32)] + back_outs,
        grad_attn, swap_core(grad_attn), out_w, own_att, own_qkv, own_probs, *shared,
        own_tokens, own_across,
    )
    pair_grad, grad_w, own_away = lax.optimization_barrier((pair_grad, grad_w, away))
    own_came = swap_core(own_away)
    pair_grads = (pair_grad, swap_core(pair_grad))
    keep, away, grad_qkv, pair_gain, pair_offsets = kernel_call(
        functools.partial(attend_backward, scale, head_dim), back_outs,
        *pair_grads, out_w, pair_qkv, pair_probs, *shared, pair_tokens, pair_across,
    )
    to_pair = (keep + swap_core(away).astype(F32)).astype(BF16)
    last = (
        *pair_grads, pair_att, grad_qkv, gains, pair_tokens, pair_across, grad_w, grad_out,
        own_gain, own_offsets, pair_gain, pair_offsets, grad_gain_two, grad_router,
    )
    flat = [((width, used), BF16), ((cols, width), BF16)]
    if aligned:
        (message,) = kernel_call(
            functools.partial(sum_weights_message, buckets, table_cols),
            [((half, total, wide), BF16)], *last, held=flat,
        )
    else:
        full, grad_out = kernel_call(
            functools.partial(sum_weights, buckets, table_cols), flat, *last
        )
        full = full.reshape(2, 2, half, rows, used).transpose(2, 0, 1, 3, 4)
        full = full.reshape(half, 4 * rows, used)
        grad_out = grad_out.reshape(half, rows, width)
        message = jnp.concatenate(
            [
                jnp.pad(full, ((0, 0), (0, 0), (0, wide - used))),
                jnp.pad(grad_out, ((0, 0), (0, 0), (0, wide - width))),
            ],
            axis=1,
        )
    came = swap_pair(to_pair)
    arrived = exchange_half(message)
    final, grad_middle = kernel_call(
        finish_layer, [((toks, width), BF16), ((toks, width), F32)],
        back, spread, later, middle, gains, g_low, gate,
    )

    arrived, grad_inner, grad_outer, final, grad_middle = lax.optimization_barrier(
        (arrived, grad_inner, grad_outer, final, grad_middle)
    )

    out_grad_w, own_piece, *pieces = kernel_call(
        sum_arrived, [((rows, width), F32), ((rows, used), F32)] + [((rows, used), BF16)] * 3,
        group_at, arrived, scalars=1,
    )
    pieces = across_group(pieces)
    query_grad, key_grad, value_grad, router_grad, one_grad, two_grad, table_grad, grad_input = kernel_call(
        functools.partial(finish_weights, own_heads, buckets, table_cols),
        [((rows, width), F32)] * 3
        + [((experts, rows), F32), ((1, rows), F32), ((1, rows), F32), ((heads, buckets), F32)]
        + [((toks, width), BF16)],
        group_at, own_piece, *pieces, grad_normed, own_came, came, grad_middle, own_tokens, gains,
        scalars=1,
    )

    return (
        final.reshape(tokens.shape),
        grad_input.reshape(tokens.shape),
        one_grad.reshape(rows),
        query_grad,
        key_grad,
        value_grad,
        out_grad_w,
        table_grad.T,
        two_grad.reshape(rows),
        router_grad.T,
        grad_inner[None],
        grad_outer[None],
    )


def solution(mesh):
    both = ("dp", "expert")
    return jax.shard_map(
        local,
        mesh=mesh,
        in_specs=(
            P("expert", "dp", None),
            P(both),
            P(both, None),
            P(both, None),
            P(both, None),
            P(both, None),
            P(),
            P(both),
            P(both, None),
            P("expert", None, "dp"),
            P("expert", "dp", None),
            P("expert", None),
            P("expert", "dp", None),
            P("expert", "dp", None),
        ),
        out_specs=(
            P("expert", "dp", None),
            P("expert", "dp", None),
            P(both),
            P(both, None),
            P(both, None),
            P(both, None),
            P(both, None),
            P(),
            P(both),
            P(both, None),
            P("expert", None, "dp"),
            P("expert", "dp", None),
        ),
        check_vma=False,
    )
```

```python
import functools

import jax
import jax.numpy as jnp
from jax import lax
from jax.experimental import pallas as pl
from jax.experimental.pallas import tpu as pltpu
from jax.sharding import PartitionSpec as P

EPSILON = 1e-06
MASKED = -1000000000.0
BUCKET_EDGES = (1, 2, 3, 4, 5, 6, 7, 8, 12, 16, 23, 32, 46, 64, 91)
F32 = jnp.float32
BF16 = jnp.bfloat16
ORDER = (3, 1, 2)
VMEM_BYTES = 24 * 1024 * 1024


def dot(left, right, dims=((1,), (0,))):
    return lax.dot_general(left, right, (dims, ((), ())), preferred_element_type=F32)


def rms_inverse(values):
    return lax.rsqrt(jnp.mean(values * values, axis=-1, keepdims=True) + EPSILON)


def norm_backward(grad_normed, unit_values, inverse, gain_values):
    grad_unit = grad_normed * gain_values
    projected = jnp.mean(grad_unit * unit_values, axis=-1, keepdims=True)
    return inverse * (grad_unit - unit_values * projected)


def swap_core(value):
    return lax.ppermute(value, "dp", [(0, 1), (1, 0)])


def swap_pair(value):
    n = lax.axis_size("expert")
    other = 3 * n // 4
    return lax.ppermute(value, "expert", [(i, i ^ other) for i in range(n)])


def exchange(value):
    return lax.all_to_all(value, "expert", split_axis=0, concat_axis=0, tiled=True)


def exchange_half(value):
    half = lax.axis_size("expert") // 2
    groups = [[q * half + s for s in range(half)] for q in range(2)]
    return lax.all_to_all(
        value, "expert", split_axis=0, concat_axis=0, tiled=True, axis_index_groups=groups
    )


def bucket_of(offset, total):
    distance = jnp.abs(offset)
    bucket = jnp.zeros(offset.shape, jnp.int32)
    for border in BUCKET_EDGES:
        bucket = bucket + (distance >= border).astype(jnp.int32)
    return bucket + total // 2 * (offset > 0).astype(jnp.int32)


def iota(shape, axis):
    return lax.broadcasted_iota(jnp.int32, shape, axis)


class LateRef:
    def __init__(self, source, target, sem):
        self.copy = pltpu.make_async_copy(source, target, sem)
        self.target = target
        self.shape = target.shape
        self.pending = True
        self.copy.start()

    def wait(self):
        if self.pending:
            self.copy.wait()
            self.pending = False

    def __getitem__(self, index):
        self.wait()
        return self.target[index]


def kernel_call(body, outs, *args, scalars=0, late=(), limit=VMEM_BYTES, held=()):
    count = len(args)
    late = sorted(late)

    def run(*refs):
        ins = list(refs[:count])
        out_refs = refs[count : count + len(outs)]
        scratch = refs[count + len(outs) :]
        for n, i in enumerate(late):
            ins[i] = LateRef(ins[i], scratch[n], scratch[-1].at[n])
        body(*ins, *out_refs, *scratch[len(late) : len(late) + len(held)])
        for i in late:
            ins[i].wait()

    spaces = [pltpu.SMEM if i < scalars else pltpu.VMEM for i in range(count)]
    for i in late:
        spaces[i] = pltpu.HBM
    scratch = [pltpu.VMEM(args[i].shape, args[i].dtype) for i in late]
    scratch += [pltpu.VMEM(shape, dtype) for shape, dtype in held]
    if late:
        scratch.append(pltpu.SemaphoreType.DMA((len(late),)))
    return pl.pallas_call(
        run,
        out_shape=[jax.ShapeDtypeStruct(shape, dtype) for shape, dtype in outs],
        in_specs=[pl.BlockSpec(memory_space=space) for space in spaces],
        out_specs=[pl.BlockSpec(memory_space=pltpu.VMEM)] * len(outs),
        scratch_shapes=scratch,
        compiler_params=pltpu.CompilerParams(vmem_limit_bytes=limit),
        cost_estimate=pl.CostEstimate(
            flops=1_000_000, bytes_accessed=1_000_000, transcendentals=0
        ),
    )(*args)


def choose(index, values):
    picked = values[0]
    for i in range(1, len(values)):
        picked = jnp.where(index == i, values[i], picked)
    return picked


def pack_weights(group_ref, q_ref, k_ref, v_ref, router_ref, one_ref, two_ref, wout_ref, docs_ref,
                 *refs):
    keep_ref, *out_refs = refs
    rows, width = q_ref.shape
    experts = router_ref.shape[0]
    cols = width // 4
    eye = iota((rows, rows), 0) == iota((rows, rows), 1)
    router = dot(eye.astype(F32).astype(BF16), router_ref[...], ((1,), (1,)))
    columns = [
        jnp.sum(jnp.where(eye, ref[...].astype(F32), 0.0), axis=1, keepdims=True)
        for ref in (one_ref, two_ref)
    ]
    docs = docs_ref[...].astype(F32)
    length = docs.shape[1]
    doc_cols = -(-length // rows)
    for t in range(doc_cols):
        belongs = iota((rows, length), 1) == iota((rows, length), 0) * doc_cols + t
        columns.append(jnp.sum(jnp.where(belongs, docs, 0.0), axis=1, keepdims=True))
    pad = out_refs[0].shape[1] - 3 * cols - experts - 2 - doc_cols
    small = jnp.concatenate(
        [router] + columns + [jnp.zeros((rows, pad), F32)], axis=1
    ).astype(BF16)
    weights = [ref[...] for ref in (q_ref, k_ref, v_ref)]
    pieces = [
        jnp.concatenate([w[:, j * cols : (j + 1) * cols] for w in weights] + [small], axis=1)
        for j in range(4)
    ]
    for d, out_ref in zip(ORDER, out_refs):
        out_ref[...] = choose(group_ref[0] ^ d, pieces)
    used = pieces[0].shape[1]
    keep_ref[:, :used] = choose(group_ref[0], pieces)
    keep_ref[:, used:] = wout_ref[...]


def put_rows(ref, dest, value):
    rows, width = value.shape
    wide = ref.shape[2]
    ref[dest, 4 * rows :, : min(wide, width)] = value[:, :wide]
    if wide > width:
        ref[dest, 4 * rows :, width:] = jnp.zeros((rows, wide - width), BF16)


def spare_lanes(value, wide):
    over = (value.shape[1] - wide) // 4
    return jnp.concatenate(
        [value[:, wide + j * over : wide + (j + 1) * over] for j in range(4)], axis=0
    )


def take_rows(held, rows, width):
    wide = held.shape[1]
    if wide >= width:
        return held[4 * rows :, :width]
    over = (width - wide) // 4
    tail = [held[j * rows : (j + 1) * rows, wide - over :] for j in range(4)]
    return jnp.concatenate([held[4 * rows :]] + tail, axis=1)


def spread_weights(group_ref, own_ref, p3_ref, p1_ref, p2_ref, out_ref):
    dests, _, wide = out_ref.shape
    rows, used = p1_ref.shape
    pieces = [own_ref[:, :used]] + [ref[...] for ref in (p1_ref, p2_ref, p3_ref)]
    value = jnp.concatenate([choose(group_ref[0] ^ j, pieces) for j in range(4)], axis=0)
    if wide > used:
        value = jnp.concatenate([value, jnp.zeros((4 * rows, wide - used), BF16)], axis=1)
    last = own_ref[:, used:]
    if wide < last.shape[1]:
        spare = spare_lanes(last, wide)
        value = jnp.concatenate([value[:, : wide - spare.shape[1]], spare], axis=1)
    for dest in range(dests):
        out_ref[dest, : 4 * rows] = value
        put_rows(out_ref, dest, last)


def prepare(capacity, pad, group_ref, table_ref, routes_ref, vector_ref, spread_ref, later_ref,
            gather_ref, send_ref):
    buckets = table_ref.shape[0]
    own_heads, length = vector_ref.shape
    toks = length // 2
    group = group_ref[0]
    spot = iota((1, length), 1)
    offset = jnp.where(spot >= toks, spot - length, spot)
    bucket = bucket_of(offset, buckets)
    for h in range(own_heads):
        vector = jnp.zeros((1, length), F32)
        for b in range(buckets):
            vector = jnp.where(bucket == b, table_ref[b, group * own_heads + h], vector)
        vector_ref[h : h + 1] = vector
    experts = gather_ref.shape[1]
    route = routes_ref[...]
    chosen = route == iota((toks, experts), 1)
    gather_ref[...] = chosen.astype(F32)
    lower = (iota((toks, toks), 0) > iota((toks, toks), 1)).astype(BF16)
    counts = dot(lower, chosen.astype(BF16))
    slot = jnp.sum(jnp.where(chosen, counts, 0.0), axis=1, keepdims=True).astype(jnp.int32)
    across = iota((toks, experts * pad), 1)
    for i in range(4):
        place = jnp.where(slot < capacity, route * pad + i * capacity + slot, -1)
        spread = (place == across).astype(F32)
        target = (spread_ref, later_ref)[i % 2]
        target[i // 2] = spread.astype(BF16)
        send_ref[:, i * toks : (i + 1) * toks] = jnp.transpose(spread).astype(BF16)


def place_weights(arrived_ref, w_ref, wout_ref):
    sources = arrived_ref.shape[0]
    rows = wout_ref.shape[0] // sources
    used = w_ref.shape[1]
    width = wout_ref.shape[1]
    block = sources * rows
    for s in range(sources):
        for j in range(4):
            w_ref[j * block + s * rows : j * block + (s + 1) * rows] = arrived_ref[
                s, j * rows : (j + 1) * rows, :used
            ]
        wout_ref[s * rows : (s + 1) * rows] = take_rows(arrived_ref[s], rows, width)


def gain_rows(experts, cols, w_ref, gains_ref):
    small = w_ref[:, 3 * cols :]
    pick = (iota((8, small.shape[1]), 1) == iota((8, small.shape[1]), 0) + experts).astype(BF16)
    gains_ref[...] = dot(pick, small, ((1,), (1,)))


def attend(scale, head_dim, docs, group_ref, w_ref, wout_ref, gains_ref, own_ref, across_ref,
           vector_ref, qkv_ref, probs_ref, att_ref, keep_ref, send_ref):
    own_heads, length = vector_ref.shape
    cols = own_heads * head_dim
    toks = own_ref.shape[0]
    vectors = vector_ref[...]
    turned = jnp.concatenate([docs[:, toks:], docs[:, :toks]], axis=1)
    across = jnp.broadcast_to(jnp.where(group_ref[0] < 2, docs, turned), (length, length))
    same = across == jnp.transpose(across)
    x = jnp.concatenate([own_ref[...], across_ref[...]], axis=0).astype(F32)
    normed = (x * rms_inverse(x) * gains_ref[0:1]).astype(BF16)
    qkv = dot(normed, w_ref[:, : 3 * cols]).astype(BF16)
    qkv_ref[...] = qkv
    parts = []
    for h in range(own_heads):
        at = h * head_dim
        q = qkv[:, at : at + head_dim]
        k = qkv[:, cols + at : cols + at + head_dim]
        v = qkv[:, 2 * cols + at : 2 * cols + at + head_dim]
        full = jnp.broadcast_to(vectors[h : h + 1], (length, length))
        bias = pltpu.roll(full, 0, 1, stride=1, stride_axis=0)
        scores = jnp.where(same, dot(q, k, ((1,), (1,))) * scale + bias, MASKED)
        top = jnp.max(scores, axis=1, keepdims=True)
        raised = jnp.exp(scores - top)
        probs = raised * (1.0 / jnp.sum(raised, axis=1, keepdims=True))
        probs_ref[h] = probs
        parts.append(dot(probs.astype(BF16), v))
    attended = jnp.concatenate(parts, axis=1).astype(BF16)
    att_ref[...] = attended
    partial = dot(attended, wout_ref[...])
    keep_ref[...] = partial[:toks]
    send_ref[...] = partial[toks:].astype(BF16)


def docs_of_pair(at, length, rows, group_ref, place_ref, arrived_ref):
    sources = arrived_ref.shape[0]
    doc_cols = -(-length // rows)
    held = arrived_ref[(place_ref[0] % sources) ^ (sources // 2)]
    blocks = [held[j * rows : (j + 1) * rows, at : at + doc_cols].astype(F32) for j in range(4)]
    block = choose(group_ref[0] ^ 1, blocks)
    docs = jnp.zeros((1, length), F32)
    for t in range(doc_cols):
        belongs = iota((rows, length), 1) == iota((rows, length), 0) * doc_cols + t
        docs = docs + jnp.sum(jnp.where(belongs, block[:, t : t + 1], 0.0), axis=0, keepdims=True)
    return docs


def attend_own(scale, head_dim, group_ref, docs_ref, *refs):
    attend(scale, head_dim, docs_ref[...].astype(F32), group_ref, *refs)


def attend_first(scale, head_dim, experts, group_ref, place_ref, arrived_ref, own_ref, across_ref,
                 vector_ref, w_ref, wout_ref, gains_ref, *outs):
    place_weights(arrived_ref, w_ref, wout_ref)
    cols = wout_ref.shape[0]
    gain_rows(experts, cols, w_ref, gains_ref)
    docs = docs_of_pair(
        3 * cols + experts + 2, vector_ref.shape[1], cols // arrived_ref.shape[0], group_ref, place_ref,
        arrived_ref,
    )
    attend(scale, head_dim, docs, group_ref, w_ref, wout_ref, gains_ref, own_ref, across_ref,
           vector_ref, *outs)


def attend_first_placed(scale, head_dim, experts, group_ref, place_ref, arrived_ref, w_ref, wout_ref,
                        own_ref, across_ref, vector_ref, gains_ref, *outs):
    cols = wout_ref.shape[0]
    gain_rows(experts, cols, w_ref, gains_ref)
    docs = docs_of_pair(
        3 * cols + experts + 2, vector_ref.shape[1], cols // arrived_ref.shape[0], group_ref, place_ref,
        arrived_ref,
    )
    attend(scale, head_dim, docs, group_ref, w_ref, wout_ref, gains_ref, own_ref, across_ref,
           vector_ref, *outs)


def route_tokens(x_ref, keep_ref, core_ref, came_ref, gains_ref, w_ref, chosen_ref, send_ref,
                 g_ref, middle_ref, gate_ref, out_ref):
    middle = x_ref[...].astype(F32) + (
        (keep_ref[...] + core_ref[...].astype(F32)) + came_ref[...].astype(F32)
    )
    middle_ref[...] = middle
    normed = (middle * rms_inverse(middle) * gains_ref[1:2]).astype(BF16)
    g = g_ref[...]
    half = g.shape[1] // 2
    both = jnp.concatenate([normed[:, :half], g[:, :half], normed[:, half:], g[:, half:]], axis=0)
    out_ref[...] = dot(send_ref[...], both).astype(BF16)
    probs = jax.nn.softmax(dot(normed, w_ref[...]), axis=-1)
    gate_ref[...] = jnp.sum(probs * chosen_ref[...], axis=1, keepdims=True)


def run_expert(capacity, place_ref, own_ref, other_ref, router_ref, inner_ref, outer_ref, buf_ref,
               dslot_ref, g_ref, probs_ref, gate_ref, hidden_ref, dpre_ref, keep_ref, send_ref):
    slots = buf_ref.shape[0] // 2
    half = own_ref.shape[1]
    experts = router_ref.shape[1]
    pad = own_ref.shape[0] // (slots // capacity)
    shape = (4 * slots, own_ref.shape[0])
    row = iota(shape, 0)
    part = row // slots
    inside = row - part * slots
    source = inside // capacity
    wanted = source * pad + part * capacity + (inside - source * capacity)
    select = (iota(shape, 1) == wanted).astype(BF16)
    rows = dot(select, jnp.concatenate([own_ref[...], other_ref[...]], axis=1))
    mine = (iota((1, experts), 1) == place_ref[0]).astype(F32)
    for side in range(2):
        at = side * slots
        cut = rows[:, side * half : (side + 1) * half]
        buffers = jnp.concatenate([cut[:slots], cut[2 * slots : 3 * slots]], axis=1).astype(BF16)
        g = jnp.concatenate([cut[slots : 2 * slots], cut[3 * slots :]], axis=1)
        buf_ref[at : at + slots] = buffers
        probs = jax.nn.softmax(dot(buffers, router_ref[...]), axis=-1)
        gate = jnp.sum(probs * mine, axis=1, keepdims=True)
        dslot_ref[at : at + slots] = (gate * g).astype(BF16)
        if side == 0:
            g_ref[...] = g.astype(BF16)
            probs_ref[...] = probs
            gate_ref[...] = gate
    inner = inner_ref[...]
    outer = outer_ref[...]
    pre = dot(buf_ref[...], inner)
    cdf = 0.5 * (1.0 + lax.erf(pre * (0.5**0.5)))
    hidden = (pre * cdf).astype(BF16)
    hidden_ref[...] = hidden
    slope = cdf + pre * jnp.exp(-0.5 * pre * pre) * 0.3989422804014327
    dpre = (dot(dslot_ref[...], outer, ((1,), (1,))) * slope).astype(BF16)
    dpre_ref[...] = dpre
    result = dot(hidden, outer)
    keep_ref[0] = result[:slots]
    send_ref[0] = result[slots:].astype(BF16)
    back = dot(dpre, inner, ((1,), (1,)))
    keep_ref[1] = back[:slots]
    send_ref[1] = back[slots:].astype(BF16)


def finish_expert(capacity, place_ref, keep_ref, came_ref, buf_ref, g_ref, probs_ref, gate_ref,
                  router_ref, out_ref, grad_ref):
    slots = g_ref.shape[0]
    experts = router_ref.shape[1]
    pad = out_ref.shape[0] // (slots // capacity)
    total = (keep_ref[...] + came_ref[...].astype(F32)).astype(BF16)
    result = total[0]
    mine = (iota((1, experts), 1) == place_ref[0]).astype(F32)
    grad_gate = jnp.sum(g_ref[...].astype(F32) * result.astype(F32), axis=1, keepdims=True)
    grad_logits = (grad_gate * gate_ref[...] * (mine - probs_ref[...])).astype(BF16)
    grad_ref[...] = dot(buf_ref[...], grad_logits, ((0,), (0,))).astype(BF16)
    back = total[1].astype(F32) + dot(grad_logits, router_ref[...], ((1,), (1,)))
    shape = (out_ref.shape[0], 4 * slots)
    row = iota(shape, 0)
    source = row // pad
    inside = row - source * pad
    part = inside // capacity
    wanted = jnp.where(part < 4, part * slots + source * capacity + inside - part * capacity, -1)
    expand = (iota(shape, 1) == wanted).astype(BF16)
    back = back.astype(BF16)
    half = back.shape[1] // 2
    both = jnp.concatenate([back[:, :half], result[:, :half], back[:, half:], result[:, half:]], axis=0)
    out_ref[...] = dot(expand, both).astype(BF16)


def middle_backward(back_ref, spread_ref, middle_ref, gains_ref, g_ref):
    middle = middle_ref[...]
    inverse = rms_inverse(middle)
    unit = middle * inverse
    rows = back_ref[...]
    grad_normed = jnp.concatenate([dot(spread_ref[i], rows) for i in range(2)], axis=1)
    dmiddle = g_ref[...].astype(F32) + norm_backward(grad_normed, unit, inverse, gains_ref[1:2])
    return dmiddle, grad_normed * unit


def norm_two_backward(back_ref, spread_ref, middle_ref, gains_ref, g_ref, da_ref, gain_ref):
    dmiddle, scaled = middle_backward(back_ref, spread_ref, middle_ref, gains_ref, g_ref)
    gain_ref[...] = jnp.sum(scaled, axis=0, keepdims=True)
    da_ref[...] = dmiddle.astype(BF16)


def finish_layer(back_ref, spread_ref, later_ref, middle_ref, gains_ref, g_ref, gate_ref, out_ref,
                 dmiddle_ref):
    rows = back_ref[...]
    combined = jnp.concatenate([dot(later_ref[i], rows) for i in range(2)], axis=1)
    out_ref[...] = (middle_ref[...] + gate_ref[...] * combined).astype(BF16)
    dmiddle_ref[...] = middle_backward(back_ref, spread_ref, middle_ref, gains_ref, g_ref)[0]


def attend_backward(scale, head_dim, own_ref, across_ref, wout_ref, qkv_ref, probs_ref, gains_ref,
                    w_ref, x_own_ref, x_across_ref, keep_ref, send_ref, grad_ref, gain_ref,
                    offsets_ref):
    own_heads = probs_ref.shape[0]
    cols = own_heads * head_dim
    toks = own_ref.shape[0]
    length = 2 * toks
    flip = (iota((length, length), 0) + iota((length, length), 1) == length - 1).astype(BF16)
    da = jnp.concatenate([own_ref[...], across_ref[...]], axis=0)
    grad_att = dot(da, wout_ref[...], ((1,), (1,))).astype(BF16)
    qkv = qkv_ref[...]
    parts = [[], [], []]
    for h in range(own_heads):
        at = h * head_dim
        q = qkv[:, at : at + head_dim]
        k = qkv[:, cols + at : cols + at + head_dim]
        v = qkv[:, 2 * cols + at : 2 * cols + at + head_dim]
        gh = grad_att[:, at : at + head_dim]
        probs = probs_ref[h]
        grad_probs = dot(gh, v, ((1,), (1,)))
        row_dot = jnp.sum(probs * grad_probs, axis=1, keepdims=True)
        ds = (probs * (grad_probs - row_dot)).astype(BF16)
        turned = pltpu.roll(dot(flip, ds), 1, 1, stride=1, stride_axis=0)
        offsets_ref[h : h + 1] = jnp.sum(turned, axis=0, keepdims=True)
        parts[0].append(dot(ds, k) * scale)
        parts[1].append(dot(ds, q, ((0,), (0,))) * scale)
        parts[2].append(dot(probs.astype(BF16), gh, ((0,), (0,))))
    grad_qkv = jnp.concatenate(parts[0] + parts[1] + parts[2], axis=1).astype(BF16)
    grad_ref[...] = grad_qkv
    grad_normed = dot(grad_qkv, w_ref[:, : 3 * cols], ((1,), (1,)))
    keep_ref[...] = grad_normed[:toks]
    send_ref[...] = grad_normed[toks:].astype(BF16)
    x = jnp.concatenate([x_own_ref[...], x_across_ref[...]], axis=0).astype(F32)
    gain_ref[...] = jnp.sum(grad_normed * (x * rms_inverse(x)), axis=0, keepdims=True)


def row_weights(own_ref, across_ref, att_ref, grad_ref, gains_ref, x_own_ref, x_across_ref):
    x = jnp.concatenate([x_own_ref[...], x_across_ref[...]], axis=0).astype(F32)
    normed = (x * rms_inverse(x) * gains_ref[0:1]).astype(BF16)
    da = jnp.concatenate([own_ref[...], across_ref[...]], axis=0)
    weights = dot(normed, grad_ref[...], ((0,), (0,)))
    return weights, dot(att_ref[...], da, ((0,), (0,)))


def backward_own(scale, head_dim, own_ref, across_ref, wout_ref, att_ref, qkv_ref, probs_ref,
                 gains_ref, w_ref, x_own_ref, x_across_ref, gw_ref, gout_ref, keep_ref, send_ref,
                 grad_ref, gain_ref, offsets_ref):
    attend_backward(
        scale, head_dim, own_ref, across_ref, wout_ref, qkv_ref, probs_ref, gains_ref, w_ref,
        x_own_ref, x_across_ref, keep_ref, send_ref, grad_ref, gain_ref, offsets_ref,
    )
    gw_ref[...], gout_ref[...] = row_weights(
        own_ref, across_ref, att_ref, grad_ref, gains_ref, x_own_ref, x_across_ref
    )


def sum_weights(packed, buckets, table_cols, *refs):
    gw_ref, gout_ref, own_gain_ref, own_offsets_ref, gain_ref, offsets_ref = refs[7:13]
    gain_two_ref, router_ref, full_ref, out_ref = refs[13:]
    weights, outs = row_weights(*refs[:7])
    own_heads, length = offsets_ref.shape
    width, experts = router_ref.shape
    toks = length // 2
    rows = own_heads * buckets // table_cols
    spot = iota((1, length), 1)
    offset = jnp.where(spot >= toks, spot - length, spot)
    bucket = bucket_of(offset, buckets)
    table = []
    for t in range(table_cols):
        column = jnp.zeros((rows, 1), F32)
        for h in range(own_heads):
            belongs = iota((rows, length), 0) * table_cols + t == bucket * own_heads + h
            value = own_offsets_ref[h : h + 1] + offsets_ref[h : h + 1]
            column = column + jnp.sum(jnp.where(belongs, value, 0.0), axis=1, keepdims=True)
        table.append(column)
    table = jnp.concatenate([jnp.concatenate(table, axis=1)] * (width // rows), axis=0)
    narrow = jnp.concatenate(
        [own_gain_ref[...] + gain_ref[...], gain_two_ref[...], jnp.zeros((6, width), F32)], axis=0
    )
    narrow = jnp.transpose(narrow)[:, :2]
    weights = weights + gw_ref[...]
    pieces = [weights, router_ref[...].astype(F32), narrow, table]
    outs = outs + gout_ref[...]
    out_ref[...] = outs.astype(BF16)
    used = full_ref.shape[1]
    tail = [spare_lanes(outs, used)] if packed else []
    spare = used - sum(p.shape[1] for p in pieces + tail)
    if spare:
        tail.insert(0, jnp.zeros((width, spare), F32))
    full_ref[...] = jnp.concatenate(pieces + tail, axis=1).astype(BF16)


def sum_weights_message(packed, buckets, table_cols, *refs):
    *rest, message_ref, full_ref, out_ref = refs
    sum_weights(packed, buckets, table_cols, *rest, full_ref, out_ref)
    dests, _, wide = message_ref.shape
    rows = out_ref.shape[0] // dests
    used = full_ref.shape[1]
    block = dests * rows
    for s in range(dests):
        for j in range(4):
            at = j * block + s * rows
            message_ref[s, j * rows : (j + 1) * rows, :used] = full_ref[at : at + rows]
            if wide > used:
                message_ref[s, j * rows : (j + 1) * rows, used:] = jnp.zeros(
                    (rows, wide - used), BF16
                )
        put_rows(message_ref, s, out_ref[s * rows : (s + 1) * rows])


def sum_arrived(group_ref, arrived_ref, out_ref, own_ref, *send_refs):
    rows, used = own_ref.shape
    total = arrived_ref[0].astype(F32)
    for s in range(1, arrived_ref.shape[0]):
        total = total + arrived_ref[s].astype(F32)
    out_ref[...] = take_rows(total, rows, out_ref.shape[1])
    pieces = [total[j * rows : (j + 1) * rows, :used] for j in range(4)]
    own_ref[...] = choose(group_ref[0], pieces)
    for d, ref in zip(ORDER, send_refs):
        ref[...] = choose(group_ref[0] ^ d, pieces).astype(BF16)


def finish_input(grad_ref, core_ref, came_ref, dmiddle_ref, x_ref, gains_ref, out_ref):
    x = x_ref[...].astype(F32)
    inverse = rms_inverse(x)
    grad_normed = grad_ref[...] + core_ref[...].astype(F32) + came_ref[...].astype(F32)
    out_ref[...] = (
        dmiddle_ref[...] + norm_backward(grad_normed, x * inverse, inverse, gains_ref[0:1])
    ).astype(BF16)


def finish_weights(own_heads, buckets, table_cols, group_ref, p0_ref, p3_ref, p1_ref, p2_ref,
                   q_ref, k_ref, v_ref, router_ref, one_ref, two_ref, table_ref):
    rows, width = q_ref.shape
    experts = router_ref.shape[0]
    cols = width // 4
    pieces = [ref[...].astype(F32) for ref in (p0_ref, p1_ref, p2_ref, p3_ref)]
    ordered = [choose(group_ref[0] ^ j, pieces) for j in range(4)]
    for n, ref in enumerate((q_ref, k_ref, v_ref)):
        ref[...] = jnp.concatenate([p[:, n * cols : (n + 1) * cols] for p in ordered], axis=1)
    at = 3 * cols
    small = sum(p[:, at : at + experts + 2] for p in pieces)
    square = -(-max(rows, experts) // 128) * 128
    padded = small[:, :experts]
    if square > experts:
        padded = jnp.concatenate([padded, jnp.zeros((rows, square - experts), F32)], axis=1)
    padded = jnp.concatenate([padded, jnp.zeros((square - rows, square), F32)], axis=0)
    router_ref[...] = jnp.transpose(padded)[:experts, :rows]
    eye = iota((rows, rows), 0) == iota((rows, rows), 1)
    for i, ref in enumerate((one_ref, two_ref)):
        column = small[:, experts + i : experts + i + 1]
        ref[...] = jnp.sum(jnp.where(eye, column, 0.0), axis=0, keepdims=True)
    at += experts + 2
    lines = []
    lane = iota((rows, 128), 1)
    for p in ordered:
        for h in range(own_heads):
            line = jnp.zeros((1, 128), F32)
            for t in range(table_cols):
                belongs = iota((rows, 128), 0) * table_cols + t == lane * own_heads + h
                value = jnp.where(belongs & (lane < buckets), p[:, at + t : at + t + 1], 0.0)
                line = line + jnp.sum(value, axis=0, keepdims=True)
            lines.append(line)
    table_ref[...] = jnp.concatenate(lines, axis=0)[:, :buckets]


def local(
    tokens,
    gain_one,
    w_query,
    w_key,
    w_value,
    w_out,
    bias_table,
    gain_two,
    w_router,
    w_inner,
    w_outer,
    segment_ids,
    routes,
    out_grad,
):
    toks = tokens.shape[1]
    width = tokens.shape[2]
    heads = bias_table.shape[1]
    buckets = bias_table.shape[0]
    head_dim = width // heads
    own_heads = heads // 4
    cols = own_heads * head_dim
    length = 2 * toks
    scale = head_dim ** (-0.5)
    sources = lax.axis_size("expert")
    experts = sources
    capacity = (5 * toks + 4 * experts - 1) // (4 * experts)
    slots = experts * capacity
    pad = -(-4 * capacity // 8) * 8
    rows = w_query.shape[0]
    core = lax.axis_index("dp")
    place = lax.axis_index("expert")
    half = sources // 2
    member = place // half
    first_core = core == 0
    place_at = place.reshape(1).astype(jnp.int32)
    group_at = (2 * core + member).reshape(1).astype(jnp.int32)
    table_cols = max(1, own_heads * buckets // rows)
    extra = max(table_cols, -(-length // rows))
    used = -(-(3 * cols + experts + 2 + extra) // 128) * 128
    aligned = rows % 8 == 0
    room = used - (3 * cols + experts + 2 + extra)
    packed = aligned and used < width <= used + 4 * room and (width - used) % 4 == 0
    wide = used if packed else max(used, width)

    def across_group(pieces):
        return [
            lax.ppermute(
                piece,
                ("dp", "expert"),
                [
                    (c * sources + e, (c ^ (d >> 1)) * sources + (e ^ (half * (d & 1))))
                    for c in range(2)
                    for e in range(sources)
                ],
            )
            for d, piece in zip(ORDER, pieces)
        ]

    own_tokens = tokens.reshape(toks, width)
    pair_tokens = swap_pair(own_tokens)

    own_piece, *pieces = kernel_call(
        pack_weights, [((rows, used + width), BF16)] + [((rows, used), BF16)] * 3,
        group_at, w_query, w_key, w_value, w_router.T, gain_one.reshape(1, rows),
        gain_two.reshape(1, rows), w_out, segment_ids, scalars=1, late=range(1, 9),
        limit=60 * 1024 * 1024,
    )
    pieces = across_group(pieces)
    pair_tokens, own_piece, *pieces = lax.optimization_barrier((pair_tokens, own_piece, *pieces))
    (message,) = kernel_call(
        spread_weights, [((half, 5 * rows, wide), BF16)],
        group_at, own_piece, *pieces, scalars=1,
    )
    arrived = exchange_half(message)

    own_across = swap_core(own_tokens)
    pair_across = swap_core(pair_tokens)
    vectors, spread, later, chosen, send = kernel_call(
        functools.partial(prepare, capacity, pad),
        [
            ((own_heads, length), F32),
            ((2, toks, experts * pad), BF16),
            ((2, toks, experts * pad), BF16),
            ((toks, experts), F32),
            ((experts * pad, 4 * toks), BF16),
        ],
        group_at, bias_table, routes.reshape(toks, 1), scalars=2,
    )
    g_low = out_grad.reshape(toks, width)

    row_outs = [
        ((length, 3 * cols), BF16),
        ((own_heads, length, length), F32),
        ((length, cols), BF16),
        ((toks, width), F32),
        ((toks, width), BF16),
    ]
    placed = [((width, used), BF16), ((cols, width), BF16)]
    if aligned:
        weights, out_w, gains, *pair_kept = kernel_call(
            functools.partial(attend_first, scale, head_dim, experts),
            placed + [((8, width), F32)] + row_outs,
            group_at, place_at, arrived, pair_tokens, pair_across, vectors, scalars=2,
        )
    else:
        weights = arrived[:, : 4 * rows, :used].reshape(half, 2, 2, rows, used)
        weights = weights.transpose(1, 2, 0, 3, 4).reshape(width, used)
        out_w = arrived[:, 4 * rows :, :width].reshape(cols, width)
        gains, *pair_kept = kernel_call(
            functools.partial(attend_first_placed, scale, head_dim, experts),
            [((8, width), F32)] + row_outs,
            group_at, place_at, arrived, weights, out_w, pair_tokens, pair_across, vectors, scalars=2,
        )
    pair_qkv, pair_probs, pair_att, keep, away = pair_kept
    pair_sum = (keep + swap_core(away).astype(F32)).astype(BF16)
    pair_sum, out_w, gains = lax.optimization_barrier((pair_sum, out_w, gains))
    pair_sum = swap_pair(pair_sum)
    own_qkv, own_probs, own_att, keep, away = kernel_call(
        functools.partial(attend_own, scale, head_dim), row_outs,
        group_at, segment_ids, weights, out_w, gains, own_tokens, own_across, vectors, scalars=1,
    )
    router_w = weights[:, 3 * cols : 3 * cols + experts]
    middle, gate, outgoing = kernel_call(
        route_tokens,
        [((toks, width), F32), ((toks, 1), F32), ((experts * pad, width // 2), BF16)],
        own_tokens, keep, swap_core(away), pair_sum, gains, router_w, chosen, send, g_low,
    )
    incoming = exchange(outgoing.reshape(experts, pad, width // 2)).reshape(-1, width // 2)

    inner, outer = w_inner[0], w_outer[0]
    units = inner.shape[1]
    buffers, dslot, slot_g, slot_probs, slot_gate, hidden, dpre, keep, away = kernel_call(
        functools.partial(run_expert, capacity),
        [
            ((2 * slots, width), BF16),
            ((2 * slots, width), BF16),
            ((slots, width), BF16),
            ((slots, experts), F32),
            ((slots, 1), F32),
            ((2 * slots, units), BF16),
            ((2 * slots, units), BF16),
            ((2, slots, width), F32),
            ((2, slots, width), BF16),
        ],
        place_at, incoming, swap_core(incoming), router_w, inner, outer, scalars=1,
    )
    grad_outer = dot(hidden, dslot, ((0,), (0,)))
    grad_inner = dot(buffers, dpre, ((0,), (0,)))
    back, grad_router = kernel_call(
        functools.partial(finish_expert, capacity),
        [((sources * pad, width // 2), BF16), ((width, experts), BF16)],
        place_at, keep, swap_core(away), buffers[:slots], slot_g, slot_probs, slot_gate, router_w,
        scalars=1,
    )
    back = exchange(back.reshape(sources, pad, width // 2)).reshape(-1, width // 2)

    grad_attn, grad_gain_two = kernel_call(
        norm_two_backward, [((toks, width), BF16), ((1, width), F32)],
        back, spread, middle, gains, g_low,
    )
    pair_grad = swap_pair(grad_attn)
    shared = (gains, weights)
    back_outs = [
        ((toks, width), F32),
        ((toks, width), BF16),
        ((length, 3 * cols), BF16),
        ((1, width), F32),
        ((own_heads, length), F32),
    ]
    grad_w, grad_out, grad_normed, away, _, own_gain, own_offsets = kernel_call(
        functools.partial(backward_own, scale, head_dim),
        [((width, 3 * cols), F32), ((cols, width), F32)] + back_outs,
        grad_attn, swap_core(grad_attn), out_w, own_att, own_qkv, own_probs, *shared,
        own_tokens, own_across,
    )
    pair_grad, grad_w, own_away = lax.optimization_barrier((pair_grad, grad_w, away))
    own_came = swap_core(own_away)
    pair_grads = (pair_grad, swap_core(pair_grad))
    keep, away, grad_qkv, pair_gain, pair_offsets = kernel_call(
        functools.partial(attend_backward, scale, head_dim), back_outs,
        *pair_grads, out_w, pair_qkv, pair_probs, *shared, pair_tokens, pair_across,
    )
    to_pair = (keep + swap_core(away).astype(F32)).astype(BF16)
    last = (
        *pair_grads, pair_att, grad_qkv, gains, pair_tokens, pair_across, grad_w, grad_out,
        own_gain, own_offsets, pair_gain, pair_offsets, grad_gain_two, grad_router,
    )
    flat = [((width, used), BF16), ((cols, width), BF16)]
    if aligned:
        (message,) = kernel_call(
            functools.partial(sum_weights_message, packed, buckets, table_cols),
            [((half, 5 * rows, wide), BF16)], *last, held=flat,
        )
    else:
        full, grad_out = kernel_call(
            functools.partial(sum_weights, packed, buckets, table_cols), flat, *last
        )
        full = full.reshape(2, 2, half, rows, used).transpose(2, 0, 1, 3, 4)
        full = full.reshape(half, 4 * rows, used)
        grad_out = grad_out.reshape(half, rows, width)
        message = jnp.concatenate(
            [
                jnp.pad(full, ((0, 0), (0, 0), (0, wide - used))),
                jnp.pad(grad_out, ((0, 0), (0, 0), (0, wide - width))),
            ],
            axis=1,
        )
    came = swap_pair(to_pair)
    arrived = exchange_half(message)
    final, grad_middle = kernel_call(
        finish_layer, [((toks, width), BF16), ((toks, width), F32)],
        back, spread, later, middle, gains, g_low, gate,
    )

    arrived, grad_inner, grad_outer, final, grad_middle = lax.optimization_barrier(
        (arrived, grad_inner, grad_outer, final, grad_middle)
    )

    out_grad_w, own_piece, *pieces = kernel_call(
        sum_arrived, [((rows, width), F32), ((rows, used), F32)] + [((rows, used), BF16)] * 3,
        group_at, arrived, scalars=1,
    )
    pieces = across_group(pieces)
    query_grad, key_grad, value_grad, router_grad, one_grad, two_grad, table_grad = kernel_call(
        functools.partial(finish_weights, own_heads, buckets, table_cols),
        [((rows, width), F32)] * 3
        + [((experts, rows), F32), ((1, rows), F32), ((1, rows), F32), ((heads, buckets), F32)],
        group_at, own_piece, *pieces, scalars=1,
    )

    (grad_input,) = kernel_call(
        finish_input, [((toks, width), BF16)],
        grad_normed, own_came, came, grad_middle, own_tokens, gains,
    )
    return (
        final.reshape(tokens.shape),
        grad_input.reshape(tokens.shape),
        one_grad.reshape(rows),
        query_grad,
        key_grad,
        value_grad,
        out_grad_w,
        table_grad.T,
        two_grad.reshape(rows),
        router_grad.T,
        grad_inner[None],
        grad_outer[None],
    )


def solution(mesh):
    both = ("dp", "expert")
    return jax.shard_map(
        local,
        mesh=mesh,
        in_specs=(
            P("expert", "dp", None),
            P(both),
            P(both, None),
            P(both, None),
            P(both, None),
            P(both, None),
            P(),
            P(both),
            P(both, None),
            P("expert", None, "dp"),
            P("expert", "dp", None),
            P("expert", None),
            P("expert", "dp", None),
            P("expert", "dp", None),
        ),
        out_specs=(
            P("expert", "dp", None),
            P("expert", "dp", None),
            P(both),
            P(both, None),
            P(both, None),
            P(both, None),
            P(both, None),
            P(),
            P(both),
            P(both, None),
            P("expert", None, "dp"),
            P("expert", "dp", None),
        ),
        check_vma=False,
    )
```

```python
import functools

import jax
import jax.numpy as jnp
from jax import lax
from jax.experimental import pallas as pl
from jax.experimental.pallas import tpu as pltpu
from jax.sharding import PartitionSpec as P

EPSILON = 1e-06
MASKED = -1000000000.0
BUCKET_EDGES = (1, 2, 3, 4, 5, 6, 7, 8, 12, 16, 23, 32, 46, 64, 91)
F32 = jnp.float32
BF16 = jnp.bfloat16
ORDER = (3, 1, 2)
VMEM_BYTES = 24 * 1024 * 1024


def dot(left, right, dims=((1,), (0,))):
    return lax.dot_general(left, right, (dims, ((), ())), preferred_element_type=F32)


def rms_inverse(values):
    return lax.rsqrt(jnp.mean(values * values, axis=-1, keepdims=True) + EPSILON)


def norm_backward(grad_normed, unit_values, inverse, gain_values):
    grad_unit = grad_normed * gain_values
    projected = jnp.mean(grad_unit * unit_values, axis=-1, keepdims=True)
    return inverse * (grad_unit - unit_values * projected)


def swap_core(value):
    return lax.ppermute(value, "dp", [(0, 1), (1, 0)])


def swap_pair(value):
    n = lax.axis_size("expert")
    return lax.ppermute(value, "expert", [(i, i ^ 1) for i in range(n)])


def exchange(value):
    return lax.all_to_all(value, "expert", split_axis=0, concat_axis=0, tiled=True)


def exchange_half(value):
    half = lax.axis_size("expert") // 2
    groups = [[q * half + s for s in range(half)] for q in range(2)]
    return lax.all_to_all(
        value, "expert", split_axis=0, concat_axis=0, tiled=True, axis_index_groups=groups
    )


def bucket_of(offset, total):
    distance = jnp.abs(offset)
    bucket = jnp.zeros(offset.shape, jnp.int32)
    for border in BUCKET_EDGES:
        bucket = bucket + (distance >= border).astype(jnp.int32)
    return bucket + total // 2 * (offset > 0).astype(jnp.int32)


def iota(shape, axis):
    return lax.broadcasted_iota(jnp.int32, shape, axis)


class LateRef:
    def __init__(self, source, target, sem):
        self.copy = pltpu.make_async_copy(source, target, sem)
        self.target = target
        self.shape = target.shape
        self.pending = True
        self.copy.start()

    def wait(self):
        if self.pending:
            self.copy.wait()
            self.pending = False

    def __getitem__(self, index):
        self.wait()
        return self.target[index]


def kernel_call(body, outs, *args, scalars=0, late=(), limit=VMEM_BYTES, held=()):
    count = len(args)
    late = sorted(late)

    def run(*refs):
        ins = list(refs[:count])
        out_refs = refs[count : count + len(outs)]
        scratch = refs[count + len(outs) :]
        for n, i in enumerate(late):
            ins[i] = LateRef(ins[i], scratch[n], scratch[-1].at[n])
        body(*ins, *out_refs, *scratch[len(late) : len(late) + len(held)])
        for i in late:
            ins[i].wait()

    spaces = [pltpu.SMEM if i < scalars else pltpu.VMEM for i in range(count)]
    for i in late:
        spaces[i] = pltpu.HBM
    scratch = [pltpu.VMEM(args[i].shape, args[i].dtype) for i in late]
    scratch += [pltpu.VMEM(shape, dtype) for shape, dtype in held]
    if late:
        scratch.append(pltpu.SemaphoreType.DMA((len(late),)))
    return pl.pallas_call(
        run,
        out_shape=[jax.ShapeDtypeStruct(shape, dtype) for shape, dtype in outs],
        in_specs=[pl.BlockSpec(memory_space=space) for space in spaces],
        out_specs=[pl.BlockSpec(memory_space=pltpu.VMEM)] * len(outs),
        scratch_shapes=scratch,
        compiler_params=pltpu.CompilerParams(vmem_limit_bytes=limit),
        cost_estimate=pl.CostEstimate(
            flops=1_000_000, bytes_accessed=1_000_000, transcendentals=0
        ),
    )(*args)


def choose(index, values):
    picked = values[0]
    for i in range(1, len(values)):
        picked = jnp.where(index == i, values[i], picked)
    return picked


def pack_weights(group_ref, q_ref, k_ref, v_ref, router_ref, one_ref, two_ref, wout_ref, docs_ref,
                 *refs):
    keep_ref, *out_refs = refs
    first_core = group_ref[0] < 2
    rows, width = q_ref.shape
    experts = router_ref.shape[0]
    cols = width // 4
    eye = iota((rows, rows), 0) == iota((rows, rows), 1)
    router = dot(eye.astype(F32).astype(BF16), router_ref[...], ((1,), (1,)))
    columns = [
        jnp.sum(jnp.where(eye, ref[...].astype(F32), 0.0), axis=1, keepdims=True)
        for ref in (one_ref, two_ref)
    ]
    docs = docs_ref[...].astype(F32)
    length = docs.shape[1]
    doc_cols = -(-length // rows)
    for t in range(doc_cols):
        belongs = iota((rows, length), 1) == iota((rows, length), 0) * doc_cols + t
        columns.append(jnp.sum(jnp.where(belongs, docs, 0.0), axis=1, keepdims=True))
    pad = out_refs[0].shape[1] - 6 * cols - experts - 2 - doc_cols
    small = jnp.concatenate(
        [router] + columns + [jnp.zeros((rows, pad), F32)], axis=1
    ).astype(BF16)
    weights = [ref[...] for ref in (q_ref, k_ref, v_ref)]
    pieces = [
        jnp.concatenate(
            [w[:, j * cols : (j + 1) * cols] for j in (2 * c, 2 * c + 1) for w in weights] + [small],
            axis=1,
        )
        for c in range(2)
    ]
    here = jnp.where(first_core, pieces[0], pieces[1])
    there = jnp.where(first_core, pieces[1], pieces[0])
    held = small.shape[1] + 6 * cols
    for d, ref in zip((0, *ORDER), (keep_ref, *out_refs)):
        ref[:, :held] = there if d > 1 else here
        if d < 2:
            ref[:, held:] = wout_ref[...]


def put_rows(ref, dest, value):
    rows, width = value.shape
    wide = ref.shape[2]
    ref[dest, 4 * rows :, : min(wide, width)] = value[:, :wide]
    if wide > width:
        ref[dest, 4 * rows :, width:] = jnp.zeros((rows, wide - width), BF16)


def spare_lanes(value, wide):
    over = (value.shape[1] - wide) // 4
    return jnp.concatenate(
        [value[:, wide + j * over : wide + (j + 1) * over] for j in range(4)], axis=0
    )


def take_rows(held, rows, width):
    wide = held.shape[1]
    if wide >= width:
        return held[4 * rows :, :width]
    over = (width - wide) // 4
    tail = [held[j * rows : (j + 1) * rows, wide - over :] for j in range(4)]
    return jnp.concatenate([held[4 * rows :]] + tail, axis=1)


def spread_weights(cols, used, block_ref, own_ref, p3_ref, p1_ref, p2_ref, out_ref):
    dests, _, wide = out_ref.shape
    rows, held = p2_ref.shape
    block = block_ref[0]
    pieces = [ref[:, :held] for ref in (own_ref, p1_ref, p2_ref, p3_ref)]
    both = jnp.concatenate([choose(block ^ j, pieces) for j in range(4)], axis=0)
    lasts = [own_ref[:, held:], p1_ref[:, held:]]
    small = both[:, 6 * cols : 3 * cols + used]
    for variant in range(2):
        at = variant * 3 * cols
        value = jnp.concatenate([both[:, at : at + 3 * cols], small], axis=1)
        if wide > used:
            value = jnp.concatenate([value, jnp.zeros((4 * rows, wide - used), BF16)], axis=1)
        last = jnp.where(block % 2 == variant, lasts[0], lasts[1])
        if wide < last.shape[1]:
            spare = spare_lanes(last, wide)
            value = jnp.concatenate([value[:, : wide - spare.shape[1]], spare], axis=1)
        for dest in range(variant, dests, 2):
            out_ref[dest, : 4 * rows] = value
            put_rows(out_ref, dest, last)


def prepare(capacity, pad, group_ref, table_ref, routes_ref, vector_ref, spread_ref, later_ref,
            gather_ref, send_ref):
    buckets = table_ref.shape[0]
    own_heads, length = vector_ref.shape
    toks = length // 2
    group = group_ref[0]
    spot = iota((1, length), 1)
    offset = jnp.where(spot >= toks, spot - length, spot)
    bucket = bucket_of(offset, buckets)
    for h in range(own_heads):
        vector = jnp.zeros((1, length), F32)
        for b in range(buckets):
            vector = jnp.where(bucket == b, table_ref[b, group * own_heads + h], vector)
        vector_ref[h : h + 1] = vector
    experts = gather_ref.shape[1]
    route = routes_ref[...]
    chosen = route == iota((toks, experts), 1)
    gather_ref[...] = chosen.astype(F32)
    lower = (iota((toks, toks), 0) > iota((toks, toks), 1)).astype(BF16)
    counts = dot(lower, chosen.astype(BF16))
    slot = jnp.sum(jnp.where(chosen, counts, 0.0), axis=1, keepdims=True).astype(jnp.int32)
    across = iota((toks, experts * pad), 1)
    for i in range(4):
        place = jnp.where(slot < capacity, route * pad + i * capacity + slot, -1)
        spread = (place == across).astype(F32)
        target = (spread_ref, later_ref)[i % 2]
        target[i // 2] = spread.astype(BF16)
        send_ref[:, i * toks : (i + 1) * toks] = jnp.transpose(spread).astype(BF16)


def place_weights(arrived_ref, w_ref, wout_ref):
    sources = arrived_ref.shape[0]
    rows = wout_ref.shape[0] // sources
    used = w_ref.shape[1]
    width = wout_ref.shape[1]
    block = sources * rows
    for s in range(sources):
        for j in range(4):
            w_ref[j * block + s * rows : j * block + (s + 1) * rows] = arrived_ref[
                s, j * rows : (j + 1) * rows, :used
            ]
        wout_ref[s * rows : (s + 1) * rows] = take_rows(arrived_ref[s], rows, width)


def gain_rows(experts, cols, w_ref, gains_ref):
    small = w_ref[:, 3 * cols :]
    pick = (iota((8, small.shape[1]), 1) == iota((8, small.shape[1]), 0) + experts).astype(BF16)
    gains_ref[...] = dot(pick, small, ((1,), (1,)))


def attend(scale, head_dim, docs, group_ref, w_ref, wout_ref, gains_ref, own_ref, across_ref,
           vector_ref, qkv_ref, probs_ref, att_ref, keep_ref, send_ref):
    own_heads, length = vector_ref.shape
    cols = own_heads * head_dim
    toks = own_ref.shape[0]
    vectors = vector_ref[...]
    turned = jnp.concatenate([docs[:, toks:], docs[:, :toks]], axis=1)
    across = jnp.broadcast_to(jnp.where(group_ref[0] < 2, docs, turned), (length, length))
    same = across == jnp.transpose(across)
    x = jnp.concatenate([own_ref[...], across_ref[...]], axis=0).astype(F32)
    normed = (x * rms_inverse(x) * gains_ref[0:1]).astype(BF16)
    qkv = dot(normed, w_ref[:, : 3 * cols]).astype(BF16)
    qkv_ref[...] = qkv
    parts = []
    for h in range(own_heads):
        at = h * head_dim
        q = qkv[:, at : at + head_dim]
        k = qkv[:, cols + at : cols + at + head_dim]
        v = qkv[:, 2 * cols + at : 2 * cols + at + head_dim]
        full = jnp.broadcast_to(vectors[h : h + 1], (length, length))
        bias = pltpu.roll(full, 0, 1, stride=1, stride_axis=0)
        scores = jnp.where(same, dot(q, k, ((1,), (1,))) * scale + bias, MASKED)
        top = jnp.max(scores, axis=1, keepdims=True)
        raised = jnp.exp(scores - top)
        probs = raised * (1.0 / jnp.sum(raised, axis=1, keepdims=True))
        probs_ref[h] = probs
        parts.append(dot(probs.astype(BF16), v))
    attended = jnp.concatenate(parts, axis=1).astype(BF16)
    att_ref[...] = attended
    partial = dot(attended, wout_ref[...])
    keep_ref[...] = partial[:toks]
    send_ref[...] = partial[toks:].astype(BF16)


def docs_of_pair(at, length, rows, block_ref, place_ref, arrived_ref):
    sources = arrived_ref.shape[0]
    doc_cols = -(-length // rows)
    held = arrived_ref[(place_ref[0] % sources) ^ 1]
    blocks = [held[j * rows : (j + 1) * rows, at : at + doc_cols].astype(F32) for j in range(4)]
    block = choose(block_ref[0], blocks)
    docs = jnp.zeros((1, length), F32)
    for t in range(doc_cols):
        belongs = iota((rows, length), 1) == iota((rows, length), 0) * doc_cols + t
        docs = docs + jnp.sum(jnp.where(belongs, block[:, t : t + 1], 0.0), axis=0, keepdims=True)
    return docs


def attend_own(scale, head_dim, group_ref, docs_ref, *refs):
    attend(scale, head_dim, docs_ref[...].astype(F32), group_ref, *refs)


def attend_first(scale, head_dim, experts, group_ref, block_ref, place_ref, arrived_ref, own_ref, across_ref,
                 vector_ref, w_ref, wout_ref, gains_ref, *outs):
    place_weights(arrived_ref, w_ref, wout_ref)
    cols = wout_ref.shape[0]
    gain_rows(experts, cols, w_ref, gains_ref)
    docs = docs_of_pair(
        3 * cols + experts + 2, vector_ref.shape[1], cols // arrived_ref.shape[0], block_ref, place_ref,
        arrived_ref,
    )
    attend(scale, head_dim, docs, group_ref, w_ref, wout_ref, gains_ref, own_ref, across_ref,
           vector_ref, *outs)


def attend_first_placed(scale, head_dim, experts, group_ref, block_ref, place_ref, arrived_ref, w_ref, wout_ref,
                        own_ref, across_ref, vector_ref, gains_ref, *outs):
    cols = wout_ref.shape[0]
    gain_rows(experts, cols, w_ref, gains_ref)
    docs = docs_of_pair(
        3 * cols + experts + 2, vector_ref.shape[1], cols // arrived_ref.shape[0], block_ref, place_ref,
        arrived_ref,
    )
    attend(scale, head_dim, docs, group_ref, w_ref, wout_ref, gains_ref, own_ref, across_ref,
           vector_ref, *outs)


def route_tokens(x_ref, keep_ref, core_ref, came_ref, gains_ref, w_ref, chosen_ref, send_ref,
                 g_ref, middle_ref, gate_ref, out_ref):
    middle = x_ref[...].astype(F32) + (
        (keep_ref[...] + core_ref[...].astype(F32)) + came_ref[...].astype(F32)
    )
    middle_ref[...] = middle
    normed = (middle * rms_inverse(middle) * gains_ref[1:2]).astype(BF16)
    g = g_ref[...]
    half = g.shape[1] // 2
    both = jnp.concatenate([normed[:, :half], g[:, :half], normed[:, half:], g[:, half:]], axis=0)
    out_ref[...] = dot(send_ref[...], both).astype(BF16)
    probs = jax.nn.softmax(dot(normed, w_ref[...]), axis=-1)
    gate_ref[...] = jnp.sum(probs * chosen_ref[...], axis=1, keepdims=True)


def run_expert(capacity, place_ref, own_ref, other_ref, router_ref, inner_ref, outer_ref, buf_ref,
               dslot_ref, g_ref, probs_ref, gate_ref, hidden_ref, dpre_ref, keep_ref, send_ref):
    slots = buf_ref.shape[0] // 2
    half = own_ref.shape[1]
    experts = router_ref.shape[1]
    pad = own_ref.shape[0] // (slots // capacity)
    shape = (4 * slots, own_ref.shape[0])
    row = iota(shape, 0)
    part = row // slots
    inside = row - part * slots
    source = inside // capacity
    wanted = source * pad + part * capacity + (inside - source * capacity)
    select = (iota(shape, 1) == wanted).astype(BF16)
    rows = dot(select, jnp.concatenate([own_ref[...], other_ref[...]], axis=1))
    mine = (iota((1, experts), 1) == place_ref[0]).astype(F32)
    for side in range(2):
        at = side * slots
        cut = rows[:, side * half : (side + 1) * half]
        buffers = jnp.concatenate([cut[:slots], cut[2 * slots : 3 * slots]], axis=1).astype(BF16)
        g = jnp.concatenate([cut[slots : 2 * slots], cut[3 * slots :]], axis=1)
        buf_ref[at : at + slots] = buffers
        probs = jax.nn.softmax(dot(buffers, router_ref[...]), axis=-1)
        gate = jnp.sum(probs * mine, axis=1, keepdims=True)
        dslot_ref[at : at + slots] = (gate * g).astype(BF16)
        if side == 0:
            g_ref[...] = g.astype(BF16)
            probs_ref[...] = probs
            gate_ref[...] = gate
    inner = inner_ref[...]
    outer = outer_ref[...]
    pre = dot(buf_ref[...], inner)
    cdf = 0.5 * (1.0 + lax.erf(pre * (0.5**0.5)))
    hidden = (pre * cdf).astype(BF16)
    hidden_ref[...] = hidden
    slope = cdf + pre * jnp.exp(-0.5 * pre * pre) * 0.3989422804014327
    dpre = (dot(dslot_ref[...], outer, ((1,), (1,))) * slope).astype(BF16)
    dpre_ref[...] = dpre
    result = dot(hidden, outer)
    keep_ref[0] = result[:slots]
    send_ref[0] = result[slots:].astype(BF16)
    back = dot(dpre, inner, ((1,), (1,)))
    keep_ref[1] = back[:slots]
    send_ref[1] = back[slots:].astype(BF16)


def finish_expert(capacity, place_ref, keep_ref, came_ref, buf_ref, g_ref, probs_ref, gate_ref,
                  router_ref, out_ref, grad_ref):
    slots = g_ref.shape[0]
    experts = router_ref.shape[1]
    pad = out_ref.shape[0] // (slots // capacity)
    total = (keep_ref[...] + came_ref[...].astype(F32)).astype(BF16)
    result = total[0]
    mine = (iota((1, experts), 1) == place_ref[0]).astype(F32)
    grad_gate = jnp.sum(g_ref[...].astype(F32) * result.astype(F32), axis=1, keepdims=True)
    grad_logits = (grad_gate * gate_ref[...] * (mine - probs_ref[...])).astype(BF16)
    grad_ref[...] = dot(buf_ref[...], grad_logits, ((0,), (0,))).astype(BF16)
    back = total[1].astype(F32) + dot(grad_logits, router_ref[...], ((1,), (1,)))
    shape = (out_ref.shape[0], 4 * slots)
    row = iota(shape, 0)
    source = row // pad
    inside = row - source * pad
    part = inside // capacity
    wanted = jnp.where(part < 4, part * slots + source * capacity + inside - part * capacity, -1)
    expand = (iota(shape, 1) == wanted).astype(BF16)
    back = back.astype(BF16)
    half = back.shape[1] // 2
    both = jnp.concatenate([back[:, :half], result[:, :half], back[:, half:], result[:, half:]], axis=0)
    out_ref[...] = dot(expand, both).astype(BF16)


def middle_backward(back_ref, spread_ref, middle_ref, gains_ref, g_ref):
    middle = middle_ref[...]
    inverse = rms_inverse(middle)
    unit = middle * inverse
    rows = back_ref[...]
    grad_normed = jnp.concatenate([dot(spread_ref[i], rows) for i in range(2)], axis=1)
    dmiddle = g_ref[...].astype(F32) + norm_backward(grad_normed, unit, inverse, gains_ref[1:2])
    return dmiddle, grad_normed * unit


def norm_two_backward(back_ref, spread_ref, middle_ref, gains_ref, g_ref, da_ref, gain_ref):
    dmiddle, scaled = middle_backward(back_ref, spread_ref, middle_ref, gains_ref, g_ref)
    gain_ref[...] = jnp.sum(scaled, axis=0, keepdims=True)
    da_ref[...] = dmiddle.astype(BF16)


def finish_layer(back_ref, spread_ref, later_ref, middle_ref, gains_ref, g_ref, gate_ref, out_ref,
                 dmiddle_ref):
    rows = back_ref[...]
    combined = jnp.concatenate([dot(later_ref[i], rows) for i in range(2)], axis=1)
    out_ref[...] = (middle_ref[...] + gate_ref[...] * combined).astype(BF16)
    dmiddle_ref[...] = middle_backward(back_ref, spread_ref, middle_ref, gains_ref, g_ref)[0]


def attend_backward(scale, head_dim, own_ref, across_ref, wout_ref, qkv_ref, probs_ref, gains_ref,
                    w_ref, x_own_ref, x_across_ref, keep_ref, send_ref, grad_ref, gain_ref,
                    offsets_ref):
    own_heads = probs_ref.shape[0]
    cols = own_heads * head_dim
    toks = own_ref.shape[0]
    length = 2 * toks
    flip = (iota((length, length), 0) + iota((length, length), 1) == length - 1).astype(BF16)
    da = jnp.concatenate([own_ref[...], across_ref[...]], axis=0)
    grad_att = dot(da, wout_ref[...], ((1,), (1,))).astype(BF16)
    qkv = qkv_ref[...]
    parts = [[], [], []]
    for h in range(own_heads):
        at = h * head_dim
        q = qkv[:, at : at + head_dim]
        k = qkv[:, cols + at : cols + at + head_dim]
        v = qkv[:, 2 * cols + at : 2 * cols + at + head_dim]
        gh = grad_att[:, at : at + head_dim]
        probs = probs_ref[h]
        grad_probs = dot(gh, v, ((1,), (1,)))
        row_dot = jnp.sum(probs * grad_probs, axis=1, keepdims=True)
        ds = (probs * (grad_probs - row_dot)).astype(BF16)
        turned = pltpu.roll(dot(flip, ds), 1, 1, stride=1, stride_axis=0)
        offsets_ref[h : h + 1] = jnp.sum(turned, axis=0, keepdims=True)
        parts[0].append(dot(ds, k) * scale)
        parts[1].append(dot(ds, q, ((0,), (0,))) * scale)
        parts[2].append(dot(probs.astype(BF16), gh, ((0,), (0,))))
    grad_qkv = jnp.concatenate(parts[0] + parts[1] + parts[2], axis=1).astype(BF16)
    grad_ref[...] = grad_qkv
    grad_normed = dot(grad_qkv, w_ref[:, : 3 * cols], ((1,), (1,)))
    keep_ref[...] = grad_normed[:toks]
    send_ref[...] = grad_normed[toks:].astype(BF16)
    x = jnp.concatenate([x_own_ref[...], x_across_ref[...]], axis=0).astype(F32)
    gain_ref[...] = jnp.sum(grad_normed * (x * rms_inverse(x)), axis=0, keepdims=True)


def row_weights(own_ref, across_ref, att_ref, grad_ref, gains_ref, x_own_ref, x_across_ref):
    x = jnp.concatenate([x_own_ref[...], x_across_ref[...]], axis=0).astype(F32)
    normed = (x * rms_inverse(x) * gains_ref[0:1]).astype(BF16)
    da = jnp.concatenate([own_ref[...], across_ref[...]], axis=0)
    weights = dot(normed, grad_ref[...], ((0,), (0,)))
    return weights, dot(att_ref[...], da, ((0,), (0,)))


def backward_own(scale, head_dim, own_ref, across_ref, wout_ref, att_ref, qkv_ref, probs_ref,
                 gains_ref, w_ref, x_own_ref, x_across_ref, gw_ref, gout_ref, keep_ref, send_ref,
                 grad_ref, gain_ref, offsets_ref):
    attend_backward(
        scale, head_dim, own_ref, across_ref, wout_ref, qkv_ref, probs_ref, gains_ref, w_ref,
        x_own_ref, x_across_ref, keep_ref, send_ref, grad_ref, gain_ref, offsets_ref,
    )
    gw_ref[...], gout_ref[...] = row_weights(
        own_ref, across_ref, att_ref, grad_ref, gains_ref, x_own_ref, x_across_ref
    )


def sum_weights(packed, buckets, table_cols, *refs):
    gw_ref, gout_ref, own_gain_ref, own_offsets_ref, gain_ref, offsets_ref = refs[7:13]
    gain_two_ref, router_ref, full_ref, out_ref = refs[13:]
    weights, outs = row_weights(*refs[:7])
    own_heads, length = offsets_ref.shape
    width, experts = router_ref.shape
    toks = length // 2
    rows = own_heads * buckets // table_cols
    spot = iota((1, length), 1)
    offset = jnp.where(spot >= toks, spot - length, spot)
    bucket = bucket_of(offset, buckets)
    table = []
    for t in range(table_cols):
        column = jnp.zeros((rows, 1), F32)
        for h in range(own_heads):
            belongs = iota((rows, length), 0) * table_cols + t == bucket * own_heads + h
            value = own_offsets_ref[h : h + 1] + offsets_ref[h : h + 1]
            column = column + jnp.sum(jnp.where(belongs, value, 0.0), axis=1, keepdims=True)
        table.append(column)
    table = jnp.concatenate([jnp.concatenate(table, axis=1)] * (width // rows), axis=0)
    narrow = jnp.concatenate(
        [own_gain_ref[...] + gain_ref[...], gain_two_ref[...], jnp.zeros((6, width), F32)], axis=0
    )
    narrow = jnp.transpose(narrow)[:, :2]
    weights = weights + gw_ref[...]
    pieces = [weights, router_ref[...].astype(F32), narrow, table]
    outs = outs + gout_ref[...]
    out_ref[...] = outs.astype(BF16)
    used = full_ref.shape[1]
    tail = [spare_lanes(outs, used)] if packed else []
    spare = used - sum(p.shape[1] for p in pieces + tail)
    if spare:
        tail.insert(0, jnp.zeros((width, spare), F32))
    full_ref[...] = jnp.concatenate(pieces + tail, axis=1).astype(BF16)


def sum_weights_message(packed, buckets, table_cols, *refs):
    *rest, message_ref, full_ref, out_ref = refs
    sum_weights(packed, buckets, table_cols, *rest, full_ref, out_ref)
    dests, _, wide = message_ref.shape
    rows = out_ref.shape[0] // dests
    used = full_ref.shape[1]
    block = dests * rows
    for s in range(dests):
        for j in range(4):
            at = j * block + s * rows
            message_ref[s, j * rows : (j + 1) * rows, :used] = full_ref[at : at + rows]
            if wide > used:
                message_ref[s, j * rows : (j + 1) * rows, used:] = jnp.zeros(
                    (rows, wide - used), BF16
                )
        put_rows(message_ref, s, out_ref[s * rows : (s + 1) * rows])


def sum_arrived(used, block_ref, arrived_ref, own_ref, *send_refs):
    rows, held = own_ref.shape
    width = held - 2 * used
    block = block_ref[0]
    totals = []
    for variant in range(2):
        total = arrived_ref[variant].astype(F32)
        for s in range(variant + 2, arrived_ref.shape[0], 2):
            total = total + arrived_ref[s].astype(F32)
        totals.append(total)
    pieces = [
        jnp.concatenate([t[j * rows : (j + 1) * rows, :used] for t in totals], axis=1)
        for j in range(4)
    ]
    lasts = [take_rows(t, rows, width) for t in totals]
    first = block % 2 == 0
    own_ref[:, : 2 * used] = choose(block, pieces)
    own_ref[:, 2 * used :] = jnp.where(first, lasts[0], lasts[1])
    for d, ref in zip(ORDER, send_refs):
        ref[:, : 2 * used] = choose(block ^ d, pieces).astype(BF16)
        if d == 1:
            ref[:, 2 * used :] = jnp.where(first, lasts[1], lasts[0]).astype(BF16)


def finish_input(grad_ref, core_ref, came_ref, dmiddle_ref, x_ref, gains_ref, out_ref):
    x = x_ref[...].astype(F32)
    inverse = rms_inverse(x)
    grad_normed = grad_ref[...] + core_ref[...].astype(F32) + came_ref[...].astype(F32)
    out_ref[...] = (
        dmiddle_ref[...] + norm_backward(grad_normed, x * inverse, inverse, gains_ref[0:1])
    ).astype(BF16)


def finish_weights(own_heads, buckets, table_cols, used, group_ref, p0_ref, p3_ref, p1_ref, p2_ref,
                   q_ref, k_ref, v_ref, w_ref, router_ref, one_ref, two_ref, table_ref):
    rows, width = q_ref.shape
    experts = router_ref.shape[0]
    cols = width // 4
    here = p0_ref[...] + p1_ref[...].astype(F32)
    there = p2_ref[...].astype(F32) + p3_ref[...].astype(F32)
    w_ref[...] = here[:, 2 * used :]
    here = here[:, : 2 * used]
    first_core = group_ref[0] < 2
    by_core = (jnp.where(first_core, here, there), jnp.where(first_core, there, here))
    ordered = [c[:, v * used : (v + 1) * used] for c in by_core for v in range(2)]
    pieces = ordered
    for n, ref in enumerate((q_ref, k_ref, v_ref)):
        ref[...] = jnp.concatenate([p[:, n * cols : (n + 1) * cols] for p in ordered], axis=1)
    at = 3 * cols
    small = sum(p[:, at : at + experts + 2] for p in pieces)
    square = -(-max(rows, experts) // 128) * 128
    padded = small[:, :experts]
    if square > experts:
        padded = jnp.concatenate([padded, jnp.zeros((rows, square - experts), F32)], axis=1)
    padded = jnp.concatenate([padded, jnp.zeros((square - rows, square), F32)], axis=0)
    router_ref[...] = jnp.transpose(padded)[:experts, :rows]
    eye = iota((rows, rows), 0) == iota((rows, rows), 1)
    for i, ref in enumerate((one_ref, two_ref)):
        column = small[:, experts + i : experts + i + 1]
        ref[...] = jnp.sum(jnp.where(eye, column, 0.0), axis=0, keepdims=True)
    at += experts + 2
    lines = []
    lane = iota((rows, 128), 1)
    for p in ordered:
        for h in range(own_heads):
            line = jnp.zeros((1, 128), F32)
            for t in range(table_cols):
                belongs = iota((rows, 128), 0) * table_cols + t == lane * own_heads + h
                value = jnp.where(belongs & (lane < buckets), p[:, at + t : at + t + 1], 0.0)
                line = line + jnp.sum(value, axis=0, keepdims=True)
            lines.append(line)
    table_ref[...] = jnp.concatenate(lines, axis=0)[:, :buckets]


def local(
    tokens,
    gain_one,
    w_query,
    w_key,
    w_value,
    w_out,
    bias_table,
    gain_two,
    w_router,
    w_inner,
    w_outer,
    segment_ids,
    routes,
    out_grad,
):
    toks = tokens.shape[1]
    width = tokens.shape[2]
    heads = bias_table.shape[1]
    buckets = bias_table.shape[0]
    head_dim = width // heads
    own_heads = heads // 4
    cols = own_heads * head_dim
    length = 2 * toks
    scale = head_dim ** (-0.5)
    sources = lax.axis_size("expert")
    experts = sources
    capacity = (5 * toks + 4 * experts - 1) // (4 * experts)
    slots = experts * capacity
    pad = -(-4 * capacity // 8) * 8
    rows = w_query.shape[0]
    core = lax.axis_index("dp")
    place = lax.axis_index("expert")
    half = sources // 2
    member = place % 2
    block_at = (2 * core + place // half).reshape(1).astype(jnp.int32)
    first_core = core == 0
    place_at = place.reshape(1).astype(jnp.int32)
    group_at = (2 * core + member).reshape(1).astype(jnp.int32)
    table_cols = max(1, own_heads * buckets // rows)
    extra = max(table_cols, -(-length // rows))
    used = -(-(3 * cols + experts + 2 + extra) // 128) * 128
    aligned = rows % 8 == 0
    held = -(-(3 * cols + used) // 128) * 128
    room = used - (3 * cols + experts + 2 + extra)
    packed = aligned and used < width <= used + 4 * room and (width - used) % 4 == 0
    wide = used if packed else max(used, width)

    def across_group(pieces):
        return [
            lax.ppermute(
                piece,
                ("dp", "expert"),
                [
                    (c * sources + e, (c ^ (d >> 1)) * sources + (e ^ (half * (d & 1))))
                    for c in range(2)
                    for e in range(sources)
                ],
            )
            for d, piece in zip(ORDER, pieces)
        ]

    own_tokens = tokens.reshape(toks, width)
    pair_tokens = swap_pair(own_tokens)

    own_piece, *pieces = kernel_call(
        pack_weights,
        [((rows, held + width * (d < 2)), BF16) for d in (0, *ORDER)],
        group_at, w_query, w_key, w_value, w_router.T, gain_one.reshape(1, rows),
        gain_two.reshape(1, rows), w_out, segment_ids, scalars=1, late=range(1, 9),
        limit=60 * 1024 * 1024,
    )
    pieces = across_group(pieces)
    pair_tokens, own_piece, *pieces = lax.optimization_barrier((pair_tokens, own_piece, *pieces))
    (message,) = kernel_call(
        functools.partial(spread_weights, cols, used), [((half, 5 * rows, wide), BF16)],
        block_at, own_piece, *pieces, scalars=1,
    )
    arrived = exchange_half(message)

    own_across = swap_core(own_tokens)
    pair_across = swap_core(pair_tokens)
    vectors, spread, later, chosen, send = kernel_call(
        functools.partial(prepare, capacity, pad),
        [
            ((own_heads, length), F32),
            ((2, toks, experts * pad), BF16),
            ((2, toks, experts * pad), BF16),
            ((toks, experts), F32),
            ((experts * pad, 4 * toks), BF16),
        ],
        group_at, bias_table, routes.reshape(toks, 1), scalars=2,
    )
    g_low = out_grad.reshape(toks, width)

    row_outs = [
        ((length, 3 * cols), BF16),
        ((own_heads, length, length), F32),
        ((length, cols), BF16),
        ((toks, width), F32),
        ((toks, width), BF16),
    ]
    placed = [((width, used), BF16), ((cols, width), BF16)]
    if aligned:
        weights, out_w, gains, *pair_kept = kernel_call(
            functools.partial(attend_first, scale, head_dim, experts),
            placed + [((8, width), F32)] + row_outs,
            group_at, block_at, place_at, arrived, pair_tokens, pair_across, vectors, scalars=3,
        )
    else:
        weights = arrived[:, : 4 * rows, :used].reshape(half, 2, 2, rows, used)
        weights = weights.transpose(1, 2, 0, 3, 4).reshape(width, used)
        out_w = arrived[:, 4 * rows :, :width].reshape(cols, width)
        gains, *pair_kept = kernel_call(
            functools.partial(attend_first_placed, scale, head_dim, experts),
            [((8, width), F32)] + row_outs,
            group_at, block_at, place_at, arrived, weights, out_w, pair_tokens, pair_across, vectors,
            scalars=3,
        )
    pair_qkv, pair_probs, pair_att, keep, away = pair_kept
    pair_sum = (keep + swap_core(away).astype(F32)).astype(BF16)
    pair_sum, out_w, gains = lax.optimization_barrier((pair_sum, out_w, gains))
    pair_sum = swap_pair(pair_sum)
    own_qkv, own_probs, own_att, keep, away = kernel_call(
        functools.partial(attend_own, scale, head_dim), row_outs,
        group_at, segment_ids, weights, out_w, gains, own_tokens, own_across, vectors, scalars=1,
    )
    router_w = weights[:, 3 * cols : 3 * cols + experts]
    middle, gate, outgoing = kernel_call(
        route_tokens,
        [((toks, width), F32), ((toks, 1), F32), ((experts * pad, width // 2), BF16)],
        own_tokens, keep, swap_core(away), pair_sum, gains, router_w, chosen, send, g_low,
    )
    incoming = exchange(outgoing.reshape(experts, pad, width // 2)).reshape(-1, width // 2)

    inner, outer = w_inner[0], w_outer[0]
    units = inner.shape[1]
    buffers, dslot, slot_g, slot_probs, slot_gate, hidden, dpre, keep, away = kernel_call(
        functools.partial(run_expert, capacity),
        [
            ((2 * slots, width), BF16),
            ((2 * slots, width), BF16),
            ((slots, width), BF16),
            ((slots, experts), F32),
            ((slots, 1), F32),
            ((2 * slots, units), BF16),
            ((2 * slots, units), BF16),
            ((2, slots, width), F32),
            ((2, slots, width), BF16),
        ],
        place_at, incoming, swap_core(incoming), router_w, inner, outer, scalars=1,
    )
    grad_outer = dot(hidden, dslot, ((0,), (0,)))
    grad_inner = dot(buffers, dpre, ((0,), (0,)))
    back, grad_router = kernel_call(
        functools.partial(finish_expert, capacity),
        [((sources * pad, width // 2), BF16), ((width, experts), BF16)],
        place_at, keep, swap_core(away), buffers[:slots], slot_g, slot_probs, slot_gate, router_w,
        scalars=1,
    )
    back = exchange(back.reshape(sources, pad, width // 2)).reshape(-1, width // 2)

    grad_attn, grad_gain_two = kernel_call(
        norm_two_backward, [((toks, width), BF16), ((1, width), F32)],
        back, spread, middle, gains, g_low,
    )
    pair_grad = swap_pair(grad_attn)
    shared = (gains, weights)
    back_outs = [
        ((toks, width), F32),
        ((toks, width), BF16),
        ((length, 3 * cols), BF16),
        ((1, width), F32),
        ((own_heads, length), F32),
    ]
    grad_w, grad_out, grad_normed, away, _, own_gain, own_offsets = kernel_call(
        functools.partial(backward_own, scale, head_dim),
        [((width, 3 * cols), F32), ((cols, width), F32)] + back_outs,
        grad_attn, swap_core(grad_attn), out_w, own_att, own_qkv, own_probs, *shared,
        own_tokens, own_across,
    )
    pair_grad, grad_w, own_away = lax.optimization_barrier((pair_grad, grad_w, away))
    own_came = swap_core(own_away)
    pair_grads = (pair_grad, swap_core(pair_grad))
    keep, away, grad_qkv, pair_gain, pair_offsets = kernel_call(
        functools.partial(attend_backward, scale, head_dim), back_outs,
        *pair_grads, out_w, pair_qkv, pair_probs, *shared, pair_tokens, pair_across,
    )
    to_pair = (keep + swap_core(away).astype(F32)).astype(BF16)
    last = (
        *pair_grads, pair_att, grad_qkv, gains, pair_tokens, pair_across, grad_w, grad_out,
        own_gain, own_offsets, pair_gain, pair_offsets, grad_gain_two, grad_router,
    )
    flat = [((width, used), BF16), ((cols, width), BF16)]
    if aligned:
        (message,) = kernel_call(
            functools.partial(sum_weights_message, packed, buckets, table_cols),
            [((half, 5 * rows, wide), BF16)], *last, held=flat,
        )
    else:
        full, grad_out = kernel_call(
            functools.partial(sum_weights, packed, buckets, table_cols), flat, *last
        )
        full = full.reshape(2, 2, half, rows, used).transpose(2, 0, 1, 3, 4)
        full = full.reshape(half, 4 * rows, used)
        grad_out = grad_out.reshape(half, rows, width)
        message = jnp.concatenate(
            [
                jnp.pad(full, ((0, 0), (0, 0), (0, wide - used))),
                jnp.pad(grad_out, ((0, 0), (0, 0), (0, wide - width))),
            ],
            axis=1,
        )
    came = swap_pair(to_pair)
    arrived = exchange_half(message)
    final, grad_middle = kernel_call(
        finish_layer, [((toks, width), BF16), ((toks, width), F32)],
        back, spread, later, middle, gains, g_low, gate,
    )

    arrived, grad_inner, grad_outer, final, grad_middle = lax.optimization_barrier(
        (arrived, grad_inner, grad_outer, final, grad_middle)
    )

    own_piece, *pieces = kernel_call(
        functools.partial(sum_arrived, used),
        [((rows, 2 * used + width), F32)]
        + [((rows, 2 * used + width * (d < 2)), BF16) for d in ORDER],
        block_at, arrived, scalars=1,
    )
    pieces = across_group(pieces)
    query_grad, key_grad, value_grad, out_grad_w, router_grad, one_grad, two_grad, table_grad = kernel_call(
        functools.partial(finish_weights, own_heads, buckets, table_cols, used),
        [((rows, width), F32)] * 4
        + [((experts, rows), F32), ((1, rows), F32), ((1, rows), F32), ((heads, buckets), F32)],
        group_at, own_piece, *pieces, scalars=1,
    )

    (grad_input,) = kernel_call(
        finish_input, [((toks, width), BF16)],
        grad_normed, own_came, came, grad_middle, own_tokens, gains,
    )
    return (
        final.reshape(tokens.shape),
        grad_input.reshape(tokens.shape),
        one_grad.reshape(rows),
        query_grad,
        key_grad,
        value_grad,
        out_grad_w,
        table_grad.T,
        two_grad.reshape(rows),
        router_grad.T,
        grad_inner[None],
        grad_outer[None],
    )


def solution(mesh):
    both = ("dp", "expert")
    return jax.shard_map(
        local,
        mesh=mesh,
        in_specs=(
            P("expert", "dp", None),
            P(both),
            P(both, None),
            P(both, None),
            P(both, None),
            P(both, None),
            P(),
            P(both),
            P(both, None),
            P("expert", None, "dp"),
            P("expert", "dp", None),
            P("expert", None),
            P("expert", "dp", None),
            P("expert", "dp", None),
        ),
        out_specs=(
            P("expert", "dp", None),
            P("expert", "dp", None),
            P(both),
            P(both, None),
            P(both, None),
            P(both, None),
            P(both, None),
            P(),
            P(both),
            P(both, None),
            P("expert", None, "dp"),
            P("expert", "dp", None),
        ),
        check_vma=False,
    )
```

```python
import functools

import jax
import jax.numpy as jnp
from jax import lax
from jax.experimental import pallas as pl
from jax.experimental.pallas import tpu as pltpu
from jax.sharding import PartitionSpec as P

EPSILON = 1e-06
MASKED = -1000000000.0
BUCKET_EDGES = (1, 2, 3, 4, 5, 6, 7, 8, 12, 16, 23, 32, 46, 64, 91)
F32 = jnp.float32
BF16 = jnp.bfloat16
ORDER = (3, 1, 2)
VMEM_BYTES = 24 * 1024 * 1024


def dot(left, right, dims=((1,), (0,))):
    return lax.dot_general(left, right, (dims, ((), ())), preferred_element_type=F32)


def rms_inverse(values):
    return lax.rsqrt(jnp.mean(values * values, axis=-1, keepdims=True) + EPSILON)


def norm_backward(grad_normed, unit_values, inverse, gain_values):
    grad_unit = grad_normed * gain_values
    projected = jnp.mean(grad_unit * unit_values, axis=-1, keepdims=True)
    return inverse * (grad_unit - unit_values * projected)


def swap_core(value):
    return lax.ppermute(value, "dp", [(0, 1), (1, 0)])


def swap_pair(value):
    n = lax.axis_size("expert")
    return lax.ppermute(value, "expert", [(i, i ^ 1) for i in range(n)])


def exchange(value):
    return lax.all_to_all(value, "expert", split_axis=0, concat_axis=0, tiled=True)


def exchange_half(value):
    half = lax.axis_size("expert") // 2
    groups = [[q * half + s for s in range(half)] for q in range(2)]
    return lax.all_to_all(
        value, "expert", split_axis=0, concat_axis=0, tiled=True, axis_index_groups=groups
    )


def bucket_of(offset, total):
    distance = jnp.abs(offset)
    bucket = jnp.zeros(offset.shape, jnp.int32)
    for border in BUCKET_EDGES:
        bucket = bucket + (distance >= border).astype(jnp.int32)
    return bucket + total // 2 * (offset > 0).astype(jnp.int32)


def iota(shape, axis):
    return lax.broadcasted_iota(jnp.int32, shape, axis)


class LateRef:
    def __init__(self, source, target, sem):
        self.copy = pltpu.make_async_copy(source, target, sem)
        self.target = target
        self.shape = target.shape
        self.pending = True
        self.copy.start()

    def wait(self):
        if self.pending:
            self.copy.wait()
            self.pending = False

    def __getitem__(self, index):
        self.wait()
        return self.target[index]


def kernel_call(body, outs, *args, scalars=0, late=(), limit=VMEM_BYTES, held=()):
    count = len(args)
    late = sorted(late)

    def run(*refs):
        ins = list(refs[:count])
        out_refs = refs[count : count + len(outs)]
        scratch = refs[count + len(outs) :]
        for n, i in enumerate(late):
            ins[i] = LateRef(ins[i], scratch[n], scratch[-1].at[n])
        body(*ins, *out_refs, *scratch[len(late) : len(late) + len(held)])
        for i in late:
            ins[i].wait()

    spaces = [pltpu.SMEM if i < scalars else pltpu.VMEM for i in range(count)]
    for i in late:
        spaces[i] = pltpu.HBM
    scratch = [pltpu.VMEM(args[i].shape, args[i].dtype) for i in late]
    scratch += [pltpu.VMEM(shape, dtype) for shape, dtype in held]
    if late:
        scratch.append(pltpu.SemaphoreType.DMA((len(late),)))
    return pl.pallas_call(
        run,
        out_shape=[jax.ShapeDtypeStruct(shape, dtype) for shape, dtype in outs],
        in_specs=[pl.BlockSpec(memory_space=space) for space in spaces],
        out_specs=[pl.BlockSpec(memory_space=pltpu.VMEM)] * len(outs),
        scratch_shapes=scratch,
        compiler_params=pltpu.CompilerParams(vmem_limit_bytes=limit),
        cost_estimate=pl.CostEstimate(
            flops=1_000_000, bytes_accessed=1_000_000, transcendentals=0
        ),
    )(*args)


def choose(index, values):
    picked = values[0]
    for i in range(1, len(values)):
        picked = jnp.where(index == i, values[i], picked)
    return picked


def pack_weights(group_ref, q_ref, k_ref, v_ref, router_ref, one_ref, two_ref, wout_ref, docs_ref,
                 *refs):
    keep_ref, *out_refs = refs
    first_core = group_ref[0] < 2
    rows, width = q_ref.shape
    experts = router_ref.shape[0]
    cols = width // 4
    eye = iota((rows, rows), 0) == iota((rows, rows), 1)
    router = dot(eye.astype(F32).astype(BF16), router_ref[...], ((1,), (1,)))
    columns = [
        jnp.sum(jnp.where(eye, ref[...].astype(F32), 0.0), axis=1, keepdims=True)
        for ref in (one_ref, two_ref)
    ]
    docs = docs_ref[...].astype(F32)
    length = docs.shape[1]
    doc_cols = -(-length // rows)
    for t in range(doc_cols):
        belongs = iota((rows, length), 1) == iota((rows, length), 0) * doc_cols + t
        columns.append(jnp.sum(jnp.where(belongs, docs, 0.0), axis=1, keepdims=True))
    pad = out_refs[0].shape[1] - 6 * cols - experts - 2 - doc_cols
    small = jnp.concatenate(
        [router] + columns + [jnp.zeros((rows, pad), F32)], axis=1
    ).astype(BF16)
    weights = [ref[...] for ref in (q_ref, k_ref, v_ref)]
    pieces = [
        jnp.concatenate(
            [w[:, j * cols : (j + 1) * cols] for j in (2 * c, 2 * c + 1) for w in weights] + [small],
            axis=1,
        )
        for c in range(2)
    ]
    here = jnp.where(first_core, pieces[0], pieces[1])
    there = jnp.where(first_core, pieces[1], pieces[0])
    held = small.shape[1] + 6 * cols
    for d, ref in zip((0, *ORDER), (keep_ref, *out_refs)):
        ref[:, :held] = there if d > 1 else here
        if d < 2:
            ref[:, held:] = wout_ref[...]


def put_rows(ref, dest, value):
    rows, width = value.shape
    wide = ref.shape[2]
    ref[dest, 4 * rows :, : min(wide, width)] = value[:, :wide]
    if wide > width:
        ref[dest, 4 * rows :, width:] = jnp.zeros((rows, wide - width), BF16)


def spare_lanes(value, wide):
    over = (value.shape[1] - wide) // 4
    return jnp.concatenate(
        [value[:, wide + j * over : wide + (j + 1) * over] for j in range(4)], axis=0
    )


def take_rows(held, rows, width):
    wide = held.shape[1]
    if wide >= width:
        return held[4 * rows :, :width]
    over = (width - wide) // 4
    tail = [held[j * rows : (j + 1) * rows, wide - over :] for j in range(4)]
    return jnp.concatenate([held[4 * rows :]] + tail, axis=1)


def spread_weights(cols, used, block_ref, own_ref, p3_ref, p1_ref, p2_ref, out_ref):
    dests, _, wide = out_ref.shape
    rows, held = p2_ref.shape
    block = block_ref[0]
    pieces = [ref[:, :held] for ref in (own_ref, p1_ref, p2_ref, p3_ref)]
    both = jnp.concatenate([choose(block ^ j, pieces) for j in range(4)], axis=0)
    lasts = [own_ref[:, held:], p1_ref[:, held:]]
    small = both[:, 6 * cols : 3 * cols + used]
    for variant in range(2):
        at = variant * 3 * cols
        value = jnp.concatenate([both[:, at : at + 3 * cols], small], axis=1)
        if wide > used:
            value = jnp.concatenate([value, jnp.zeros((4 * rows, wide - used), BF16)], axis=1)
        last = jnp.where(block % 2 == variant, lasts[0], lasts[1])
        if wide < last.shape[1]:
            spare = spare_lanes(last, wide)
            value = jnp.concatenate([value[:, : wide - spare.shape[1]], spare], axis=1)
        for dest in range(variant, dests, 2):
            out_ref[dest, : 4 * rows] = value
            put_rows(out_ref, dest, last)


def prepare(capacity, pad, group_ref, table_ref, routes_ref, vector_ref, spread_ref, later_ref,
            gather_ref):
    buckets = table_ref.shape[0]
    own_heads, length = vector_ref.shape
    toks = length // 2
    group = group_ref[0]
    spot = iota((1, length), 1)
    offset = jnp.where(spot >= toks, spot - length, spot)
    bucket = bucket_of(offset, buckets)
    for h in range(own_heads):
        vector = jnp.zeros((1, length), F32)
        for b in range(buckets):
            vector = jnp.where(bucket == b, table_ref[b, group * own_heads + h], vector)
        vector_ref[h : h + 1] = vector
    experts = gather_ref.shape[1]
    route = routes_ref[...]
    chosen = route == iota((toks, experts), 1)
    gather_ref[...] = chosen.astype(F32)
    lower = (iota((toks, toks), 0) > iota((toks, toks), 1)).astype(BF16)
    counts = dot(lower, chosen.astype(BF16))
    slot = jnp.sum(jnp.where(chosen, counts, 0.0), axis=1, keepdims=True).astype(jnp.int32)
    across = iota((toks, experts * pad), 1)
    for i in range(4):
        place = jnp.where(slot < capacity, route * pad + i * capacity + slot, -1)
        spread = (place == across).astype(F32)
        target = (spread_ref, later_ref)[i % 2]
        target[i // 2] = spread.astype(BF16)


def place_weights(arrived_ref, w_ref, wout_ref):
    sources = arrived_ref.shape[0]
    rows = wout_ref.shape[0] // sources
    used = w_ref.shape[1]
    width = wout_ref.shape[1]
    block = sources * rows
    for s in range(sources):
        for j in range(4):
            w_ref[j * block + s * rows : j * block + (s + 1) * rows] = arrived_ref[
                s, j * rows : (j + 1) * rows, :used
            ]
        wout_ref[s * rows : (s + 1) * rows] = take_rows(arrived_ref[s], rows, width)


def gain_rows(experts, cols, w_ref, gains_ref):
    small = w_ref[:, 3 * cols :]
    pick = (iota((8, small.shape[1]), 1) == iota((8, small.shape[1]), 0) + experts).astype(BF16)
    gains_ref[...] = dot(pick, small, ((1,), (1,)))


def attend(scale, head_dim, docs, group_ref, w_ref, wout_ref, gains_ref, own_ref, across_ref,
           vector_ref, qkv_ref, probs_ref, att_ref, keep_ref, send_ref):
    own_heads, length = vector_ref.shape
    cols = own_heads * head_dim
    toks = own_ref.shape[0]
    vectors = vector_ref[...]
    turned = jnp.concatenate([docs[:, toks:], docs[:, :toks]], axis=1)
    across = jnp.broadcast_to(jnp.where(group_ref[0] < 2, docs, turned), (length, length))
    same = across == jnp.transpose(across)
    x = jnp.concatenate([own_ref[...], across_ref[...]], axis=0).astype(F32)
    normed = (x * rms_inverse(x) * gains_ref[0:1]).astype(BF16)
    qkv = dot(normed, w_ref[:, : 3 * cols]).astype(BF16)
    qkv_ref[...] = qkv
    parts = []
    for h in range(own_heads):
        at = h * head_dim
        q = qkv[:, at : at + head_dim]
        k = qkv[:, cols + at : cols + at + head_dim]
        v = qkv[:, 2 * cols + at : 2 * cols + at + head_dim]
        full = jnp.broadcast_to(vectors[h : h + 1], (length, length))
        bias = pltpu.roll(full, 0, 1, stride=1, stride_axis=0)
        scores = jnp.where(same, dot(q, k, ((1,), (1,))) * scale + bias, MASKED)
        top = jnp.max(scores, axis=1, keepdims=True)
        raised = jnp.exp(scores - top)
        probs = raised * (1.0 / jnp.sum(raised, axis=1, keepdims=True))
        probs_ref[h] = probs
        parts.append(dot(probs.astype(BF16), v))
    attended = jnp.concatenate(parts, axis=1).astype(BF16)
    att_ref[...] = attended
    partial = dot(attended, wout_ref[...])
    keep_ref[...] = partial[:toks]
    send_ref[...] = partial[toks:].astype(BF16)


def docs_of_pair(at, length, rows, block_ref, place_ref, arrived_ref):
    sources = arrived_ref.shape[0]
    doc_cols = -(-length // rows)
    held = arrived_ref[(place_ref[0] % sources) ^ 1]
    blocks = [held[j * rows : (j + 1) * rows, at : at + doc_cols].astype(F32) for j in range(4)]
    block = choose(block_ref[0], blocks)
    docs = jnp.zeros((1, length), F32)
    for t in range(doc_cols):
        belongs = iota((rows, length), 1) == iota((rows, length), 0) * doc_cols + t
        docs = docs + jnp.sum(jnp.where(belongs, block[:, t : t + 1], 0.0), axis=0, keepdims=True)
    return docs


def attend_own(scale, head_dim, group_ref, docs_ref, *refs):
    attend(scale, head_dim, docs_ref[...].astype(F32), group_ref, *refs)


def attend_first(scale, head_dim, experts, group_ref, block_ref, place_ref, arrived_ref, own_ref, across_ref,
                 vector_ref, w_ref, wout_ref, gains_ref, *outs):
    place_weights(arrived_ref, w_ref, wout_ref)
    cols = wout_ref.shape[0]
    gain_rows(experts, cols, w_ref, gains_ref)
    docs = docs_of_pair(
        3 * cols + experts + 2, vector_ref.shape[1], cols // arrived_ref.shape[0], block_ref, place_ref,
        arrived_ref,
    )
    attend(scale, head_dim, docs, group_ref, w_ref, wout_ref, gains_ref, own_ref, across_ref,
           vector_ref, *outs)


def attend_first_placed(scale, head_dim, experts, group_ref, block_ref, place_ref, arrived_ref, w_ref, wout_ref,
                        own_ref, across_ref, vector_ref, gains_ref, *outs):
    cols = wout_ref.shape[0]
    gain_rows(experts, cols, w_ref, gains_ref)
    docs = docs_of_pair(
        3 * cols + experts + 2, vector_ref.shape[1], cols // arrived_ref.shape[0], block_ref, place_ref,
        arrived_ref,
    )
    attend(scale, head_dim, docs, group_ref, w_ref, wout_ref, gains_ref, own_ref, across_ref,
           vector_ref, *outs)


def route_tokens(capacity, pad, x_ref, keep_ref, core_ref, came_ref, gains_ref, w_ref, chosen_ref,
                 routes_ref, g_ref, middle_ref, gate_ref, out_ref):
    middle = x_ref[...].astype(F32) + (
        (keep_ref[...] + core_ref[...].astype(F32)) + came_ref[...].astype(F32)
    )
    middle_ref[...] = middle
    normed = (middle * rms_inverse(middle) * gains_ref[1:2]).astype(BF16)
    g = g_ref[...]
    half = g.shape[1] // 2
    both = jnp.concatenate([normed[:, :half], g[:, :half], normed[:, half:], g[:, half:]], axis=0)
    toks = g.shape[0]
    experts = w_ref.shape[1]
    route = routes_ref[...]
    chosen = iota((experts, toks), 0) == route
    upper = (iota((toks, toks), 0) < iota((toks, toks), 1)).astype(BF16)
    counts = dot(chosen.astype(BF16), upper)
    slot = jnp.sum(jnp.where(chosen, counts, 0.0), axis=0, keepdims=True).astype(jnp.int32)
    rows = out_ref.shape[0]
    place = jnp.where(slot < capacity, route * pad + slot, -4 * rows)
    down = iota((rows, toks), 0)
    send = jnp.concatenate(
        [(down == place + i * capacity).astype(BF16) for i in range(4)], axis=1
    )
    out_ref[...] = dot(send, both).astype(BF16)
    probs = jax.nn.softmax(dot(normed, w_ref[...]), axis=-1)
    gate_ref[...] = jnp.sum(probs * chosen_ref[...], axis=1, keepdims=True)


def run_expert(capacity, place_ref, own_ref, other_ref, router_ref, inner_ref, outer_ref, buf_ref,
               dslot_ref, g_ref, probs_ref, gate_ref, hidden_ref, dpre_ref, keep_ref, send_ref):
    slots = buf_ref.shape[0] // 2
    half = own_ref.shape[1]
    experts = router_ref.shape[1]
    pad = own_ref.shape[0] // (slots // capacity)
    shape = (4 * slots, own_ref.shape[0])
    row = iota(shape, 0)
    part = row // slots
    inside = row - part * slots
    source = inside // capacity
    wanted = source * pad + part * capacity + (inside - source * capacity)
    select = (iota(shape, 1) == wanted).astype(BF16)
    rows = dot(select, jnp.concatenate([own_ref[...], other_ref[...]], axis=1))
    mine = (iota((1, experts), 1) == place_ref[0]).astype(F32)
    for side in range(2):
        at = side * slots
        cut = rows[:, side * half : (side + 1) * half]
        buffers = jnp.concatenate([cut[:slots], cut[2 * slots : 3 * slots]], axis=1).astype(BF16)
        g = jnp.concatenate([cut[slots : 2 * slots], cut[3 * slots :]], axis=1)
        buf_ref[at : at + slots] = buffers
        probs = jax.nn.softmax(dot(buffers, router_ref[...]), axis=-1)
        gate = jnp.sum(probs * mine, axis=1, keepdims=True)
        dslot_ref[at : at + slots] = (gate * g).astype(BF16)
        if side == 0:
            g_ref[...] = g.astype(BF16)
            probs_ref[...] = probs
            gate_ref[...] = gate
    inner = inner_ref[...]
    outer = outer_ref[...]
    pre = dot(buf_ref[...], inner)
    cdf = 0.5 * (1.0 + lax.erf(pre * (0.5**0.5)))
    hidden = (pre * cdf).astype(BF16)
    hidden_ref[...] = hidden
    slope = cdf + pre * jnp.exp(-0.5 * pre * pre) * 0.3989422804014327
    dpre = (dot(dslot_ref[...], outer, ((1,), (1,))) * slope).astype(BF16)
    dpre_ref[...] = dpre
    result = dot(hidden, outer)
    keep_ref[0] = result[:slots]
    send_ref[0] = result[slots:].astype(BF16)
    back = dot(dpre, inner, ((1,), (1,)))
    keep_ref[1] = back[:slots]
    send_ref[1] = back[slots:].astype(BF16)


def finish_expert(capacity, place_ref, keep_ref, came_ref, buf_ref, g_ref, probs_ref, gate_ref,
                  router_ref, out_ref, grad_ref):
    slots = g_ref.shape[0]
    experts = router_ref.shape[1]
    pad = out_ref.shape[0] // (slots // capacity)
    total = (keep_ref[...] + came_ref[...].astype(F32)).astype(BF16)
    result = total[0]
    mine = (iota((1, experts), 1) == place_ref[0]).astype(F32)
    grad_gate = jnp.sum(g_ref[...].astype(F32) * result.astype(F32), axis=1, keepdims=True)
    grad_logits = (grad_gate * gate_ref[...] * (mine - probs_ref[...])).astype(BF16)
    grad_ref[...] = dot(buf_ref[...], grad_logits, ((0,), (0,))).astype(BF16)
    back = total[1].astype(F32) + dot(grad_logits, router_ref[...], ((1,), (1,)))
    shape = (out_ref.shape[0], 4 * slots)
    row = iota(shape, 0)
    source = row // pad
    inside = row - source * pad
    part = inside // capacity
    wanted = jnp.where(part < 4, part * slots + source * capacity + inside - part * capacity, -1)
    expand = (iota(shape, 1) == wanted).astype(BF16)
    back = back.astype(BF16)
    half = back.shape[1] // 2
    both = jnp.concatenate([back[:, :half], result[:, :half], back[:, half:], result[:, half:]], axis=0)
    out_ref[...] = dot(expand, both).astype(BF16)


def middle_backward(back_ref, spread_ref, middle_ref, gains_ref, g_ref):
    middle = middle_ref[...]
    inverse = rms_inverse(middle)
    unit = middle * inverse
    rows = back_ref[...]
    grad_normed = jnp.concatenate([dot(spread_ref[i], rows) for i in range(2)], axis=1)
    dmiddle = g_ref[...].astype(F32) + norm_backward(grad_normed, unit, inverse, gains_ref[1:2])
    return dmiddle, grad_normed * unit


def norm_two_backward(back_ref, spread_ref, middle_ref, gains_ref, g_ref, da_ref, gain_ref):
    dmiddle, scaled = middle_backward(back_ref, spread_ref, middle_ref, gains_ref, g_ref)
    gain_ref[...] = jnp.sum(scaled, axis=0, keepdims=True)
    da_ref[...] = dmiddle.astype(BF16)


def finish_layer(back_ref, spread_ref, later_ref, middle_ref, gains_ref, g_ref, gate_ref, out_ref,
                 dmiddle_ref):
    rows = back_ref[...]
    combined = jnp.concatenate([dot(later_ref[i], rows) for i in range(2)], axis=1)
    out_ref[...] = (middle_ref[...] + gate_ref[...] * combined).astype(BF16)
    dmiddle_ref[...] = middle_backward(back_ref, spread_ref, middle_ref, gains_ref, g_ref)[0]


def attend_backward(scale, head_dim, own_ref, across_ref, wout_ref, qkv_ref, probs_ref, gains_ref,
                    w_ref, x_own_ref, x_across_ref, keep_ref, send_ref, grad_ref, gain_ref,
                    offsets_ref):
    own_heads = probs_ref.shape[0]
    cols = own_heads * head_dim
    toks = own_ref.shape[0]
    length = 2 * toks
    flip = (iota((length, length), 0) + iota((length, length), 1) == length - 1).astype(BF16)
    da = jnp.concatenate([own_ref[...], across_ref[...]], axis=0)
    grad_att = dot(da, wout_ref[...], ((1,), (1,))).astype(BF16)
    qkv = qkv_ref[...]
    parts = [[], [], []]
    for h in range(own_heads):
        at = h * head_dim
        q = qkv[:, at : at + head_dim]
        k = qkv[:, cols + at : cols + at + head_dim]
        v = qkv[:, 2 * cols + at : 2 * cols + at + head_dim]
        gh = grad_att[:, at : at + head_dim]
        probs = probs_ref[h]
        grad_probs = dot(gh, v, ((1,), (1,)))
        row_dot = jnp.sum(probs * grad_probs, axis=1, keepdims=True)
        ds = (probs * (grad_probs - row_dot)).astype(BF16)
        turned = pltpu.roll(dot(flip, ds), 1, 1, stride=1, stride_axis=0)
        offsets_ref[h : h + 1] = jnp.sum(turned, axis=0, keepdims=True)
        parts[0].append(dot(ds, k) * scale)
        parts[1].append(dot(ds, q, ((0,), (0,))) * scale)
        parts[2].append(dot(probs.astype(BF16), gh, ((0,), (0,))))
    grad_qkv = jnp.concatenate(parts[0] + parts[1] + parts[2], axis=1).astype(BF16)
    grad_ref[...] = grad_qkv
    grad_normed = dot(grad_qkv, w_ref[:, : 3 * cols], ((1,), (1,)))
    keep_ref[...] = grad_normed[:toks]
    send_ref[...] = grad_normed[toks:].astype(BF16)
    x = jnp.concatenate([x_own_ref[...], x_across_ref[...]], axis=0).astype(F32)
    gain_ref[...] = jnp.sum(grad_normed * (x * rms_inverse(x)), axis=0, keepdims=True)


def row_weights(own_ref, across_ref, att_ref, grad_ref, gains_ref, x_own_ref, x_across_ref):
    x = jnp.concatenate([x_own_ref[...], x_across_ref[...]], axis=0).astype(F32)
    normed = (x * rms_inverse(x) * gains_ref[0:1]).astype(BF16)
    da = jnp.concatenate([own_ref[...], across_ref[...]], axis=0)
    weights = dot(normed, grad_ref[...], ((0,), (0,)))
    return weights, dot(att_ref[...], da, ((0,), (0,)))


def backward_own(scale, head_dim, own_ref, across_ref, wout_ref, att_ref, qkv_ref, probs_ref,
                 gains_ref, w_ref, x_own_ref, x_across_ref, gw_ref, gout_ref, keep_ref, send_ref,
                 grad_ref, gain_ref, offsets_ref):
    attend_backward(
        scale, head_dim, own_ref, across_ref, wout_ref, qkv_ref, probs_ref, gains_ref, w_ref,
        x_own_ref, x_across_ref, keep_ref, send_ref, grad_ref, gain_ref, offsets_ref,
    )
    gw_ref[...], gout_ref[...] = row_weights(
        own_ref, across_ref, att_ref, grad_ref, gains_ref, x_own_ref, x_across_ref
    )


def sum_weights(packed, buckets, table_cols, *refs):
    gw_ref, gout_ref, own_gain_ref, own_offsets_ref, gain_ref, offsets_ref = refs[7:13]
    gain_two_ref, router_ref, full_ref, out_ref = refs[13:]
    weights, outs = row_weights(*refs[:7])
    own_heads, length = offsets_ref.shape
    width, experts = router_ref.shape
    toks = length // 2
    rows = own_heads * buckets // table_cols
    spot = iota((1, length), 1)
    offset = jnp.where(spot >= toks, spot - length, spot)
    bucket = bucket_of(offset, buckets)
    table = []
    for t in range(table_cols):
        column = jnp.zeros((rows, 1), F32)
        for h in range(own_heads):
            belongs = iota((rows, length), 0) * table_cols + t == bucket * own_heads + h
            value = own_offsets_ref[h : h + 1] + offsets_ref[h : h + 1]
            column = column + jnp.sum(jnp.where(belongs, value, 0.0), axis=1, keepdims=True)
        table.append(column)
    table = jnp.concatenate([jnp.concatenate(table, axis=1)] * (width // rows), axis=0)
    narrow = jnp.concatenate(
        [own_gain_ref[...] + gain_ref[...], gain_two_ref[...], jnp.zeros((6, width), F32)], axis=0
    )
    narrow = jnp.transpose(narrow)[:, :2]
    weights = weights + gw_ref[...]
    pieces = [weights, router_ref[...].astype(F32), narrow, table]
    outs = outs + gout_ref[...]
    out_ref[...] = outs.astype(BF16)
    used = full_ref.shape[1]
    tail = [spare_lanes(outs, used)] if packed else []
    spare = used - sum(p.shape[1] for p in pieces + tail)
    if spare:
        tail.insert(0, jnp.zeros((width, spare), F32))
    full_ref[...] = jnp.concatenate(pieces + tail, axis=1).astype(BF16)


def sum_weights_message(packed, buckets, table_cols, *refs):
    *rest, message_ref, full_ref, out_ref = refs
    sum_weights(packed, buckets, table_cols, *rest, full_ref, out_ref)
    dests, _, wide = message_ref.shape
    rows = out_ref.shape[0] // dests
    used = full_ref.shape[1]
    block = dests * rows
    for s in range(dests):
        for j in range(4):
            at = j * block + s * rows
            message_ref[s, j * rows : (j + 1) * rows, :used] = full_ref[at : at + rows]
            if wide > used:
                message_ref[s, j * rows : (j + 1) * rows, used:] = jnp.zeros(
                    (rows, wide - used), BF16
                )
        put_rows(message_ref, s, out_ref[s * rows : (s + 1) * rows])


def sum_arrived(used, block_ref, arrived_ref, own_ref, *send_refs):
    rows, held = own_ref.shape
    width = held - 2 * used
    block = block_ref[0]
    totals = []
    for variant in range(2):
        total = arrived_ref[variant].astype(F32)
        for s in range(variant + 2, arrived_ref.shape[0], 2):
            total = total + arrived_ref[s].astype(F32)
        totals.append(total)
    pieces = [
        jnp.concatenate([t[j * rows : (j + 1) * rows, :used] for t in totals], axis=1)
        for j in range(4)
    ]
    lasts = [take_rows(t, rows, width) for t in totals]
    first = block % 2 == 0
    own_ref[:, : 2 * used] = choose(block, pieces)
    own_ref[:, 2 * used :] = jnp.where(first, lasts[0], lasts[1])
    for d, ref in zip(ORDER, send_refs):
        ref[:, : 2 * used] = choose(block ^ d, pieces).astype(BF16)
        if d == 1:
            ref[:, 2 * used :] = jnp.where(first, lasts[1], lasts[0]).astype(BF16)


def finish_input(grad_ref, core_ref, came_ref, dmiddle_ref, x_ref, gains_ref, out_ref):
    x = x_ref[...].astype(F32)
    inverse = rms_inverse(x)
    grad_normed = grad_ref[...] + core_ref[...].astype(F32) + came_ref[...].astype(F32)
    out_ref[...] = (
        dmiddle_ref[...] + norm_backward(grad_normed, x * inverse, inverse, gains_ref[0:1])
    ).astype(BF16)


def finish_weights(own_heads, buckets, table_cols, used, group_ref, p0_ref, p3_ref, p1_ref, p2_ref,
                   q_ref, k_ref, v_ref, w_ref, router_ref, one_ref, two_ref, table_ref):
    rows, width = q_ref.shape
    experts = router_ref.shape[0]
    cols = width // 4
    here = p0_ref[...] + p1_ref[...].astype(F32)
    there = p2_ref[...].astype(F32) + p3_ref[...].astype(F32)
    w_ref[...] = here[:, 2 * used :]
    here = here[:, : 2 * used]
    first_core = group_ref[0] < 2
    by_core = (jnp.where(first_core, here, there), jnp.where(first_core, there, here))
    ordered = [c[:, v * used : (v + 1) * used] for c in by_core for v in range(2)]
    pieces = ordered
    for n, ref in enumerate((q_ref, k_ref, v_ref)):
        ref[...] = jnp.concatenate([p[:, n * cols : (n + 1) * cols] for p in ordered], axis=1)
    at = 3 * cols
    small = sum(p[:, at : at + experts + 2] for p in pieces)
    square = -(-max(rows, experts) // 128) * 128
    padded = small[:, :experts]
    if square > experts:
        padded = jnp.concatenate([padded, jnp.zeros((rows, square - experts), F32)], axis=1)
    padded = jnp.concatenate([padded, jnp.zeros((square - rows, square), F32)], axis=0)
    router_ref[...] = jnp.transpose(padded)[:experts, :rows]
    eye = iota((rows, rows), 0) == iota((rows, rows), 1)
    for i, ref in enumerate((one_ref, two_ref)):
        column = small[:, experts + i : experts + i + 1]
        ref[...] = jnp.sum(jnp.where(eye, column, 0.0), axis=0, keepdims=True)
    at += experts + 2
    lines = []
    lane = iota((rows, 128), 1)
    for p in ordered:
        for h in range(own_heads):
            line = jnp.zeros((1, 128), F32)
            for t in range(table_cols):
                belongs = iota((rows, 128), 0) * table_cols + t == lane * own_heads + h
                value = jnp.where(belongs & (lane < buckets), p[:, at + t : at + t + 1], 0.0)
                line = line + jnp.sum(value, axis=0, keepdims=True)
            lines.append(line)
    table_ref[...] = jnp.concatenate(lines, axis=0)[:, :buckets]


def local(
    tokens,
    gain_one,
    w_query,
    w_key,
    w_value,
    w_out,
    bias_table,
    gain_two,
    w_router,
    w_inner,
    w_outer,
    segment_ids,
    routes,
    out_grad,
):
    toks = tokens.shape[1]
    width = tokens.shape[2]
    heads = bias_table.shape[1]
    buckets = bias_table.shape[0]
    head_dim = width // heads
    own_heads = heads // 4
    cols = own_heads * head_dim
    length = 2 * toks
    scale = head_dim ** (-0.5)
    sources = lax.axis_size("expert")
    experts = sources
    capacity = (5 * toks + 4 * experts - 1) // (4 * experts)
    slots = experts * capacity
    pad = -(-4 * capacity // 8) * 8
    rows = w_query.shape[0]
    core = lax.axis_index("dp")
    place = lax.axis_index("expert")
    half = sources // 2
    member = place % 2
    block_at = (2 * core + place // half).reshape(1).astype(jnp.int32)
    first_core = core == 0
    place_at = place.reshape(1).astype(jnp.int32)
    group_at = (2 * core + member).reshape(1).astype(jnp.int32)
    table_cols = max(1, own_heads * buckets // rows)
    extra = max(table_cols, -(-length // rows))
    used = -(-(3 * cols + experts + 2 + extra) // 128) * 128
    aligned = rows % 8 == 0
    held = -(-(3 * cols + used) // 128) * 128
    room = used - (3 * cols + experts + 2 + extra)
    packed = aligned and used < width <= used + 4 * room and (width - used) % 4 == 0
    wide = used if packed else max(used, width)

    def across_group(pieces):
        return [
            lax.ppermute(
                piece,
                ("dp", "expert"),
                [
                    (c * sources + e, (c ^ (d >> 1)) * sources + (e ^ (half * (d & 1))))
                    for c in range(2)
                    for e in range(sources)
                ],
            )
            for d, piece in zip(ORDER, pieces)
        ]

    own_tokens = tokens.reshape(toks, width)
    pair_tokens = swap_pair(own_tokens)

    own_piece, *pieces = kernel_call(
        pack_weights,
        [((rows, held + width * (d < 2)), BF16) for d in (0, *ORDER)],
        group_at, w_query, w_key, w_value, w_router.T, gain_one.reshape(1, rows),
        gain_two.reshape(1, rows), w_out, segment_ids, scalars=1, late=range(1, 9),
        limit=60 * 1024 * 1024,
    )
    pieces = across_group(pieces)
    pair_tokens, own_piece, *pieces = lax.optimization_barrier((pair_tokens, own_piece, *pieces))
    (message,) = kernel_call(
        functools.partial(spread_weights, cols, used), [((half, 5 * rows, wide), BF16)],
        block_at, own_piece, *pieces, scalars=1,
    )
    arrived = exchange_half(message)

    own_across = swap_core(own_tokens)
    pair_across = swap_core(pair_tokens)
    vectors, spread, later, chosen = kernel_call(
        functools.partial(prepare, capacity, pad),
        [
            ((own_heads, length), F32),
            ((2, toks, experts * pad), BF16),
            ((2, toks, experts * pad), BF16),
            ((toks, experts), F32),
        ],
        group_at, bias_table, routes.reshape(toks, 1), scalars=2,
    )
    g_low = out_grad.reshape(toks, width)

    row_outs = [
        ((length, 3 * cols), BF16),
        ((own_heads, length, length), F32),
        ((length, cols), BF16),
        ((toks, width), F32),
        ((toks, width), BF16),
    ]
    placed = [((width, used), BF16), ((cols, width), BF16)]
    if aligned:
        weights, out_w, gains, *pair_kept = kernel_call(
            functools.partial(attend_first, scale, head_dim, experts),
            placed + [((8, width), F32)] + row_outs,
            group_at, block_at, place_at, arrived, pair_tokens, pair_across, vectors, scalars=3,
        )
    else:
        weights = arrived[:, : 4 * rows, :used].reshape(half, 2, 2, rows, used)
        weights = weights.transpose(1, 2, 0, 3, 4).reshape(width, used)
        out_w = arrived[:, 4 * rows :, :width].reshape(cols, width)
        gains, *pair_kept = kernel_call(
            functools.partial(attend_first_placed, scale, head_dim, experts),
            [((8, width), F32)] + row_outs,
            group_at, block_at, place_at, arrived, weights, out_w, pair_tokens, pair_across, vectors,
            scalars=3,
        )
    pair_qkv, pair_probs, pair_att, keep, away = pair_kept
    pair_sum = (keep + swap_core(away).astype(F32)).astype(BF16)
    pair_sum, out_w, gains = lax.optimization_barrier((pair_sum, out_w, gains))
    pair_sum = swap_pair(pair_sum)
    own_qkv, own_probs, own_att, keep, away = kernel_call(
        functools.partial(attend_own, scale, head_dim), row_outs,
        group_at, segment_ids, weights, out_w, gains, own_tokens, own_across, vectors, scalars=1,
    )
    router_w = weights[:, 3 * cols : 3 * cols + experts]
    middle, gate, outgoing = kernel_call(
        functools.partial(route_tokens, capacity, pad),
        [((toks, width), F32), ((toks, 1), F32), ((experts * pad, width // 2), BF16)],
        own_tokens, keep, swap_core(away), pair_sum, gains, router_w, chosen,
        routes.reshape(1, toks), g_low,
    )
    incoming = exchange(outgoing.reshape(experts, pad, width // 2)).reshape(-1, width // 2)

    inner, outer = w_inner[0], w_outer[0]
    units = inner.shape[1]
    buffers, dslot, slot_g, slot_probs, slot_gate, hidden, dpre, keep, away = kernel_call(
        functools.partial(run_expert, capacity),
        [
            ((2 * slots, width), BF16),
            ((2 * slots, width), BF16),
            ((slots, width), BF16),
            ((slots, experts), F32),
            ((slots, 1), F32),
            ((2 * slots, units), BF16),
            ((2 * slots, units), BF16),
            ((2, slots, width), F32),
            ((2, slots, width), BF16),
        ],
        place_at, incoming, swap_core(incoming), router_w, inner, outer, scalars=1,
    )
    grad_outer = dot(hidden, dslot, ((0,), (0,)))
    grad_inner = dot(buffers, dpre, ((0,), (0,)))
    back, grad_router = kernel_call(
        functools.partial(finish_expert, capacity),
        [((sources * pad, width // 2), BF16), ((width, experts), BF16)],
        place_at, keep, swap_core(away), buffers[:slots], slot_g, slot_probs, slot_gate, router_w,
        scalars=1,
    )
    back = exchange(back.reshape(sources, pad, width // 2)).reshape(-1, width // 2)

    grad_attn, grad_gain_two = kernel_call(
        norm_two_backward, [((toks, width), BF16), ((1, width), F32)],
        back, spread, middle, gains, g_low,
    )
    pair_grad = swap_pair(grad_attn)
    shared = (gains, weights)
    back_outs = [
        ((toks, width), F32),
        ((toks, width), BF16),
        ((length, 3 * cols), BF16),
        ((1, width), F32),
        ((own_heads, length), F32),
    ]
    grad_w, grad_out, grad_normed, away, _, own_gain, own_offsets = kernel_call(
        functools.partial(backward_own, scale, head_dim),
        [((width, 3 * cols), F32), ((cols, width), F32)] + back_outs,
        grad_attn, swap_core(grad_attn), out_w, own_att, own_qkv, own_probs, *shared,
        own_tokens, own_across,
    )
    pair_grad, grad_w, own_away = lax.optimization_barrier((pair_grad, grad_w, away))
    own_came = swap_core(own_away)
    pair_grads = (pair_grad, swap_core(pair_grad))
    keep, away, grad_qkv, pair_gain, pair_offsets = kernel_call(
        functools.partial(attend_backward, scale, head_dim), back_outs,
        *pair_grads, out_w, pair_qkv, pair_probs, *shared, pair_tokens, pair_across,
    )
    to_pair = (keep + swap_core(away).astype(F32)).astype(BF16)
    last = (
        *pair_grads, pair_att, grad_qkv, gains, pair_tokens, pair_across, grad_w, grad_out,
        own_gain, own_offsets, pair_gain, pair_offsets, grad_gain_two, grad_router,
    )
    flat = [((width, used), BF16), ((cols, width), BF16)]
    if aligned:
        (message,) = kernel_call(
            functools.partial(sum_weights_message, packed, buckets, table_cols),
            [((half, 5 * rows, wide), BF16)], *last, held=flat,
        )
    else:
        full, grad_out = kernel_call(
            functools.partial(sum_weights, packed, buckets, table_cols), flat, *last
        )
        full = full.reshape(2, 2, half, rows, used).transpose(2, 0, 1, 3, 4)
        full = full.reshape(half, 4 * rows, used)
        grad_out = grad_out.reshape(half, rows, width)
        message = jnp.concatenate(
            [
                jnp.pad(full, ((0, 0), (0, 0), (0, wide - used))),
                jnp.pad(grad_out, ((0, 0), (0, 0), (0, wide - width))),
            ],
            axis=1,
        )
    came = swap_pair(to_pair)
    arrived = exchange_half(message)
    final, grad_middle = kernel_call(
        finish_layer, [((toks, width), BF16), ((toks, width), F32)],
        back, spread, later, middle, gains, g_low, gate,
    )

    arrived, grad_inner, grad_outer, final, grad_middle = lax.optimization_barrier(
        (arrived, grad_inner, grad_outer, final, grad_middle)
    )

    own_piece, *pieces = kernel_call(
        functools.partial(sum_arrived, used),
        [((rows, 2 * used + width), F32)]
        + [((rows, 2 * used + width * (d < 2)), BF16) for d in ORDER],
        block_at, arrived, scalars=1,
    )
    pieces = across_group(pieces)
    query_grad, key_grad, value_grad, out_grad_w, router_grad, one_grad, two_grad, table_grad = kernel_call(
        functools.partial(finish_weights, own_heads, buckets, table_cols, used),
        [((rows, width), F32)] * 4
        + [((experts, rows), F32), ((1, rows), F32), ((1, rows), F32), ((heads, buckets), F32)],
        group_at, own_piece, *pieces, scalars=1,
    )

    (grad_input,) = kernel_call(
        finish_input, [((toks, width), BF16)],
        grad_normed, own_came, came, grad_middle, own_tokens, gains,
    )
    return (
        final.reshape(tokens.shape),
        grad_input.reshape(tokens.shape),
        one_grad.reshape(rows),
        query_grad,
        key_grad,
        value_grad,
        out_grad_w,
        table_grad.T,
        two_grad.reshape(rows),
        router_grad.T,
        grad_inner[None],
        grad_outer[None],
    )


def solution(mesh):
    both = ("dp", "expert")
    return jax.shard_map(
        local,
        mesh=mesh,
        in_specs=(
            P("expert", "dp", None),
            P(both),
            P(both, None),
            P(both, None),
            P(both, None),
            P(both, None),
            P(),
            P(both),
            P(both, None),
            P("expert", None, "dp"),
            P("expert", "dp", None),
            P("expert", None),
            P("expert", "dp", None),
            P("expert", "dp", None),
        ),
        out_specs=(
            P("expert", "dp", None),
            P("expert", "dp", None),
            P(both),
            P(both, None),
            P(both, None),
            P(both, None),
            P(both, None),
            P(),
            P(both),
            P(both, None),
            P("expert", None, "dp"),
            P("expert", "dp", None),
        ),
        check_vma=False,
    )
```

```python
import functools

import jax
import jax.numpy as jnp
from jax import lax
from jax.experimental import pallas as pl
from jax.experimental.pallas import tpu as pltpu
from jax.sharding import PartitionSpec as P

EPSILON = 1e-06
MASKED = -1000000000.0
BUCKET_EDGES = (1, 2, 3, 4, 5, 6, 7, 8, 12, 16, 23, 32, 46, 64, 91)
F32 = jnp.float32
BF16 = jnp.bfloat16
ORDER = (3, 1, 2)
VMEM_BYTES = 24 * 1024 * 1024


def dot(left, right, dims=((1,), (0,))):
    return lax.dot_general(left, right, (dims, ((), ())), preferred_element_type=F32)


def rms_inverse(values):
    return lax.rsqrt(jnp.mean(values * values, axis=-1, keepdims=True) + EPSILON)


def norm_backward(grad_normed, unit_values, inverse, gain_values):
    grad_unit = grad_normed * gain_values
    projected = jnp.mean(grad_unit * unit_values, axis=-1, keepdims=True)
    return inverse * (grad_unit - unit_values * projected)


def swap_core(value):
    return lax.ppermute(value, "dp", [(0, 1), (1, 0)])


def swap_pair(value):
    n = lax.axis_size("expert")
    return lax.ppermute(value, "expert", [(i, i ^ 1) for i in range(n)])


def exchange(value):
    return lax.all_to_all(value, "expert", split_axis=0, concat_axis=0, tiled=True)


def exchange_half(value):
    half = lax.axis_size("expert") // 2
    groups = [[q * half + s for s in range(half)] for q in range(2)]
    return lax.all_to_all(
        value, "expert", split_axis=0, concat_axis=0, tiled=True, axis_index_groups=groups
    )


def bucket_of(offset, total):
    distance = jnp.abs(offset)
    bucket = jnp.zeros(offset.shape, jnp.int32)
    for border in BUCKET_EDGES:
        bucket = bucket + (distance >= border).astype(jnp.int32)
    return bucket + total // 2 * (offset > 0).astype(jnp.int32)


def iota(shape, axis):
    return lax.broadcasted_iota(jnp.int32, shape, axis)


class LateRef:
    def __init__(self, source, target, sem):
        self.copy = pltpu.make_async_copy(source, target, sem)
        self.target = target
        self.shape = target.shape
        self.pending = True
        self.copy.start()

    def wait(self):
        if self.pending:
            self.copy.wait()
            self.pending = False

    def __getitem__(self, index):
        self.wait()
        return self.target[index]


def kernel_call(body, outs, *args, scalars=0, late=(), limit=VMEM_BYTES, held=()):
    count = len(args)
    late = sorted(late)

    def run(*refs):
        ins = list(refs[:count])
        out_refs = refs[count : count + len(outs)]
        scratch = refs[count + len(outs) :]
        for n, i in enumerate(late):
            ins[i] = LateRef(ins[i], scratch[n], scratch[-1].at[n])
        body(*ins, *out_refs, *scratch[len(late) : len(late) + len(held)])
        for i in late:
            ins[i].wait()

    spaces = [pltpu.SMEM if i < scalars else pltpu.VMEM for i in range(count)]
    for i in late:
        spaces[i] = pltpu.HBM
    scratch = [pltpu.VMEM(args[i].shape, args[i].dtype) for i in late]
    scratch += [pltpu.VMEM(shape, dtype) for shape, dtype in held]
    if late:
        scratch.append(pltpu.SemaphoreType.DMA((len(late),)))
    return pl.pallas_call(
        run,
        out_shape=[jax.ShapeDtypeStruct(shape, dtype) for shape, dtype in outs],
        in_specs=[pl.BlockSpec(memory_space=space) for space in spaces],
        out_specs=[pl.BlockSpec(memory_space=pltpu.VMEM)] * len(outs),
        scratch_shapes=scratch,
        compiler_params=pltpu.CompilerParams(vmem_limit_bytes=limit),
        cost_estimate=pl.CostEstimate(
            flops=1_000_000, bytes_accessed=1_000_000, transcendentals=0
        ),
    )(*args)


def choose(index, values):
    picked = values[0]
    for i in range(1, len(values)):
        picked = jnp.where(index == i, values[i], picked)
    return picked


def pack_weights(group_ref, q_ref, k_ref, v_ref, router_ref, one_ref, two_ref, wout_ref, docs_ref,
                 *refs):
    keep_ref, *out_refs = refs
    first_core = group_ref[0] < 2
    rows, width = q_ref.shape
    experts = router_ref.shape[0]
    cols = width // 4
    eye = iota((rows, rows), 0) == iota((rows, rows), 1)
    router = dot(eye.astype(F32).astype(BF16), router_ref[...], ((1,), (1,)))
    columns = [
        jnp.sum(jnp.where(eye, ref[...].astype(F32), 0.0), axis=1, keepdims=True)
        for ref in (one_ref, two_ref)
    ]
    docs = docs_ref[...].astype(F32)
    length = docs.shape[1]
    doc_cols = -(-length // rows)
    for t in range(doc_cols):
        belongs = iota((rows, length), 1) == iota((rows, length), 0) * doc_cols + t
        columns.append(jnp.sum(jnp.where(belongs, docs, 0.0), axis=1, keepdims=True))
    pad = out_refs[0].shape[1] - 6 * cols - experts - 2 - doc_cols
    small = jnp.concatenate(
        [router] + columns + [jnp.zeros((rows, pad), F32)], axis=1
    ).astype(BF16)
    weights = [ref[...] for ref in (q_ref, k_ref, v_ref)]
    pieces = [
        jnp.concatenate(
            [w[:, j * cols : (j + 1) * cols] for j in (2 * c, 2 * c + 1) for w in weights] + [small],
            axis=1,
        )
        for c in range(2)
    ]
    here = jnp.where(first_core, pieces[0], pieces[1])
    there = jnp.where(first_core, pieces[1], pieces[0])
    held = small.shape[1] + 6 * cols
    for d, ref in zip((0, *ORDER), (keep_ref, *out_refs)):
        ref[:, :held] = there if d > 1 else here
        if d < 2:
            ref[:, held:] = wout_ref[...]


def put_rows(ref, dest, value):
    rows, width = value.shape
    wide = ref.shape[2]
    ref[dest, 4 * rows :, : min(wide, width)] = value[:, :wide]
    if wide > width:
        ref[dest, 4 * rows :, width:] = jnp.zeros((rows, wide - width), BF16)


def spare_lanes(value, wide):
    over = (value.shape[1] - wide) // 4
    return jnp.concatenate(
        [value[:, wide + j * over : wide + (j + 1) * over] for j in range(4)], axis=0
    )


def take_rows(held, rows, width):
    wide = held.shape[1]
    if wide >= width:
        return held[4 * rows :, :width]
    over = (width - wide) // 4
    tail = [held[j * rows : (j + 1) * rows, wide - over :] for j in range(4)]
    return jnp.concatenate([held[4 * rows :]] + tail, axis=1)


def hand_on(in_ref, out_ref):
    out_ref[...] = in_ref[...]


def spread_weights(cols, used, block_ref, own_ref, p3_ref, p1_ref, p2_ref, out_ref):
    dests, _, wide = out_ref.shape
    rows, held = p2_ref.shape
    block = block_ref[0]
    pieces = [ref[:, :held] for ref in (own_ref, p1_ref, p2_ref, p3_ref)]
    both = jnp.concatenate([choose(block ^ j, pieces) for j in range(4)], axis=0)
    lasts = [own_ref[:, held:], p1_ref[:, held:]]
    small = both[:, 6 * cols : 3 * cols + used]
    for variant in range(2):
        at = variant * 3 * cols
        value = jnp.concatenate([both[:, at : at + 3 * cols], small], axis=1)
        if wide > used:
            value = jnp.concatenate([value, jnp.zeros((4 * rows, wide - used), BF16)], axis=1)
        last = jnp.where(block % 2 == variant, lasts[0], lasts[1])
        if wide < last.shape[1]:
            spare = spare_lanes(last, wide)
            value = jnp.concatenate([value[:, : wide - spare.shape[1]], spare], axis=1)
        for dest in range(variant, dests, 2):
            out_ref[dest, : 4 * rows] = value
            put_rows(out_ref, dest, last)


def prepare(capacity, pad, group_ref, table_ref, routes_ref, vector_ref, spread_ref, later_ref,
            gather_ref):
    buckets = table_ref.shape[0]
    own_heads, length = vector_ref.shape
    toks = length // 2
    group = group_ref[0]
    spot = iota((1, length), 1)
    offset = jnp.where(spot >= toks, spot - length, spot)
    bucket = bucket_of(offset, buckets)
    for h in range(own_heads):
        vector = jnp.zeros((1, length), F32)
        for b in range(buckets):
            vector = jnp.where(bucket == b, table_ref[b, group * own_heads + h], vector)
        vector_ref[h : h + 1] = vector
    experts = gather_ref.shape[1]
    route = routes_ref[...]
    chosen = route == iota((toks, experts), 1)
    gather_ref[...] = chosen.astype(F32)
    lower = (iota((toks, toks), 0) > iota((toks, toks), 1)).astype(BF16)
    counts = dot(lower, chosen.astype(BF16))
    slot = jnp.sum(jnp.where(chosen, counts, 0.0), axis=1, keepdims=True).astype(jnp.int32)
    across = iota((toks, experts * pad), 1)
    for i in range(4):
        place = jnp.where(slot < capacity, route * pad + i * capacity + slot, -1)
        spread = (place == across).astype(F32)
        target = (spread_ref, later_ref)[i % 2]
        target[i // 2] = spread.astype(BF16)


def place_weights(arrived_ref, w_ref, wout_ref):
    sources = arrived_ref.shape[0]
    rows = wout_ref.shape[0] // sources
    used = w_ref.shape[1]
    width = wout_ref.shape[1]
    block = sources * rows
    for s in range(sources):
        for j in range(4):
            w_ref[j * block + s * rows : j * block + (s + 1) * rows] = arrived_ref[
                s, j * rows : (j + 1) * rows, :used
            ]
        wout_ref[s * rows : (s + 1) * rows] = take_rows(arrived_ref[s], rows, width)


def gain_rows(experts, cols, w_ref, gains_ref):
    small = w_ref[:, 3 * cols :]
    pick = (iota((8, small.shape[1]), 1) == iota((8, small.shape[1]), 0) + experts).astype(BF16)
    gains_ref[...] = dot(pick, small, ((1,), (1,)))


def attend(scale, head_dim, docs, group_ref, w_ref, wout_ref, gains_ref, own_ref, across_ref,
           vector_ref, qkv_ref, probs_ref, att_ref, keep_ref, send_ref):
    own_heads, length = vector_ref.shape
    cols = own_heads * head_dim
    toks = own_ref.shape[0]
    vectors = vector_ref[...]
    turned = jnp.concatenate([docs[:, toks:], docs[:, :toks]], axis=1)
    across = jnp.broadcast_to(jnp.where(group_ref[0] < 2, docs, turned), (length, length))
    same = across == jnp.transpose(across)
    x = jnp.concatenate([own_ref[...], across_ref[...]], axis=0).astype(F32)
    normed = (x * rms_inverse(x) * gains_ref[0:1]).astype(BF16)
    qkv = dot(normed, w_ref[:, : 3 * cols]).astype(BF16)
    qkv_ref[...] = qkv
    parts = []
    for h in range(own_heads):
        at = h * head_dim
        q = qkv[:, at : at + head_dim]
        k = qkv[:, cols + at : cols + at + head_dim]
        v = qkv[:, 2 * cols + at : 2 * cols + at + head_dim]
        full = jnp.broadcast_to(vectors[h : h + 1], (length, length))
        bias = pltpu.roll(full, 0, 1, stride=1, stride_axis=0)
        scores = jnp.where(same, dot(q, k, ((1,), (1,))) * scale + bias, MASKED)
        top = jnp.max(scores, axis=1, keepdims=True)
        raised = jnp.exp(scores - top)
        probs = raised * (1.0 / jnp.sum(raised, axis=1, keepdims=True))
        probs_ref[h] = probs
        parts.append(dot(probs.astype(BF16), v))
    attended = jnp.concatenate(parts, axis=1).astype(BF16)
    att_ref[...] = attended
    partial = dot(attended, wout_ref[...])
    keep_ref[...] = partial[:toks]
    send_ref[...] = partial[toks:].astype(BF16)


def docs_of_pair(at, length, rows, block_ref, place_ref, arrived_ref):
    sources = arrived_ref.shape[0]
    doc_cols = -(-length // rows)
    held = arrived_ref[(place_ref[0] % sources) ^ 1]
    blocks = [held[j * rows : (j + 1) * rows, at : at + doc_cols].astype(F32) for j in range(4)]
    block = choose(block_ref[0], blocks)
    docs = jnp.zeros((1, length), F32)
    for t in range(doc_cols):
        belongs = iota((rows, length), 1) == iota((rows, length), 0) * doc_cols + t
        docs = docs + jnp.sum(jnp.where(belongs, block[:, t : t + 1], 0.0), axis=0, keepdims=True)
    return docs


def attend_own(scale, head_dim, group_ref, docs_ref, *refs):
    attend(scale, head_dim, docs_ref[...].astype(F32), group_ref, *refs)


def attend_first(scale, head_dim, experts, group_ref, block_ref, place_ref, arrived_ref, own_ref, across_ref,
                 vector_ref, w_ref, wout_ref, gains_ref, *outs):
    place_weights(arrived_ref, w_ref, wout_ref)
    cols = wout_ref.shape[0]
    gain_rows(experts, cols, w_ref, gains_ref)
    docs = docs_of_pair(
        3 * cols + experts + 2, vector_ref.shape[1], cols // arrived_ref.shape[0], block_ref, place_ref,
        arrived_ref,
    )
    attend(scale, head_dim, docs, group_ref, w_ref, wout_ref, gains_ref, own_ref, across_ref,
           vector_ref, *outs)


def attend_first_placed(scale, head_dim, experts, group_ref, block_ref, place_ref, arrived_ref, w_ref, wout_ref,
                        own_ref, across_ref, vector_ref, gains_ref, *outs):
    cols = wout_ref.shape[0]
    gain_rows(experts, cols, w_ref, gains_ref)
    docs = docs_of_pair(
        3 * cols + experts + 2, vector_ref.shape[1], cols // arrived_ref.shape[0], block_ref, place_ref,
        arrived_ref,
    )
    attend(scale, head_dim, docs, group_ref, w_ref, wout_ref, gains_ref, own_ref, across_ref,
           vector_ref, *outs)


def route_tokens(capacity, pad, x_ref, keep_ref, core_ref, came_ref, gains_ref, w_ref, chosen_ref,
                 routes_ref, g_ref, middle_ref, gate_ref, out_ref):
    middle = x_ref[...].astype(F32) + (
        (keep_ref[...] + core_ref[...].astype(F32)) + came_ref[...].astype(F32)
    )
    middle_ref[...] = middle
    normed = (middle * rms_inverse(middle) * gains_ref[1:2]).astype(BF16)
    g = g_ref[...]
    half = g.shape[1] // 2
    both = jnp.concatenate([normed[:, :half], g[:, :half], normed[:, half:], g[:, half:]], axis=0)
    toks = g.shape[0]
    experts = w_ref.shape[1]
    route = routes_ref[...]
    chosen = iota((experts, toks), 0) == route
    upper = (iota((toks, toks), 0) < iota((toks, toks), 1)).astype(BF16)
    counts = dot(chosen.astype(BF16), upper)
    slot = jnp.sum(jnp.where(chosen, counts, 0.0), axis=0, keepdims=True).astype(jnp.int32)
    rows = out_ref.shape[0]
    place = jnp.where(slot < capacity, route * pad + slot, -4 * rows)
    down = iota((rows, toks), 0)
    send = jnp.concatenate(
        [(down == place + i * capacity).astype(BF16) for i in range(4)], axis=1
    )
    out_ref[...] = dot(send, both).astype(BF16)
    probs = jax.nn.softmax(dot(normed, w_ref[...]), axis=-1)
    gate_ref[...] = jnp.sum(probs * chosen_ref[...], axis=1, keepdims=True)


def run_expert(capacity, place_ref, own_ref, other_ref, router_ref, inner_ref, outer_ref, buf_ref,
               dslot_ref, g_ref, probs_ref, gate_ref, hidden_ref, dpre_ref, keep_ref, send_ref):
    slots = buf_ref.shape[0] // 2
    half = own_ref.shape[1]
    experts = router_ref.shape[1]
    pad = own_ref.shape[0] // (slots // capacity)
    shape = (4 * slots, own_ref.shape[0])
    row = iota(shape, 0)
    part = row // slots
    inside = row - part * slots
    source = inside // capacity
    wanted = source * pad + part * capacity + (inside - source * capacity)
    select = (iota(shape, 1) == wanted).astype(BF16)
    rows = dot(select, jnp.concatenate([own_ref[...], other_ref[...]], axis=1))
    mine = (iota((1, experts), 1) == place_ref[0]).astype(F32)
    for side in range(2):
        at = side * slots
        cut = rows[:, side * half : (side + 1) * half]
        buffers = jnp.concatenate([cut[:slots], cut[2 * slots : 3 * slots]], axis=1).astype(BF16)
        g = jnp.concatenate([cut[slots : 2 * slots], cut[3 * slots :]], axis=1)
        buf_ref[at : at + slots] = buffers
        probs = jax.nn.softmax(dot(buffers, router_ref[...]), axis=-1)
        gate = jnp.sum(probs * mine, axis=1, keepdims=True)
        dslot_ref[at : at + slots] = (gate * g).astype(BF16)
        if side == 0:
            g_ref[...] = g.astype(BF16)
            probs_ref[...] = probs
            gate_ref[...] = gate
    inner = inner_ref[...]
    outer = outer_ref[...]
    pre = dot(buf_ref[...], inner)
    cdf = 0.5 * (1.0 + lax.erf(pre * (0.5**0.5)))
    hidden = (pre * cdf).astype(BF16)
    hidden_ref[...] = hidden
    slope = cdf + pre * jnp.exp(-0.5 * pre * pre) * 0.3989422804014327
    dpre = (dot(dslot_ref[...], outer, ((1,), (1,))) * slope).astype(BF16)
    dpre_ref[...] = dpre
    result = dot(hidden, outer)
    keep_ref[0] = result[:slots]
    send_ref[0] = result[slots:].astype(BF16)
    back = dot(dpre, inner, ((1,), (1,)))
    keep_ref[1] = back[:slots]
    send_ref[1] = back[slots:].astype(BF16)


def finish_expert(capacity, place_ref, keep_ref, came_ref, buf_ref, g_ref, probs_ref, gate_ref,
                  router_ref, out_ref, grad_ref):
    slots = g_ref.shape[0]
    experts = router_ref.shape[1]
    pad = out_ref.shape[0] // (slots // capacity)
    total = (keep_ref[...] + came_ref[...].astype(F32)).astype(BF16)
    result = total[0]
    mine = (iota((1, experts), 1) == place_ref[0]).astype(F32)
    grad_gate = jnp.sum(g_ref[...].astype(F32) * result.astype(F32), axis=1, keepdims=True)
    grad_logits = (grad_gate * gate_ref[...] * (mine - probs_ref[...])).astype(BF16)
    grad_ref[...] = dot(buf_ref[...], grad_logits, ((0,), (0,))).astype(BF16)
    back = total[1].astype(F32) + dot(grad_logits, router_ref[...], ((1,), (1,)))
    shape = (out_ref.shape[0], 4 * slots)
    row = iota(shape, 0)
    source = row // pad
    inside = row - source * pad
    part = inside // capacity
    wanted = jnp.where(part < 4, part * slots + source * capacity + inside - part * capacity, -1)
    expand = (iota(shape, 1) == wanted).astype(BF16)
    back = back.astype(BF16)
    half = back.shape[1] // 2
    both = jnp.concatenate([back[:, :half], result[:, :half], back[:, half:], result[:, half:]], axis=0)
    out_ref[...] = dot(expand, both).astype(BF16)


def middle_backward(back_ref, spread_ref, middle_ref, gains_ref, g_ref):
    middle = middle_ref[...]
    inverse = rms_inverse(middle)
    unit = middle * inverse
    rows = back_ref[...]
    grad_normed = jnp.concatenate([dot(spread_ref[i], rows) for i in range(2)], axis=1)
    dmiddle = g_ref[...].astype(F32) + norm_backward(grad_normed, unit, inverse, gains_ref[1:2])
    return dmiddle, grad_normed * unit


def norm_two_backward(back_ref, spread_ref, middle_ref, gains_ref, g_ref, da_ref, gain_ref):
    dmiddle, scaled = middle_backward(back_ref, spread_ref, middle_ref, gains_ref, g_ref)
    gain_ref[...] = jnp.sum(scaled, axis=0, keepdims=True)
    da_ref[...] = dmiddle.astype(BF16)


def finish_layer(back_ref, spread_ref, later_ref, middle_ref, gains_ref, g_ref, gate_ref, out_ref,
                 dmiddle_ref):
    rows = back_ref[...]
    combined = jnp.concatenate([dot(later_ref[i], rows) for i in range(2)], axis=1)
    out_ref[...] = (middle_ref[...] + gate_ref[...] * combined).astype(BF16)
    dmiddle_ref[...] = middle_backward(back_ref, spread_ref, middle_ref, gains_ref, g_ref)[0]


def attend_backward(scale, head_dim, own_ref, across_ref, wout_ref, qkv_ref, probs_ref, gains_ref,
                    w_ref, x_own_ref, x_across_ref, keep_ref, send_ref, grad_ref, gain_ref,
                    offsets_ref):
    own_heads = probs_ref.shape[0]
    cols = own_heads * head_dim
    toks = own_ref.shape[0]
    length = 2 * toks
    flip = (iota((length, length), 0) + iota((length, length), 1) == length - 1).astype(BF16)
    da = jnp.concatenate([own_ref[...], across_ref[...]], axis=0)
    grad_att = dot(da, wout_ref[...], ((1,), (1,))).astype(BF16)
    qkv = qkv_ref[...]
    parts = [[], [], []]
    for h in range(own_heads):
        at = h * head_dim
        q = qkv[:, at : at + head_dim]
        k = qkv[:, cols + at : cols + at + head_dim]
        v = qkv[:, 2 * cols + at : 2 * cols + at + head_dim]
        gh = grad_att[:, at : at + head_dim]
        probs = probs_ref[h]
        grad_probs = dot(gh, v, ((1,), (1,)))
        row_dot = jnp.sum(probs * grad_probs, axis=1, keepdims=True)
        ds = (probs * (grad_probs - row_dot)).astype(BF16)
        turned = pltpu.roll(dot(flip, ds), 1, 1, stride=1, stride_axis=0)
        offsets_ref[h : h + 1] = jnp.sum(turned, axis=0, keepdims=True)
        parts[0].append(dot(ds, k) * scale)
        parts[1].append(dot(ds, q, ((0,), (0,))) * scale)
        parts[2].append(dot(probs.astype(BF16), gh, ((0,), (0,))))
    grad_qkv = jnp.concatenate(parts[0] + parts[1] + parts[2], axis=1).astype(BF16)
    grad_ref[...] = grad_qkv
    grad_normed = dot(grad_qkv, w_ref[:, : 3 * cols], ((1,), (1,)))
    keep_ref[...] = grad_normed[:toks]
    send_ref[...] = grad_normed[toks:].astype(BF16)
    x = jnp.concatenate([x_own_ref[...], x_across_ref[...]], axis=0).astype(F32)
    gain_ref[...] = jnp.sum(grad_normed * (x * rms_inverse(x)), axis=0, keepdims=True)


def row_weights(own_ref, across_ref, att_ref, grad_ref, gains_ref, x_own_ref, x_across_ref):
    x = jnp.concatenate([x_own_ref[...], x_across_ref[...]], axis=0).astype(F32)
    normed = (x * rms_inverse(x) * gains_ref[0:1]).astype(BF16)
    da = jnp.concatenate([own_ref[...], across_ref[...]], axis=0)
    weights = dot(normed, grad_ref[...], ((0,), (0,)))
    return weights, dot(att_ref[...], da, ((0,), (0,)))


def backward_own(scale, head_dim, own_ref, across_ref, wout_ref, att_ref, qkv_ref, probs_ref,
                 gains_ref, w_ref, x_own_ref, x_across_ref, gw_ref, gout_ref, keep_ref, send_ref,
                 grad_ref, gain_ref, offsets_ref):
    attend_backward(
        scale, head_dim, own_ref, across_ref, wout_ref, qkv_ref, probs_ref, gains_ref, w_ref,
        x_own_ref, x_across_ref, keep_ref, send_ref, grad_ref, gain_ref, offsets_ref,
    )
    gw_ref[...], gout_ref[...] = row_weights(
        own_ref, across_ref, att_ref, grad_ref, gains_ref, x_own_ref, x_across_ref
    )


def sum_weights(packed, buckets, table_cols, *refs):
    gw_ref, gout_ref, own_gain_ref, own_offsets_ref, gain_ref, offsets_ref = refs[7:13]
    gain_two_ref, router_ref, full_ref, out_ref = refs[13:]
    weights, outs = row_weights(*refs[:7])
    own_heads, length = offsets_ref.shape
    width, experts = router_ref.shape
    toks = length // 2
    rows = own_heads * buckets // table_cols
    spot = iota((1, length), 1)
    offset = jnp.where(spot >= toks, spot - length, spot)
    bucket = bucket_of(offset, buckets)
    table = []
    for t in range(table_cols):
        column = jnp.zeros((rows, 1), F32)
        for h in range(own_heads):
            belongs = iota((rows, length), 0) * table_cols + t == bucket * own_heads + h
            value = own_offsets_ref[h : h + 1] + offsets_ref[h : h + 1]
            column = column + jnp.sum(jnp.where(belongs, value, 0.0), axis=1, keepdims=True)
        table.append(column)
    table = jnp.concatenate([jnp.concatenate(table, axis=1)] * (width // rows), axis=0)
    narrow = jnp.concatenate(
        [own_gain_ref[...] + gain_ref[...], gain_two_ref[...], jnp.zeros((6, width), F32)], axis=0
    )
    narrow = jnp.transpose(narrow)[:, :2]
    weights = weights + gw_ref[...]
    pieces = [weights, router_ref[...].astype(F32), narrow, table]
    outs = outs + gout_ref[...]
    out_ref[...] = outs.astype(BF16)
    used = full_ref.shape[1]
    tail = [spare_lanes(outs, used)] if packed else []
    spare = used - sum(p.shape[1] for p in pieces + tail)
    if spare:
        tail.insert(0, jnp.zeros((width, spare), F32))
    full_ref[...] = jnp.concatenate(pieces + tail, axis=1).astype(BF16)


def sum_weights_message(packed, buckets, table_cols, *refs):
    *rest, message_ref, full_ref, out_ref = refs
    sum_weights(packed, buckets, table_cols, *rest, full_ref, out_ref)
    dests, _, wide = message_ref.shape
    rows = out_ref.shape[0] // dests
    used = full_ref.shape[1]
    block = dests * rows
    for s in range(dests):
        for j in range(4):
            at = j * block + s * rows
            message_ref[s, j * rows : (j + 1) * rows, :used] = full_ref[at : at + rows]
            if wide > used:
                message_ref[s, j * rows : (j + 1) * rows, used:] = jnp.zeros(
                    (rows, wide - used), BF16
                )
        put_rows(message_ref, s, out_ref[s * rows : (s + 1) * rows])


def sum_arrived(used, block_ref, arrived_ref, own_ref, *send_refs):
    rows, held = own_ref.shape
    width = held - 2 * used
    block = block_ref[0]
    totals = []
    for variant in range(2):
        total = arrived_ref[variant].astype(F32)
        for s in range(variant + 2, arrived_ref.shape[0], 2):
            total = total + arrived_ref[s].astype(F32)
        totals.append(total)
    pieces = [
        jnp.concatenate([t[j * rows : (j + 1) * rows, :used] for t in totals], axis=1)
        for j in range(4)
    ]
    lasts = [take_rows(t, rows, width) for t in totals]
    first = block % 2 == 0
    own_ref[:, : 2 * used] = choose(block, pieces)
    own_ref[:, 2 * used :] = jnp.where(first, lasts[0], lasts[1])
    for d, ref in zip(ORDER, send_refs):
        ref[:, : 2 * used] = choose(block ^ d, pieces).astype(BF16)
        if d == 1:
            ref[:, 2 * used :] = jnp.where(first, lasts[1], lasts[0]).astype(BF16)


def finish_input(grad_ref, core_ref, came_ref, dmiddle_ref, x_ref, gains_ref, out_ref):
    x = x_ref[...].astype(F32)
    inverse = rms_inverse(x)
    grad_normed = grad_ref[...] + core_ref[...].astype(F32) + came_ref[...].astype(F32)
    out_ref[...] = (
        dmiddle_ref[...] + norm_backward(grad_normed, x * inverse, inverse, gains_ref[0:1])
    ).astype(BF16)


def finish_weights(own_heads, buckets, table_cols, used, group_ref, p0_ref, p3_ref, p1_ref, p2_ref,
                   q_ref, k_ref, v_ref, w_ref, router_ref, one_ref, two_ref, table_ref):
    rows, width = q_ref.shape
    experts = router_ref.shape[0]
    cols = width // 4
    here = p0_ref[...] + p1_ref[...].astype(F32)
    there = p2_ref[...].astype(F32) + p3_ref[...].astype(F32)
    w_ref[...] = here[:, 2 * used :]
    here = here[:, : 2 * used]
    first_core = group_ref[0] < 2
    by_core = (jnp.where(first_core, here, there), jnp.where(first_core, there, here))
    ordered = [c[:, v * used : (v + 1) * used] for c in by_core for v in range(2)]
    pieces = ordered
    for n, ref in enumerate((q_ref, k_ref, v_ref)):
        ref[...] = jnp.concatenate([p[:, n * cols : (n + 1) * cols] for p in ordered], axis=1)
    at = 3 * cols
    small = sum(p[:, at : at + experts + 2] for p in pieces)
    square = -(-max(rows, experts) // 128) * 128
    padded = small[:, :experts]
    if square > experts:
        padded = jnp.concatenate([padded, jnp.zeros((rows, square - experts), F32)], axis=1)
    padded = jnp.concatenate([padded, jnp.zeros((square - rows, square), F32)], axis=0)
    router_ref[...] = jnp.transpose(padded)[:experts, :rows]
    eye = iota((rows, rows), 0) == iota((rows, rows), 1)
    for i, ref in enumerate((one_ref, two_ref)):
        column = small[:, experts + i : experts + i + 1]
        ref[...] = jnp.sum(jnp.where(eye, column, 0.0), axis=0, keepdims=True)
    at += experts + 2
    lines = []
    lane = iota((rows, 128), 1)
    for p in ordered:
        for h in range(own_heads):
            line = jnp.zeros((1, 128), F32)
            for t in range(table_cols):
                belongs = iota((rows, 128), 0) * table_cols + t == lane * own_heads + h
                value = jnp.where(belongs & (lane < buckets), p[:, at + t : at + t + 1], 0.0)
                line = line + jnp.sum(value, axis=0, keepdims=True)
            lines.append(line)
    table_ref[...] = jnp.concatenate(lines, axis=0)[:, :buckets]


def local(
    tokens,
    gain_one,
    w_query,
    w_key,
    w_value,
    w_out,
    bias_table,
    gain_two,
    w_router,
    w_inner,
    w_outer,
    segment_ids,
    routes,
    out_grad,
):
    toks = tokens.shape[1]
    width = tokens.shape[2]
    heads = bias_table.shape[1]
    buckets = bias_table.shape[0]
    head_dim = width // heads
    own_heads = heads // 4
    cols = own_heads * head_dim
    length = 2 * toks
    scale = head_dim ** (-0.5)
    sources = lax.axis_size("expert")
    experts = sources
    capacity = (5 * toks + 4 * experts - 1) // (4 * experts)
    slots = experts * capacity
    pad = -(-4 * capacity // 8) * 8
    rows = w_query.shape[0]
    core = lax.axis_index("dp")
    place = lax.axis_index("expert")
    half = sources // 2
    member = place % 2
    block_at = (2 * core + place // half).reshape(1).astype(jnp.int32)
    first_core = core == 0
    place_at = place.reshape(1).astype(jnp.int32)
    group_at = (2 * core + member).reshape(1).astype(jnp.int32)
    table_cols = max(1, own_heads * buckets // rows)
    extra = max(table_cols, -(-length // rows))
    used = -(-(3 * cols + experts + 2 + extra) // 128) * 128
    aligned = rows % 8 == 0
    held = -(-(3 * cols + used) // 128) * 128
    room = used - (3 * cols + experts + 2 + extra)
    packed = aligned and used < width <= used + 4 * room and (width - used) % 4 == 0
    wide = used if packed else max(used, width)

    def across_group(pieces):
        return [
            lax.ppermute(
                piece,
                ("dp", "expert"),
                [
                    (c * sources + e, (c ^ (d >> 1)) * sources + (e ^ (half * (d & 1))))
                    for c in range(2)
                    for e in range(sources)
                ],
            )
            for d, piece in zip(ORDER, pieces)
        ]

    own_tokens = tokens.reshape(toks, width)
    pair_tokens = swap_pair(own_tokens)

    own_piece, *pieces = kernel_call(
        pack_weights,
        [((rows, held + width * (d < 2)), BF16) for d in (0, *ORDER)],
        group_at, w_query, w_key, w_value, w_router.T, gain_one.reshape(1, rows),
        gain_two.reshape(1, rows), w_out, segment_ids, scalars=1, late=range(1, 9),
        limit=60 * 1024 * 1024,
    )
    pieces = across_group(pieces)
    (own_piece,) = kernel_call(hand_on, [(own_piece.shape, BF16)], own_piece)
    pair_tokens, own_piece, *pieces = lax.optimization_barrier((pair_tokens, own_piece, *pieces))
    (message,) = kernel_call(
        functools.partial(spread_weights, cols, used), [((half, 5 * rows, wide), BF16)],
        block_at, own_piece, *pieces, scalars=1,
    )
    arrived = exchange_half(message)

    own_across = swap_core(own_tokens)
    pair_across = swap_core(pair_tokens)
    vectors, spread, later, chosen = kernel_call(
        functools.partial(prepare, capacity, pad),
        [
            ((own_heads, length), F32),
            ((2, toks, experts * pad), BF16),
            ((2, toks, experts * pad), BF16),
            ((toks, experts), F32),
        ],
        group_at, bias_table, routes.reshape(toks, 1), scalars=2,
    )
    g_low = out_grad.reshape(toks, width)

    row_outs = [
        ((length, 3 * cols), BF16),
        ((own_heads, length, length), F32),
        ((length, cols), BF16),
        ((toks, width), F32),
        ((toks, width), BF16),
    ]
    placed = [((width, used), BF16), ((cols, width), BF16)]
    if aligned:
        weights, out_w, gains, *pair_kept = kernel_call(
            functools.partial(attend_first, scale, head_dim, experts),
            placed + [((8, width), F32)] + row_outs,
            group_at, block_at, place_at, arrived, pair_tokens, pair_across, vectors, scalars=3,
        )
    else:
        weights = arrived[:, : 4 * rows, :used].reshape(half, 2, 2, rows, used)
        weights = weights.transpose(1, 2, 0, 3, 4).reshape(width, used)
        out_w = arrived[:, 4 * rows :, :width].reshape(cols, width)
        gains, *pair_kept = kernel_call(
            functools.partial(attend_first_placed, scale, head_dim, experts),
            [((8, width), F32)] + row_outs,
            group_at, block_at, place_at, arrived, weights, out_w, pair_tokens, pair_across, vectors,
            scalars=3,
        )
    pair_qkv, pair_probs, pair_att, keep, away = pair_kept
    pair_sum = (keep + swap_core(away).astype(F32)).astype(BF16)
    pair_sum, out_w, gains = lax.optimization_barrier((pair_sum, out_w, gains))
    pair_sum = swap_pair(pair_sum)
    own_qkv, own_probs, own_att, keep, away = kernel_call(
        functools.partial(attend_own, scale, head_dim), row_outs,
        group_at, segment_ids, weights, out_w, gains, own_tokens, own_across, vectors, scalars=1,
    )
    router_w = weights[:, 3 * cols : 3 * cols + experts]
    middle, gate, outgoing = kernel_call(
        functools.partial(route_tokens, capacity, pad),
        [((toks, width), F32), ((toks, 1), F32), ((experts * pad, width // 2), BF16)],
        own_tokens, keep, swap_core(away), pair_sum, gains, router_w, chosen,
        routes.reshape(1, toks), g_low,
    )
    incoming = exchange(outgoing.reshape(experts, pad, width // 2)).reshape(-1, width // 2)

    inner, outer = w_inner[0], w_outer[0]
    units = inner.shape[1]
    buffers, dslot, slot_g, slot_probs, slot_gate, hidden, dpre, keep, away = kernel_call(
        functools.partial(run_expert, capacity),
        [
            ((2 * slots, width), BF16),
            ((2 * slots, width), BF16),
            ((slots, width), BF16),
            ((slots, experts), F32),
            ((slots, 1), F32),
            ((2 * slots, units), BF16),
            ((2 * slots, units), BF16),
            ((2, slots, width), F32),
            ((2, slots, width), BF16),
        ],
        place_at, incoming, swap_core(incoming), router_w, inner, outer, scalars=1,
    )
    grad_outer = dot(hidden, dslot, ((0,), (0,)))
    grad_inner = dot(buffers, dpre, ((0,), (0,)))
    back, grad_router = kernel_call(
        functools.partial(finish_expert, capacity),
        [((sources * pad, width // 2), BF16), ((width, experts), BF16)],
        place_at, keep, swap_core(away), buffers[:slots], slot_g, slot_probs, slot_gate, router_w,
        scalars=1,
    )
    back = exchange(back.reshape(sources, pad, width // 2)).reshape(-1, width // 2)

    grad_attn, grad_gain_two = kernel_call(
        norm_two_backward, [((toks, width), BF16), ((1, width), F32)],
        back, spread, middle, gains, g_low,
    )
    pair_grad = swap_pair(grad_attn)
    shared = (gains, weights)
    back_outs = [
        ((toks, width), F32),
        ((toks, width), BF16),
        ((length, 3 * cols), BF16),
        ((1, width), F32),
        ((own_heads, length), F32),
    ]
    grad_w, grad_out, grad_normed, away, _, own_gain, own_offsets = kernel_call(
        functools.partial(backward_own, scale, head_dim),
        [((width, 3 * cols), F32), ((cols, width), F32)] + back_outs,
        grad_attn, swap_core(grad_attn), out_w, own_att, own_qkv, own_probs, *shared,
        own_tokens, own_across,
    )
    pair_grad, grad_w, own_away = lax.optimization_barrier((pair_grad, grad_w, away))
    own_came = swap_core(own_away)
    pair_grads = (pair_grad, swap_core(pair_grad))
    keep, away, grad_qkv, pair_gain, pair_offsets = kernel_call(
        functools.partial(attend_backward, scale, head_dim), back_outs,
        *pair_grads, out_w, pair_qkv, pair_probs, *shared, pair_tokens, pair_across,
    )
    to_pair = (keep + swap_core(away).astype(F32)).astype(BF16)
    last = (
        *pair_grads, pair_att, grad_qkv, gains, pair_tokens, pair_across, grad_w, grad_out,
        own_gain, own_offsets, pair_gain, pair_offsets, grad_gain_two, grad_router,
    )
    flat = [((width, used), BF16), ((cols, width), BF16)]
    if aligned:
        (message,) = kernel_call(
            functools.partial(sum_weights_message, packed, buckets, table_cols),
            [((half, 5 * rows, wide), BF16)], *last, held=flat,
        )
    else:
        full, grad_out = kernel_call(
            functools.partial(sum_weights, packed, buckets, table_cols), flat, *last
        )
        full = full.reshape(2, 2, half, rows, used).transpose(2, 0, 1, 3, 4)
        full = full.reshape(half, 4 * rows, used)
        grad_out = grad_out.reshape(half, rows, width)
        message = jnp.concatenate(
            [
                jnp.pad(full, ((0, 0), (0, 0), (0, wide - used))),
                jnp.pad(grad_out, ((0, 0), (0, 0), (0, wide - width))),
            ],
            axis=1,
        )
    came = swap_pair(to_pair)
    arrived = exchange_half(message)
    final, grad_middle = kernel_call(
        finish_layer, [((toks, width), BF16), ((toks, width), F32)],
        back, spread, later, middle, gains, g_low, gate,
    )

    arrived, grad_inner, grad_outer, final, grad_middle = lax.optimization_barrier(
        (arrived, grad_inner, grad_outer, final, grad_middle)
    )

    own_piece, *pieces = kernel_call(
        functools.partial(sum_arrived, used),
        [((rows, 2 * used + width), F32)]
        + [((rows, 2 * used + width * (d < 2)), BF16) for d in ORDER],
        block_at, arrived, scalars=1,
    )
    pieces = across_group(pieces)
    query_grad, key_grad, value_grad, out_grad_w, router_grad, one_grad, two_grad, table_grad = kernel_call(
        functools.partial(finish_weights, own_heads, buckets, table_cols, used),
        [((rows, width), F32)] * 4
        + [((experts, rows), F32), ((1, rows), F32), ((1, rows), F32), ((heads, buckets), F32)],
        group_at, own_piece, *pieces, scalars=1,
    )

    (grad_input,) = kernel_call(
        finish_input, [((toks, width), BF16)],
        grad_normed, own_came, came, grad_middle, own_tokens, gains,
    )
    return (
        final.reshape(tokens.shape),
        grad_input.reshape(tokens.shape),
        one_grad.reshape(rows),
        query_grad,
        key_grad,
        value_grad,
        out_grad_w,
        table_grad.T,
        two_grad.reshape(rows),
        router_grad.T,
        grad_inner[None],
        grad_outer[None],
    )


def solution(mesh):
    both = ("dp", "expert")
    return jax.shard_map(
        local,
        mesh=mesh,
        in_specs=(
            P("expert", "dp", None),
            P(both),
            P(both, None),
            P(both, None),
            P(both, None),
            P(both, None),
            P(),
            P(both),
            P(both, None),
            P("expert", None, "dp"),
            P("expert", "dp", None),
            P("expert", None),
            P("expert", "dp", None),
            P("expert", "dp", None),
        ),
        out_specs=(
            P("expert", "dp", None),
            P("expert", "dp", None),
            P(both),
            P(both, None),
            P(both, None),
            P(both, None),
            P(both, None),
            P(),
            P(both),
            P(both, None),
            P("expert", None, "dp"),
            P("expert", "dp", None),
        ),
        check_vma=False,
    )
```
